32 devices in a mesh: shard: 4 (over x, core), rep: 8 (over z, y).
Axes of the slice: x: 2, y: 2, z: 4, core: 2. Of those that a mesh axis runs over, the one named last changes fastest.
Arguments:
- tokens: bfloat16 [8, 1024, 1024], P('rep', 'shard'), may hold values from -6 to 6
- segments: int32 [8, 1024], P('rep', 'shard'), may hold values from 0 to 2, as said below
- grad_out: bfloat16 [8, 1024, 1024], P('rep', 'shard'), may hold values from -6 to 6
- attention_gain: bfloat16 [1024], P('shard'), may hold values from 0.25 to 1.75
- query_weight: bfloat16 [1024, 2048], P('shard'), may hold values from -0.1875 to 0.1875
- key_matrix: bfloat16 [1024, 1024], P('shard'), may hold values from -0.1875 to 0.1875
- value_matrix: bfloat16 [1024, 1024], P('shard'), may hold values from -0.1875 to 0.1875
- query_gain: bfloat16 [128], P('shard'), may hold values from 0.25 to 1.75
- key_gain: bfloat16 [128], P('shard'), may hold values from 0.25 to 1.75
- output_weight: bfloat16 [2048, 1024], P(None, 'shard'), may hold values from -1.5 to 1.5
- mlp_gain: bfloat16 [1024], P('shard'), may hold values from 0.25 to 1.75
- gate_weight: bfloat16 [1024, 3072], P('shard'), may hold values from -0.1875 to 0.1875
- up_weight: bfloat16 [1024, 3072], P('shard'), may hold values from -0.1875 to 0.1875
- down_weight: bfloat16 [3072, 1024], P('shard'), may hold values from -0.109375 to 0.109375
Outputs:
- layer_out: bfloat16 [8, 1024, 1024], P('rep', 'shard')
- grad_tokens: float32 [8, 1024, 1024], P('rep', 'shard')
- grad_attention_gain: float32 [1024], P('shard')
- grad_query_weight: float32 [1024, 2048], P('shard')
- grad_key_weight: float32 [1024, 1024], P('shard')
- grad_value_weight: float32 [1024, 1024], P('shard')
- grad_query_gain: float32 [128], P('shard')
- grad_key_gain: float32 [128], P('shard')
- grad_output_weight: float32 [2048, 1024], P(None, 'shard')
- grad_mlp_gain: float32 [1024], P('shard')
- grad_gate_weight: float32 [1024, 3072], P('shard')
- grad_up_weight: float32 [1024, 3072], P('shard')
- grad_down_weight: float32 [3072, 1024], P('shard')
The draws below stay inside these ranges and needn't reach their ends.
Inputs may be any that keep to these rules, and one draw needn't show every extreme that they name: `segments`: in each sequence the ids are 0, 1 and 2 in this order, never falling, each present; document 1 begins within the first 256 tokens of the sequence and ends within its last 256 tokens.
All inputs are finite; a program needn't handle non-finite values.
Results may differ from the reference program's by a relative error of at most 0.019.
Values may be sent and summed in bfloat16 or wider, within the bound.
No kernel may reach another device: no remote copies, remote signals or barrier semaphores. Data moves between devices by JAX's collectives and lax.ppermute only.
A program may use at most 192 MiB of HBM per device.

```python
import jax
import jax.numpy as jnp
from jax import lax

MODEL_WIDTH = 1024
QUERY_HEAD_COUNT = 16
KEY_VALUE_HEADS = 8
HEAD_SIZE = 128
FF = 3072
SEQUENCE_TOKENS = 1024
ROWS = 256
SEQS = 8


def draw_segments(key, part):
    key = jax.random.fold_in(key, 7)
    first_key, last_key = jax.random.split(key)
    opening = jax.random.randint(first_key, (SEQS, 1), 1, ROWS)
    closing = jax.random.randint(last_key, (SEQS, 1), SEQUENCE_TOKENS - ROWS + 1, SEQUENCE_TOKENS)
    places = jnp.arange(SEQUENCE_TOKENS, dtype=jnp.int32)[None, :]
    return (places >= opening).astype(jnp.int32) + (places >= closing).astype(jnp.int32)


def shard_levels(key, dims, pieces, least, top_value):
    level = 1.0
    for dim, shards_of in pieces:
        draws = jax.random.uniform(jax.random.fold_in(jax.random.fold_in(key, 6), dim), (shards_of,), jnp.float32, least / len(pieces), top_value / len(pieces))
        level = level * jnp.repeat(jnp.exp(draws), dims[dim] // shards_of).reshape((-1,) + (1,) * (len(dims) - 1 - dim))
    return level


def bell_draw(rng, dims, scale, reach, pieces=(), kind=jnp.bfloat16):
    drawn = jax.random.normal(rng, dims, jnp.float32) * scale
    if len(pieces) > 0:
        drawn = shard_levels(rng, dims, pieces, -0.22, 0.18) * drawn
    return jnp.clip(drawn, min=-reach, max=reach).astype(kind)


def setup_inputs(seed: int = 0) -> dict:
    splits = jax.random.split(jax.random.key(seed), 15)
    tokens = bell_draw(splits[0], (SEQS, SEQUENCE_TOKENS, MODEL_WIDTH), 1.0, 6.0, ((0, 8), (1, 4)))
    segments = draw_segments(jax.random.fold_in(splits[14], 71), 0)
    grad_out = bell_draw(splits[2], (SEQS, SEQUENCE_TOKENS, MODEL_WIDTH), 1.0, 6.0, ((0, 8), (1, 4)))
    attention_gain = jnp.clip(1.0 + 0.15 * jax.random.normal(splits[3], (MODEL_WIDTH,), jnp.float32), 0.25, 1.75).astype(jnp.bfloat16)
    query_weight = bell_draw(splits[4], (MODEL_WIDTH, QUERY_HEAD_COUNT * HEAD_SIZE), MODEL_WIDTH ** -0.5, 0.1875, ((0, 4),))
    key_matrix = bell_draw(splits[5], (MODEL_WIDTH, KEY_VALUE_HEADS * HEAD_SIZE), MODEL_WIDTH ** -0.5, 0.1875, ((0, 4),))
    value_matrix = bell_draw(splits[6], (MODEL_WIDTH, KEY_VALUE_HEADS * HEAD_SIZE), MODEL_WIDTH ** -0.5, 0.1875, ((0, 4),))
    query_gain = jnp.clip(1.0 + 0.15 * jax.random.normal(splits[7], (HEAD_SIZE,), jnp.float32), 0.25, 1.75).astype(jnp.bfloat16)
    key_gain = jnp.clip(1.0 + 0.15 * jax.random.normal(splits[8], (HEAD_SIZE,), jnp.float32), 0.25, 1.75).astype(jnp.bfloat16)
    output_weight = bell_draw(splits[9], (QUERY_HEAD_COUNT * HEAD_SIZE, MODEL_WIDTH), (max(QUERY_HEAD_COUNT * HEAD_SIZE // 128, 4)) ** -0.5, 1.5, ((1, 4),))
    mlp_gain = jnp.clip(1.0 + 0.15 * jax.random.normal(splits[10], (MODEL_WIDTH,), jnp.float32), 0.25, 1.75).astype(jnp.bfloat16)
    gate_weight = bell_draw(splits[11], (MODEL_WIDTH, FF), MODEL_WIDTH ** -0.5, 0.1875, ((0, 4),))
    up_weight = bell_draw(splits[12], (MODEL_WIDTH, FF), MODEL_WIDTH ** -0.5, 0.1875, ((0, 4),))
    down_weight = bell_draw(splits[13], (FF, MODEL_WIDTH), FF ** -0.5, 0.109375, ((0, 4),))
    return dict(tokens=tokens, segments=segments, grad_out=grad_out, attention_gain=attention_gain, query_weight=query_weight, key_matrix=key_matrix, value_matrix=value_matrix, query_gain=query_gain, key_gain=key_gain, output_weight=output_weight, mlp_gain=mlp_gain, gate_weight=gate_weight, up_weight=up_weight, down_weight=down_weight)


eps_norm = 1e-06
theta_base = 1000000.0
masked_score = -1e+30

@jax.custom_vjp
def lowered_copy(v):
    return lax.optimization_barrier(v.astype(jnp.bfloat16)).astype(jnp.float32)

@jax.custom_vjp
def lowered_backward(v):
    return v

def low_keep(v):
    return (lowered_copy(v), None)

def low_pass(kept, grad):
    return (grad,)

def back_keep(v):
    return (v, None)

def back_low(kept, grad):
    return (lowered_copy(grad),)
lowered_copy.defvjp(low_keep, low_pass)
lowered_backward.defvjp(back_keep, back_low)

def inverse_root(value_rows):
    return lax.rsqrt(lax.optimization_barrier(jnp.mean(value_rows * value_rows, axis=-1, keepdims=True)) + eps_norm)

def turned(value_rows):
    half = value_rows.shape[-1] // 2
    return jnp.concatenate([-value_rows[..., half:], value_rows[..., :half]], axis=-1)

def rotate(value_rows, cosine, sine):
    return value_rows * cosine + turned(value_rows) * sine

def tables(position):
    freqs = theta_base ** (-(jnp.arange(HEAD_SIZE // 2, dtype=jnp.float32) * 2.0) / HEAD_SIZE)
    angles = position.astype(jnp.float32)[..., None] * freqs
    angles = jnp.concatenate([angles, angles], axis=-1)
    return (jnp.cos(angles), jnp.sin(angles))

def apply_projection(left, weight):
    return jnp.einsum('gsd,df->gsf', left, weight, precision=lax.Precision.HIGHEST)

def attention(query_rotary, key_rot, value_rows, segments):
    item_count = query_rotary.shape[0]
    head_group = QUERY_HEAD_COUNT // KEY_VALUE_HEADS
    grouped_query = query_rotary.reshape(item_count, SEQUENCE_TOKENS, KEY_VALUE_HEADS, head_group, HEAD_SIZE)
    block = min(512, SEQUENCE_TOKENS)
    key_places = jnp.arange(SEQUENCE_TOKENS, dtype=jnp.int32)
    scale = HEAD_SIZE ** (-0.5)

    def one_block(start):
        query_block = lax.dynamic_slice_in_dim(grouped_query, start, block, 1)
        query_segments = lax.dynamic_slice_in_dim(segments, start, block, 1)
        places = start + jnp.arange(block, dtype=jnp.int32)
        raw = lowered_backward(jnp.einsum('gqhpd,gkhd->ghpqk', query_block, key_rot, precision=lax.Precision.HIGHEST))
        allowed = (query_segments[:, :, None] == segments[:, None, :]) & (places[None, :, None] >= key_places[None, None, :])
        scores = jnp.where(allowed[:, None, None], raw * scale, masked_score)
        peak = lax.optimization_barrier(jnp.max(scores, axis=-1, keepdims=True))
        expo = jnp.exp(scores - peak)
        probs = lowered_copy(expo / lax.optimization_barrier(jnp.sum(expo, axis=-1, keepdims=True)))
        return jnp.einsum('ghpqk,gkhd->gqhpd', probs, value_rows, precision=lax.Precision.HIGHEST)
    starts = (jnp.arange(SEQUENCE_TOKENS // block, dtype=jnp.int32) * block).astype(jnp.int32)
    blocks = lax.map(jax.checkpoint(one_block), starts)
    return jnp.moveaxis(blocks, 0, 1).reshape(item_count, SEQUENCE_TOKENS, QUERY_HEAD_COUNT * HEAD_SIZE)

def forward(tokens, segments, attention_gain, query_weight, key_matrix, value_matrix, query_gain, key_gain, output_weight, mlp_gain, gate_weight, up_weight, down_weight):
    item_count = tokens.shape[0]
    index = jnp.arange(SEQUENCE_TOKENS, dtype=jnp.int32)
    opening = lax.optimization_barrier(jnp.sum((segments[:, None, :] < segments[:, :, None]).astype(jnp.int32), axis=-1))
    cosine, sine = tables(index[None, :] - opening)
    cosine = cosine[:, :, None, :]
    sine = sine[:, :, None, :]
    first_normalized = lowered_copy(tokens * inverse_root(tokens) * attention_gain)
    query_lin = lowered_backward(apply_projection(first_normalized, query_weight)).reshape(item_count, SEQUENCE_TOKENS, QUERY_HEAD_COUNT, HEAD_SIZE)
    key_linear = lowered_backward(apply_projection(first_normalized, key_matrix)).reshape(item_count, SEQUENCE_TOKENS, KEY_VALUE_HEADS, HEAD_SIZE)
    value_rows = lowered_copy(lowered_backward(apply_projection(first_normalized, value_matrix))).reshape(item_count, SEQUENCE_TOKENS, KEY_VALUE_HEADS, HEAD_SIZE)
    query_rotary = lowered_copy(rotate(query_lin * inverse_root(query_lin) * query_gain, cosine, sine))
    key_rot = lowered_copy(rotate(key_linear * inverse_root(key_linear) * key_gain, cosine, sine))
    attended = lowered_copy(lowered_backward(attention(query_rotary, key_rot, value_rows, segments)))
    residual_one = tokens + lowered_backward(apply_projection(attended, output_weight))
    normed_two = lowered_copy(residual_one * inverse_root(residual_one) * mlp_gain)
    gate = lowered_backward(apply_projection(normed_two, gate_weight))
    upper = lowered_backward(apply_projection(normed_two, up_weight))
    hidden = lowered_copy(jax.nn.silu(gate) * upper)
    return residual_one + apply_projection(hidden, down_weight)

def reference(tokens, segments, grad_out, attention_gain, query_weight, key_matrix, value_matrix, query_gain, key_gain, output_weight, mlp_gain, gate_weight, up_weight, down_weight):
    weights = tuple((item.astype(jnp.float32) for item in (attention_gain, query_weight, key_matrix, value_matrix, query_gain, key_gain, output_weight, mlp_gain, gate_weight, up_weight, down_weight)))
    item_count = max((item for item in range(1, SEQS + 1) if SEQS % item == 0 and item * SEQUENCE_TOKENS <= max(4096, SEQUENCE_TOKENS)))
    inputs = tokens.astype(jnp.float32).reshape(SEQS // item_count, item_count, SEQUENCE_TOKENS, MODEL_WIDTH)
    cotangent = grad_out.astype(jnp.float32).reshape(SEQS // item_count, item_count, SEQUENCE_TOKENS, MODEL_WIDTH)
    grouped = segments.reshape(SEQS // item_count, item_count, SEQUENCE_TOKENS)

    def one_group(totals, item):
        span_in, span_seg, span_cot = item
        result, pull = jax.vjp(lambda first, *rest: forward(first, span_seg, *rest), span_in, *weights)
        grads = pull(span_cot)
        totals = tuple((left + right for left, right in zip(totals, grads[1:])))
        return (totals, (result, grads[0]))
    zeros = tuple((jnp.zeros_like(item) for item in weights))
    totals, (results, input_grads) = lax.scan(one_group, zeros, (inputs, grouped, cotangent))
    layer_out = results.reshape(SEQS, SEQUENCE_TOKENS, MODEL_WIDTH).astype(jnp.bfloat16)
    grad_tokens = input_grads.reshape(SEQS, SEQUENCE_TOKENS, MODEL_WIDTH)
    grad_attention_gain, grad_query_weight, grad_key_weight, grad_value_weight, grad_query_gain, grad_key_gain, grad_output_weight, grad_mlp_gain, grad_gate_weight, grad_up_weight, grad_down_weight = totals
    return (layer_out, grad_tokens, grad_attention_gain, grad_query_weight, grad_key_weight, grad_value_weight, grad_query_gain, grad_key_gain, grad_output_weight, grad_mlp_gain, grad_gate_weight, grad_up_weight, grad_down_weight)
```

```python
import functools
import math

import jax
import jax.numpy as jnp
from jax import lax
from jax.experimental import pallas as pl
from jax.experimental.pallas import tpu as pltpu
from jax.sharding import PartitionSpec as P

eps_norm = 1e-06
theta_base = 1000000.0
f32 = jnp.float32
bf16 = jnp.bfloat16
vmem_bytes = 50 * 1024 * 1024


def dot(left, right):
    return lax.dot_general(left, right, (((1,), (0,)), ((), ())), preferred_element_type=f32)


def dot_nt(left, right):
    return lax.dot_general(left, right, (((1,), (1,)), ((), ())), preferred_element_type=f32)


def dot_tn(left, right):
    return lax.dot_general(left, right, (((0,), (0,)), ((), ())), preferred_element_type=f32)


def inverse_root(rows):
    return lax.rsqrt(jnp.mean(rows * rows, axis=-1, keepdims=True) + eps_norm)


def norm_back(grad, rows, scale):
    return scale * grad - rows * (scale * scale * scale) * jnp.mean(
        grad * rows, axis=-1, keepdims=True
    )


def params():
    return pltpu.CompilerParams(vmem_limit_bytes=vmem_bytes)


def cost(flops, moved, trans=0):
    return pl.CostEstimate(flops=int(flops), bytes_accessed=int(moved), transcendentals=int(trans))


def half_turn(rows):
    return pltpu.roll(rows, rows.shape[-1] // 2, axis=1)


def project_kernel(q_heads, k_heads, tok, gain, weight, cosine, sine, gains, normed, lin, rot, val):
    rows = tok[...].astype(f32)
    low = (rows * inverse_root(rows) * gain[...]).astype(bf16)
    normed[...] = low
    head = cosine.shape[1]
    full = dot(low, weight[...])
    cos_, sin_ = cosine[...], sine[...]
    for index in range(q_heads + k_heads):
        part = full[:, index * head : (index + 1) * head]
        lin[:, index * head : (index + 1) * head] = part
        which = 0 if index < q_heads else 1
        unit = part * inverse_root(part) * gains[which : which + 1, :]
        rot[:, index * head : (index + 1) * head] = (unit * cos_ + half_turn(unit) * sin_).astype(
            bf16
        )
    val[...] = full[:, (q_heads + k_heads) * head :].astype(bf16)


def project(tok, gain, weight, cosine, sine, gains, q_heads, k_heads, block):
    total, width = tok.shape
    head = cosine.shape[1]
    qk = (q_heads + k_heads) * head
    kv = k_heads * head
    row = lambda n: pl.BlockSpec((block, n), lambda i: (i, 0))
    fixed = lambda a, b: pl.BlockSpec((a, b), lambda i: (0, 0))
    return pl.pallas_call(
        functools.partial(project_kernel, q_heads, k_heads),
        grid=(total // block,),
        in_specs=[
            row(width),
            fixed(1, width),
            fixed(*weight.shape),
            row(head),
            row(head),
            fixed(2, head),
        ],
        out_specs=[row(width), row(qk), row(qk), row(kv)],
        out_shape=[
            jax.ShapeDtypeStruct((total, width), bf16),
            jax.ShapeDtypeStruct((total, qk), f32),
            jax.ShapeDtypeStruct((total, qk), bf16),
            jax.ShapeDtypeStruct((total, kv), bf16),
        ],
        compiler_params=params(),
        cost_estimate=cost(2 * total * weight.size, 2 * weight.size + total * width * 12),
    )(tok, gain, weight, cosine, sine, gains)


def allowed_pairs(j, k, start_q, start_k, block, seg_col, seg_row):
    own = seg_col[pl.ds(start_q, block), :]
    other = seg_row[:, pl.ds(start_k, block)]
    allowed = own == other
    if j == k:
        at_q = lax.broadcasted_iota(jnp.int32, (block, block), 0)
        at_k = lax.broadcasted_iota(jnp.int32, (block, block), 1)
        allowed = allowed & (at_q >= at_k)
    return allowed


def attend_kernel(blocks, group, factor, order, query, key, val, seg_col, seg_row, out, logs):
    total, head = key.shape
    block = total // blocks
    flip = order[0]
    start = [pl.multiple_of((jnp.int32(i) ^ flip) * block, block) for i in range(blocks)]
    ones = jnp.ones((block, head), bf16)
    for j in range(blocks):
        stacked = jnp.concatenate(
            [query[pl.ds(start[j], block), h * head : (h + 1) * head] for h in range(group)], axis=0
        )
        acc = jnp.zeros((group * block, 2 * head), f32)
        for k in range(j + 1):
            raw = dot_nt(stacked, key[pl.ds(start[k], block), :])
            allowed = allowed_pairs(j, k, start[j], start[k], block, seg_col, seg_row)
            allowed = jnp.concatenate([allowed] * group, axis=0)
            probs = jnp.where(allowed, jnp.exp2(raw * factor), 0.0).astype(bf16)
            both = jnp.concatenate([val[pl.ds(start[k], block), :], ones], axis=1)
            acc = acc + dot(probs, both)
        sums = acc[:, head:]
        result = acc[:, :head] / sums
        log_sums = jnp.log2(sums)
        for h in range(group):
            out[pl.ds(start[j], block), h * head : (h + 1) * head] = result[
                h * block : (h + 1) * block
            ]
            logs[pl.ds(start[j], block), h * head : (h + 1) * head] = log_sums[
                h * block : (h + 1) * block
            ]


def attend(order, rot, val, seg_col, seg_row, q_heads, k_heads, head, blocks):
    total = rot.shape[0]
    group = q_heads // k_heads
    factor = head**-0.5 * math.log2(math.e)
    wide = pl.BlockSpec((total, group * head), lambda g, o: (0, g))
    return pl.pallas_call(
        functools.partial(attend_kernel, blocks, group, factor),
        grid_spec=pltpu.PrefetchScalarGridSpec(
            num_scalar_prefetch=1,
            grid=(k_heads,),
            in_specs=[
                wide,
                pl.BlockSpec((total, head), lambda g, o: (0, q_heads + g)),
                pl.BlockSpec((total, head), lambda g, o: (0, g)),
                pl.BlockSpec((total, 1), lambda g, o: (0, 0)),
                pl.BlockSpec((1, total), lambda g, o: (0, 0)),
            ],
            out_specs=[wide, wide],
        ),
        out_shape=[jax.ShapeDtypeStruct((total, q_heads * head), f32)] * 2,
        compiler_params=params(),
        cost_estimate=cost(4 * total * total * q_heads * head, total * q_heads * head * 12),
    )(order, rot, rot, val, seg_col, seg_row)


def attend_back_kernel(
    blocks, group, factor, scale, order, query, key, val, out_grad, out, logs, seg_col, seg_row,
    query_grad, key_grad, val_grad,
):
    total, head = key.shape
    block = total // blocks
    flip = order[0]
    start = [pl.multiple_of((jnp.int32(i) ^ flip) * block, block) for i in range(blocks)]

    def heads_of(ref, at):
        return jnp.concatenate(
            [ref[pl.ds(at, block), h * head : (h + 1) * head] for h in range(group)], axis=0
        )

    deltas = []
    for j in range(blocks):
        product = heads_of(out_grad, start[j]).astype(f32) * heads_of(out, start[j])
        deltas.append(jnp.sum(product, axis=1, keepdims=True))
    sums = [None] * blocks
    for k in range(blocks):
        key_block = key[pl.ds(start[k], block), :]
        val_block = val[pl.ds(start[k], block), :]
        key_sum = jnp.zeros((block, head), f32)
        val_sum = jnp.zeros((block, head), f32)
        for j in range(k, blocks):
            stacked = heads_of(query, start[j])
            grads = heads_of(out_grad, start[j])
            logged = heads_of(logs, start[j])
            logged = jnp.concatenate([logged] * (block // head), axis=1)
            raw = dot_nt(stacked, key_block)
            allowed = allowed_pairs(j, k, start[j], start[k], block, seg_col, seg_row)
            allowed = jnp.concatenate([allowed] * group, axis=0)
            probs = jnp.where(allowed, jnp.exp2(raw * factor - logged), 0.0)
            prob_grad = dot_nt(grads, val_block)
            score_grad = (probs * (prob_grad - deltas[j]) * scale).astype(bf16)
            val_sum = val_sum + dot_tn(probs.astype(bf16), grads)
            key_sum = key_sum + dot_tn(score_grad, stacked)
            piece = dot(score_grad, key_block)
            sums[j] = piece if k == 0 else sums[j] + piece
        key_grad[pl.ds(start[k], block), :] = key_sum
        val_grad[pl.ds(start[k], block), :] = val_sum
        for h in range(group):
            query_grad[pl.ds(start[k], block), h * head : (h + 1) * head] = sums[k][
                h * block : (h + 1) * block
            ]


def attend_back(order, rot, val, out_grad, out, logs, seg_col, seg_row, q_heads, k_heads, head, blocks):
    total = rot.shape[0]
    group = q_heads // k_heads
    scale = head**-0.5
    wide = pl.BlockSpec((total, group * head), lambda g, o: (0, g))
    thin = pl.BlockSpec((total, head), lambda g, o: (0, g))
    return pl.pallas_call(
        functools.partial(attend_back_kernel, blocks, group, scale * math.log2(math.e), scale),
        grid_spec=pltpu.PrefetchScalarGridSpec(
            num_scalar_prefetch=1,
            grid=(k_heads,),
            in_specs=[
                wide,
                pl.BlockSpec((total, head), lambda g, o: (0, q_heads + g)),
                thin,
                wide,
                wide,
                wide,
                pl.BlockSpec((total, 1), lambda g, o: (0, 0)),
                pl.BlockSpec((1, total), lambda g, o: (0, 0)),
            ],
            out_specs=[wide, thin, thin],
        ),
        out_shape=[
            jax.ShapeDtypeStruct((total, q_heads * head), f32),
            jax.ShapeDtypeStruct((total, k_heads * head), f32),
            jax.ShapeDtypeStruct((total, k_heads * head), f32),
        ],
        compiler_params=params(),
        cost_estimate=cost(10 * total * total * q_heads * head, total * q_heads * head * 20),
    )(order, rot, rot, val, out_grad, out, logs, seg_col, seg_row)


def feed_kernel(norm, cot, weight, down, hidden, gate_up_grad, norm_grad, out):
    units = down.shape[0]
    low = norm[...]
    gate = dot(low, weight[:, :units])
    upper = dot(low, weight[:, units:])
    sigma = 1.0 / (1.0 + jnp.exp(-gate))
    silu = gate * sigma
    hid = (silu * upper).astype(bf16)
    hidden[...] = hid
    back = dot_nt(cot[...], down[...])
    gate_grad = (back * upper * sigma * (1.0 + gate * (1.0 - sigma))).astype(bf16)
    up_grad = (back * silu).astype(bf16)
    gate_up_grad[:, :units] = gate_grad
    gate_up_grad[:, units:] = up_grad
    norm_grad[...] = (
        dot_nt(gate_grad, weight[:, :units]) + dot_nt(up_grad, weight[:, units:])
    ).astype(bf16)
    out[...] = dot(hid, down[...]).astype(bf16)


def feed(norm, cot, weight, down, block):
    total, width = norm.shape
    units = down.shape[0]
    row = lambda n: pl.BlockSpec((block, n), lambda i: (i, 0))
    fixed = lambda a, b: pl.BlockSpec((a, b), lambda i: (0, 0))
    return pl.pallas_call(
        feed_kernel,
        grid=(total // block,),
        in_specs=[row(width), row(width), fixed(*weight.shape), fixed(*down.shape)],
        out_specs=[row(units), row(2 * units), row(width), row(width)],
        out_shape=[
            jax.ShapeDtypeStruct((total, units), bf16),
            jax.ShapeDtypeStruct((total, 2 * units), bf16),
            jax.ShapeDtypeStruct((total, width), bf16),
            jax.ShapeDtypeStruct((total, width), bf16),
        ],
        compiler_params=params(),
        cost_estimate=cost(12 * total * down.size, 6 * down.size + total * width * 16, total * units),
    )(norm, cot, weight, down)


def unproject_kernel(
    q_heads, k_heads, query_grad, key_grad, val_grad, lin, cosine, sine, gains, weight, tok,
    lin_grad, norm_grad, gain_sum, head_sum,
):
    head = cosine.shape[1]
    cos_, sin_ = cosine[...], sine[...]
    sums = [jnp.zeros((1, head), f32), jnp.zeros((1, head), f32)]
    for index in range(q_heads + k_heads):
        which = 0 if index < q_heads else 1
        ref, place = (query_grad, index) if which == 0 else (key_grad, index - q_heads)
        turned = ref[:, place * head : (place + 1) * head]
        grad = turned * cos_ - half_turn(turned) * sin_
        rows = lin[:, index * head : (index + 1) * head]
        scale = inverse_root(rows)
        sums[which] = sums[which] + jnp.sum(grad * rows * scale, axis=0, keepdims=True)
        lin_grad[:, index * head : (index + 1) * head] = norm_back(
            grad * gains[which : which + 1, :], rows, scale
        ).astype(bf16)
    lin_grad[:, (q_heads + k_heads) * head :] = val_grad[...].astype(bf16)
    normed_grad = dot_nt(lin_grad[...], weight[...])
    norm_grad[...] = normed_grad.astype(bf16)
    rows = tok[...].astype(f32)
    gain_part = jnp.sum(normed_grad * rows * inverse_root(rows), axis=0, keepdims=True)

    @pl.when(pl.program_id(0) == 0)
    def _():
        gain_sum[...] = jnp.zeros_like(gain_sum)
        head_sum[...] = jnp.zeros_like(head_sum)

    gain_sum[...] += gain_part
    head_sum[...] += jnp.concatenate(sums, axis=0)


def unproject(query_grad, key_grad, val_grad, lin, cosine, sine, gains, weight, tok, q_heads, k_heads, block):
    total, width = tok.shape
    head = cosine.shape[1]
    row = lambda n: pl.BlockSpec((block, n), lambda i: (i, 0))
    fixed = lambda a, b: pl.BlockSpec((a, b), lambda i: (0, 0))
    return pl.pallas_call(
        functools.partial(unproject_kernel, q_heads, k_heads),
        grid=(total // block,),
        in_specs=[
            row(q_heads * head),
            row(k_heads * head),
            row(k_heads * head),
            row((q_heads + k_heads) * head),
            row(head),
            row(head),
            fixed(2, head),
            fixed(*weight.shape),
            row(width),
        ],
        out_specs=[row(weight.shape[1]), row(width), fixed(1, width), fixed(2, head)],
        out_shape=[
            jax.ShapeDtypeStruct((total, weight.shape[1]), bf16),
            jax.ShapeDtypeStruct((total, width), bf16),
            jax.ShapeDtypeStruct((1, width), f32),
            jax.ShapeDtypeStruct((2, head), f32),
        ],
        compiler_params=params(),
        cost_estimate=cost(2 * total * weight.size, 2 * weight.size + total * width * 16),
    )(query_grad, key_grad, val_grad, lin, cosine, sine, gains, weight, tok)


def place_kernel(count, outs, moves, scalars, *refs):
    inputs, results = refs[:count], refs[count:]
    shard, pos = scalars[0], scalars[1]
    for source, index, rows, columns, target, spot in moves:
        piece = inputs[source][index + (slice(rows[0], rows[1]), slice(columns[0], columns[1]))]
        row, column = spot(shard, pos)
        results[target][
            pl.ds(pl.multiple_of(row, 16), rows[1] - rows[0]),
            pl.ds(pl.multiple_of(column, 128), columns[1] - columns[0]),
        ] = piece.astype(results[target].dtype)


def place(scalars, inputs, out_shapes, moves):
    moved = sum(item.size * 2 for item in inputs) + sum(
        math.prod(shape) * (4 if kind == f32 else 2) for shape, kind in out_shapes
    )
    whole = pl.BlockSpec(memory_space=pltpu.VMEM)
    return pl.pallas_call(
        functools.partial(place_kernel, len(inputs), len(out_shapes), moves),
        in_specs=[pl.BlockSpec(memory_space=pltpu.SMEM)] + [whole] * len(inputs),
        out_specs=[whole] * len(out_shapes),
        out_shape=[jax.ShapeDtypeStruct(shape, kind) for shape, kind in out_shapes],
        compiler_params=params(),
        cost_estimate=cost(0, moved),
    )(scalars, *inputs)


class Moves:
    def __init__(self):
        self.shards = lax.axis_size("shard")
        self.reps = lax.axis_size("rep")
        self.mine = lax.axis_index("shard")
        self.direct = self.shards == 4 and self.reps == 8
        self.flip = self.mine if self.direct else jnp.int32(0)
        rep = lax.axis_index("rep")
        self.pos = jnp.where(rep % 2 == 0, rep // 2, 7 - rep // 2)
        self.ring = [0, 2, 4, 6, 7, 5, 3, 1]
        self.scalars = jnp.stack([self.mine, self.pos]).astype(jnp.int32)

    def swap(self, item, mask):
        return lax.ppermute(item, "shard", [(i, i ^ mask) for i in range(4)])

    def up(self, item):
        ring = self.ring
        return lax.ppermute(item, "rep", [(ring[i], ring[(i + 1) % 8]) for i in range(8)])

    def down(self, item):
        ring = self.ring
        return lax.ppermute(item, "rep", [(ring[(i + 1) % 8], ring[i]) for i in range(8)])

    def gather(self, item):
        if not self.direct:
            return lax.all_gather(item, "shard", axis=0, tiled=True)
        far = self.swap(item, 2)
        near = self.swap(item, 1)
        cross = self.swap(far, 1)
        return jnp.concatenate([item, near, far, cross], axis=0)

    def scatter(self, item):
        if not self.direct:
            return lax.psum_scatter(item.astype(f32), "shard", scatter_dimension=0, tiled=True)
        rows = item.shape[0] // 4
        own, near, far, cross = (item[i * rows : (i + 1) * rows] for i in range(4))
        far = self.swap(far + self.swap(cross, 1), 2)
        near = self.swap(near, 1)
        return own.astype(f32) + near.astype(f32) + far.astype(f32)

    def ring_gather(self, item, axis):
        half = item.shape[axis] // 2
        first = lambda v: lax.slice_in_dim(v, 0, half, axis=axis)
        last = lambda v: lax.slice_in_dim(v, half, 2 * half, axis=axis)
        u1, d1 = self.up(item), self.down(item)
        u2, d2 = self.up(u1), self.down(d1)
        u3, d3 = self.up(u2), self.down(d2)
        u4, d4 = self.up(first(u3)), self.down(last(d3))
        return [
            (item, 0, None), (u1, -1, None), (d1, 1, None), (u2, -2, None), (d2, 2, None),
            (u3, -3, None), (d3, 3, None), (u4, 4, 0), (d4, 4, 1),
        ]

    def ring_scatter(self, item, axis):
        def local(offset):
            return lax.dynamic_index_in_dim(item, (self.pos + offset) % 8, axis, keepdims=False)

        first = lambda v: lax.slice_in_dim(v, 0, 1, axis=axis)
        last = lambda v: lax.slice_in_dim(v, 1, 2, axis=axis)
        u = self.up(first(local(4)))
        d = self.down(last(local(4)))
        a, b = local(3), local(5)
        u = self.up(jnp.concatenate([first(a) + u, last(a)], axis=axis))
        d = self.down(jnp.concatenate([first(b), last(b) + d], axis=axis))
        u, d = self.up(u + local(2)), self.down(d + local(6))
        u, d = self.up(u + local(1)), self.down(d + local(7))
        return (u.astype(f32) + d.astype(f32) + local(0).astype(f32)).astype(bf16)

    def exchange(self, block):
        return [
            block(0), self.swap(block(1), 1), self.swap(block(2), 2), self.swap(block(3), 3),
        ]


def fetch(moves, block, rows, spot, shape):
    eighth = rows // 8
    pos = moves.pos
    own = block(0, 0, rows)
    width = own.shape[1]
    near = moves.swap(block(1, 0, rows), 1)
    begin = pos * eighth
    piece = jnp.stack([block(2, begin, eighth), block(3, begin, eighth)])
    parts = moves.ring_gather(moves.swap(piece, 2), 1)
    far = jnp.concatenate([part[0] for part, _, _ in parts], axis=0)
    cross = moves.swap(jnp.concatenate([part[1] for part, _, _ in parts], axis=0), 1)
    todo = []

    def where(which, offset, half):
        def at(shard, pos_):
            line = 0
            if offset is not None:
                line = lax.rem(pos_ + (offset + 8), 8) * eighth + half * (eighth // 2)
            return spot(shard ^ which, line)

        return at

    for which in (0, 1):
        todo.append((which, (), (0, rows), (0, width), 0, where(which, None, 0)))
    for which in (2, 3):
        line = 0
        for part, offset, half in parts:
            size = part.shape[1]
            todo.append(
                (which, (), (line, line + size), (0, width), 0, where(which, offset, half or 0))
            )
            line += size
    return place(moves.scalars, [own, near, far, cross], [(shape, bf16)], todo)[0]


def per_device(
    tokens, segments, grad_out, attention_gain, query_weight, key_matrix, value_matrix, query_gain,
    key_gain, output_weight, mlp_gain, gate_weight, up_weight, down_weight,
):
    moves = Moves()
    shards, mine, direct = moves.shards, moves.mine, moves.direct
    rows, width = tokens.shape[1:]
    total = rows * shards
    slice_width = attention_gain.shape[0]
    head_slice = query_gain.shape[0]
    head = head_slice * shards
    k_heads = key_matrix.shape[1] // head // shards
    q_heads = query_weight.shape[1] // head // shards
    q_width, k_width = q_heads * head, k_heads * head
    units = down_weight.shape[0]
    own_tokens = tokens[0]
    cot = grad_out[0]

    small = jnp.concatenate(
        [attention_gain, mlp_gain, query_gain, key_gain, segments[0].astype(bf16)]
    )[None]
    small = moves.gather(small)
    if direct:
        whole = jnp.where(mine % 2 == 0, small, small[jnp.array([1, 0, 3, 2])])
        whole = jnp.where(mine // 2 == 0, whole, whole[jnp.array([2, 3, 0, 1])])
    else:
        whole = small
    cut = [slice_width, 2 * slice_width, 2 * slice_width + head_slice, 2 * slice_width + 2 * head_slice]
    input_gain = whole[:, : cut[0]].reshape(1, width).astype(f32)
    second_gain = whole[:, cut[0] : cut[1]].reshape(1, width).astype(f32)
    head_gains = jnp.stack(
        [whole[:, cut[1] : cut[2]].reshape(head), whole[:, cut[2] : cut[3]].reshape(head)]
    ).astype(f32)
    segs = small[:, cut[3] :].reshape(total).astype(f32)
    index = jnp.arange(shards, dtype=jnp.int32) ^ moves.flip
    places = (index[:, None] * rows + jnp.arange(rows, dtype=jnp.int32)[None]).reshape(total)
    firsts = jnp.sum((segs < 0.5).astype(jnp.int32))
    seconds = jnp.sum((segs < 1.5).astype(jnp.int32))
    opening = jnp.where(segs < 0.5, 0, jnp.where(segs < 1.5, firsts, seconds))
    freqs = theta_base ** (-(jnp.arange(head // 2, dtype=f32) * 2.0) / head)
    angles = (places - opening).astype(f32)[:, None] * freqs
    cosine, sine = jnp.cos(angles), jnp.sin(angles)
    cosine = jnp.concatenate([cosine, cosine], axis=1)
    sine = jnp.concatenate([-sine, sine], axis=1)
    seg_col, seg_row = segs[:, None], segs[None, :]
    order = moves.flip.astype(jnp.int32)[None]

    def columns(item, i, begin, count, size):
        return lax.dynamic_slice(item, (begin, (mine ^ i) * size), (count, size))

    if direct:
        qkv_weight = fetch(
            moves,
            lambda i, begin, n: jnp.concatenate(
                [
                    columns(query_weight, i, begin, n, q_width),
                    columns(key_matrix, i, begin, n, k_width),
                    columns(value_matrix, i, begin, n, k_width),
                ],
                axis=1,
            ),
            slice_width,
            lambda source, line: (source * slice_width + line, 0),
            (width, q_width + 2 * k_width),
        )
        out_weight = fetch(
            moves,
            lambda i, begin, n: lax.dynamic_slice(
                output_weight, ((mine ^ i) * q_width + begin, 0), (n, slice_width)
            ),
            q_width,
            lambda source, line: (line, source * slice_width),
            (q_width, width),
        )
        feed_weight = fetch(
            moves,
            lambda i, begin, n: jnp.concatenate(
                [
                    columns(gate_weight, i, begin, n, units),
                    columns(up_weight, i, begin, n, units),
                ],
                axis=1,
            ),
            slice_width,
            lambda source, line: (source * slice_width + line, 0),
            (width, 2 * units),
        )
    else:
        spread = lambda item: lax.all_to_all(item, "shard", split_axis=1, concat_axis=0, tiled=True)
        qkv_weight = jnp.concatenate(
            [spread(query_weight), spread(key_matrix), spread(value_matrix)], axis=1
        )
        out_weight = lax.all_to_all(output_weight, "shard", split_axis=0, concat_axis=1, tiled=True)
        feed_weight = jnp.concatenate([spread(gate_weight), spread(up_weight)], axis=1)

    all_tokens = moves.gather(own_tokens)
    normed_one, lin, rot, val = project(
        all_tokens, input_gain, qkv_weight, cosine, sine, head_gains, q_heads, k_heads, rows
    )
    attended, logs = attend(order, rot, val, seg_col, seg_row, q_heads, k_heads, head, shards)
    attended_low = attended.astype(bf16)
    inputs = own_tokens.astype(f32)
    residual_one = inputs + moves.scatter(dot(attended_low, out_weight).astype(bf16))
    residual_scale = inverse_root(residual_one)
    normed_two = moves.gather((residual_one * residual_scale * second_gain).astype(bf16))

    all_cot = moves.gather(cot)
    hidden, gate_up_grad, norm_grad, out_part = feed(normed_two, all_cot, feed_weight, down_weight, rows)
    share_down = dot_tn(hidden, all_cot).astype(bf16)
    share_feed = dot_tn(normed_two, gate_up_grad).astype(bf16)
    layer_out = (residual_one + moves.scatter(out_part)).astype(bf16)
    normed_grad_two = moves.scatter(norm_grad)
    mlp_gain_part = jnp.sum(normed_grad_two * residual_one * residual_scale, axis=0)
    residual_grad = cot.astype(f32) + norm_back(
        normed_grad_two * second_gain, residual_one, residual_scale
    )
    branch_grad = moves.gather(residual_grad.astype(bf16))

    out_grad = dot_nt(branch_grad, out_weight).astype(bf16)
    share_out = dot_tn(attended_low, branch_grad).astype(bf16)
    query_grad, key_grad, val_grad = attend_back(
        order, rot, val, out_grad, attended, logs, seg_col, seg_row, q_heads, k_heads, head, shards
    )
    lin_grad, norm_one_part, gain_part, head_part = unproject(
        query_grad, key_grad, val_grad, lin, cosine, sine, head_gains, qkv_weight, all_tokens,
        q_heads, k_heads, rows,
    )
    share_qkv = dot_tn(normed_one, lin_grad).astype(bf16)
    normed_grad_one = moves.scatter(norm_one_part)
    grad_tokens = residual_grad + norm_back(normed_grad_one * input_gain, inputs, inverse_root(inputs))

    gains = jnp.concatenate([gain_part[0], mlp_gain_part, head_part.reshape(2 * head)])[None]
    if direct:
        gains = gains + moves.swap(gains, 1)
        gains = gains + moves.swap(gains, 2)
        for mask in (1, 2, 4):
            gains = gains + lax.ppermute(gains, "rep", [(i, i ^ mask) for i in range(8)])
    else:
        gains = lax.psum(gains, ("shard", "rep"))
    gains = gains[0]

    def own_part(begin, size):
        return lax.dynamic_slice_in_dim(gains, begin + mine * size, size, 0)

    grad_attention_gain = own_part(0, slice_width)
    grad_mlp_gain = own_part(width, slice_width)
    grad_query_gain = own_part(2 * width, head_slice)
    grad_key_gain = own_part(2 * width + head, head_slice)

    if direct:
        ring_at = lambda pos_, offset: lax.rem(pos_ + (offset + 8), 8)

        def finish_columns(share, pieces):
            n = share.shape[1]
            sub = slice_width // 16
            chunk = moves.ring_scatter(share.reshape(4, 8, 2, sub, n), 1)
            got = moves.exchange(lambda i: lax.dynamic_index_in_dim(chunk, mine ^ i, 0, keepdims=False))
            parts = moves.ring_gather(jnp.stack(got), 1)
            todo = []
            for source, (part, offset, half) in enumerate(parts):
                for i in range(4):
                    for h in range(part.shape[1]):
                        begin = 0
                        for target, size in enumerate(pieces):

                            def at(shard, pos_, i=i, line=(half or 0) + h, offset=offset, size=size):
                                row = ring_at(pos_, offset) * (2 * sub) + line * sub
                                return row, (shard ^ i) * size

                            todo.append((source, (i, h), (0, sub), (begin, begin + size), target, at))
                            begin += size
            shapes = [((slice_width, size * shards), f32) for size in pieces]
            return place(moves.scalars, [part for part, _, _ in parts], shapes, todo)

        def finish_down(share):
            sub = units // 16
            chunk = moves.ring_scatter(share.reshape(8, 2, sub, width), 0)
            parts = moves.ring_gather(chunk, 0)
            todo = []
            for source, (part, offset, half) in enumerate(parts):
                for h in range(part.shape[0]):

                    def at(shard, pos_, line=(half or 0) + h, offset=offset):
                        return ring_at(pos_, offset) * (2 * sub) + line * sub, 0

                    todo.append((source, (h,), (0, sub), (0, width), 0, at))
            return place(
                moves.scalars, [part for part, _, _ in parts], [((units, width), f32)], todo
            )[0]

        def finish_out(share):
            sub = q_width // 16
            chunk = moves.ring_scatter(share.reshape(8, 2, sub, width), 0)
            got = moves.exchange(
                lambda i: lax.dynamic_slice_in_dim(chunk, (mine ^ i) * slice_width, slice_width, 2)
            )
            parts = moves.ring_gather(jnp.stack(got), 1)
            todo = []
            for source, (part, offset, half) in enumerate(parts):
                for i in range(4):
                    for h in range(part.shape[1]):

                        def at(shard, pos_, i=i, line=(half or 0) + h, offset=offset):
                            row = ring_at(pos_, offset) * (2 * sub) + line * sub
                            return (shard ^ i) * q_width + row, 0

                        todo.append((source, (i, h), (0, sub), (0, slice_width), 0, at))
            return place(
                moves.scalars,
                [part for part, _, _ in parts],
                [((q_width * shards, slice_width), f32)],
                todo,
            )[0]

        grad_down = finish_down(share_down)
        grad_gate, grad_up = finish_columns(share_feed, [units, units])
        grad_output = finish_out(share_out)
        grad_query, grad_key, grad_value = finish_columns(share_qkv, [q_width, k_width, k_width])
    else:

        def finish(share, begin, size):
            part = lax.all_to_all(
                share[:, begin : begin + size], "shard", split_axis=0, concat_axis=1, tiled=True
            )
            return lax.psum(part, "rep").astype(f32)

        grad_down = lax.psum(share_down, "rep").astype(f32)
        grad_gate = finish(share_feed, 0, units)
        grad_up = finish(share_feed, units, units)
        grad_output = lax.psum(
            lax.all_to_all(share_out, "shard", split_axis=1, concat_axis=0, tiled=True), "rep"
        ).astype(f32)
        grad_query = finish(share_qkv, 0, q_width)
        grad_key = finish(share_qkv, q_width, k_width)
        grad_value = finish(share_qkv, q_width + k_width, k_width)

    return (
        layer_out[None], grad_tokens[None], grad_attention_gain, grad_query, grad_key, grad_value,
        grad_query_gain, grad_key_gain, grad_output, grad_mlp_gain, grad_gate, grad_up, grad_down,
    )


def solution(mesh):
    rows_over = P("shard", None)
    return jax.shard_map(
        per_device,
        mesh=mesh,
        in_specs=(
            P("rep", "shard", None), P("rep", "shard"), P("rep", "shard", None), P("shard"), rows_over,
            rows_over, rows_over, P("shard"), P("shard"), P(None, "shard"), P("shard"), rows_over,
            rows_over, rows_over,
        ),
        out_specs=(
            P("rep", "shard", None), P("rep", "shard", None), P("shard"), rows_over, rows_over,
            rows_over, P("shard"), P("shard"), P(None, "shard"), P("shard"), rows_over, rows_over,
            rows_over,
        ),
        check_vma=False,
    )
```

```python
import functools
import math

import jax
import jax.numpy as jnp
from jax import lax
from jax.experimental import pallas as pl
from jax.experimental.pallas import tpu as pltpu
from jax.sharding import PartitionSpec as P

eps_norm = 1e-06
theta_base = 1000000.0
f32 = jnp.float32
bf16 = jnp.bfloat16
vmem_bytes = 50 * 1024 * 1024


def dot(left, right):
    return lax.dot_general(left, right, (((1,), (0,)), ((), ())), preferred_element_type=f32)


def dot_nt(left, right):
    return lax.dot_general(left, right, (((1,), (1,)), ((), ())), preferred_element_type=f32)


def dot_tn(left, right):
    return lax.dot_general(left, right, (((0,), (0,)), ((), ())), preferred_element_type=f32)


def inverse_root(rows):
    return lax.rsqrt(jnp.mean(rows * rows, axis=-1, keepdims=True) + eps_norm)


def norm_back(grad, rows, scale):
    return scale * grad - rows * (scale * scale * scale) * jnp.mean(
        grad * rows, axis=-1, keepdims=True
    )


def params():
    return pltpu.CompilerParams(vmem_limit_bytes=vmem_bytes)


def cost(flops, moved, trans=0):
    return pl.CostEstimate(flops=int(flops), bytes_accessed=int(moved), transcendentals=int(trans))


def half_turn(rows):
    return pltpu.roll(rows, rows.shape[-1] // 2, axis=1)


def pick(refs, held):
    for k, ref in enumerate(refs):

        @pl.when(pl.program_id(0) == k)
        def _(ref=ref):
            held[...] = ref[...]


def project_kernel(
    q_heads, k_heads, count, gain, weight, cosine, sine, gains, *refs
):
    tok, (normed, lin, rot, val, held) = refs[:count], refs[count:]
    pick(tok, held)
    rows = held[...].astype(f32)
    low = (rows * inverse_root(rows) * gain[...]).astype(bf16)
    normed[...] = low
    head = cosine.shape[1]
    full = dot(low, weight[...])
    cos_, sin_ = cosine[...], sine[...]
    for index in range(q_heads + k_heads):
        part = full[:, index * head : (index + 1) * head]
        lin[:, index * head : (index + 1) * head] = part
        which = 0 if index < q_heads else 1
        unit = part * inverse_root(part) * gains[which : which + 1, :]
        rot[:, index * head : (index + 1) * head] = (unit * cos_ + half_turn(unit) * sin_).astype(
            bf16
        )
    val[...] = full[:, (q_heads + k_heads) * head :].astype(bf16)


def row_block(rows, columns, first=0):
    return pl.BlockSpec((rows, columns), lambda i: (i + first, 0))


def fixed_block(rows, columns):
    return pl.BlockSpec((rows, columns), lambda i: (0, 0))


def project(tok, gain, weight, cosine, sine, gains, q_heads, k_heads):
    count = len(tok)
    block, width = tok[0].shape
    total = block * count
    head = cosine.shape[1]
    qk = (q_heads + k_heads) * head
    kv = k_heads * head
    return pl.pallas_call(
        functools.partial(project_kernel, q_heads, k_heads, count),
        grid=(count,),
        in_specs=[
            fixed_block(1, width),
            fixed_block(*weight.shape),
            row_block(block, head),
            row_block(block, head),
            fixed_block(2, head),
        ]
        + [fixed_block(block, width)] * count,
        out_specs=[row_block(block, n) for n in (width, qk, qk, kv)],
        out_shape=[
            jax.ShapeDtypeStruct((total, width), bf16),
            jax.ShapeDtypeStruct((total, qk), f32),
            jax.ShapeDtypeStruct((total, qk), bf16),
            jax.ShapeDtypeStruct((total, kv), bf16),
        ],
        scratch_shapes=[pltpu.VMEM((block, width), bf16)],
        compiler_params=params(),
        cost_estimate=cost(2 * total * weight.size, 2 * weight.size + total * width * 12),
    )(gain, weight, cosine, sine, gains, *tok)


def allowed_pairs(j, k, start_q, start_k, block, seg_col, seg_row):
    own = seg_col[pl.ds(start_q, block), :]
    other = seg_row[:, pl.ds(start_k, block)]
    allowed = own == other
    if j == k:
        at_q = lax.broadcasted_iota(jnp.int32, (block, block), 0)
        at_k = lax.broadcasted_iota(jnp.int32, (block, block), 1)
        allowed = allowed & (at_q >= at_k)
    return allowed


def attend_kernel(blocks, group, factor, order, query, key, val, seg_col, seg_row, out, low, logs):
    total, head = key.shape
    block = total // blocks
    flip = order[0]
    start = [pl.multiple_of((jnp.int32(i) ^ flip) * block, block) for i in range(blocks)]
    ones = jnp.ones((block, head), bf16)
    for j in range(blocks):
        stacked = jnp.concatenate(
            [query[pl.ds(start[j], block), h * head : (h + 1) * head] for h in range(group)], axis=0
        )
        acc = jnp.zeros((group * block, 2 * head), f32)
        for k in range(j + 1):
            raw = dot_nt(stacked, key[pl.ds(start[k], block), :])
            allowed = allowed_pairs(j, k, start[j], start[k], block, seg_col, seg_row)
            allowed = jnp.concatenate([allowed] * group, axis=0)
            probs = jnp.where(allowed, jnp.exp2(raw * factor), 0.0).astype(bf16)
            both = jnp.concatenate([val[pl.ds(start[k], block), :], ones], axis=1)
            acc = acc + dot(probs, both)
        sums = acc[:, head:]
        result = acc[:, :head] / sums
        log_sums = jnp.log2(sums)
        for h in range(group):
            out[pl.ds(start[j], block), h * head : (h + 1) * head] = result[
                h * block : (h + 1) * block
            ]
            low[pl.ds(start[j], block), h * head : (h + 1) * head] = result[
                h * block : (h + 1) * block
            ].astype(bf16)
            logs[pl.ds(start[j], block), h * head : (h + 1) * head] = log_sums[
                h * block : (h + 1) * block
            ]


def attend(order, rot, val, seg_col, seg_row, q_heads, k_heads, head, blocks):
    total = rot.shape[0]
    group = q_heads // k_heads
    factor = head**-0.5 * math.log2(math.e)
    wide = pl.BlockSpec((total, group * head), lambda g, o: (0, g))
    return pl.pallas_call(
        functools.partial(attend_kernel, blocks, group, factor),
        grid_spec=pltpu.PrefetchScalarGridSpec(
            num_scalar_prefetch=1,
            grid=(k_heads,),
            in_specs=[
                wide,
                pl.BlockSpec((total, head), lambda g, o: (0, q_heads + g)),
                pl.BlockSpec((total, head), lambda g, o: (0, g)),
                pl.BlockSpec((total, 1), lambda g, o: (0, 0)),
                pl.BlockSpec((1, total), lambda g, o: (0, 0)),
            ],
            out_specs=[wide, wide, wide],
        ),
        out_shape=[jax.ShapeDtypeStruct((total, q_heads * head), kind) for kind in (f32, bf16, f32)],
        compiler_params=params(),
        cost_estimate=cost(4 * total * total * q_heads * head, total * q_heads * head * 12),
    )(order, rot, rot, val, seg_col, seg_row)


def attend_back_kernel(
    blocks, group, factor, scale, order, query, key, val, out_grad, out, logs, seg_col, seg_row,
    query_grad, key_grad, val_grad,
):
    total, head = key.shape
    block = total // blocks
    flip = order[0]
    start = [pl.multiple_of((jnp.int32(i) ^ flip) * block, block) for i in range(blocks)]

    def heads_of(ref, at):
        return jnp.concatenate(
            [ref[pl.ds(at, block), h * head : (h + 1) * head] for h in range(group)], axis=0
        )

    deltas = []
    for j in range(blocks):
        product = heads_of(out_grad, start[j]).astype(f32) * heads_of(out, start[j])
        deltas.append(jnp.sum(product, axis=1, keepdims=True))
    sums = [None] * blocks
    for k in range(blocks):
        key_block = key[pl.ds(start[k], block), :]
        val_block = val[pl.ds(start[k], block), :]
        key_sum = jnp.zeros((block, head), f32)
        val_sum = jnp.zeros((block, head), f32)
        for j in range(k, blocks):
            stacked = heads_of(query, start[j])
            grads = heads_of(out_grad, start[j])
            logged = heads_of(logs, start[j])
            logged = jnp.concatenate([logged] * (block // head), axis=1)
            raw = dot_nt(stacked, key_block)
            allowed = allowed_pairs(j, k, start[j], start[k], block, seg_col, seg_row)
            allowed = jnp.concatenate([allowed] * group, axis=0)
            probs = jnp.where(allowed, jnp.exp2(raw * factor - logged), 0.0)
            prob_grad = dot_nt(grads, val_block)
            score_grad = (probs * (prob_grad - deltas[j]) * scale).astype(bf16)
            val_sum = val_sum + dot_tn(probs.astype(bf16), grads)
            key_sum = key_sum + dot_tn(score_grad, stacked)
            piece = dot(score_grad, key_block)
            sums[j] = piece if k == 0 else sums[j] + piece
        key_grad[pl.ds(start[k], block), :] = key_sum
        val_grad[pl.ds(start[k], block), :] = val_sum
        for h in range(group):
            query_grad[pl.ds(start[k], block), h * head : (h + 1) * head] = sums[k][
                h * block : (h + 1) * block
            ]


def attend_back(order, rot, val, out_grad, out, logs, seg_col, seg_row, q_heads, k_heads, head, blocks):
    total = rot.shape[0]
    group = q_heads // k_heads
    scale = head**-0.5
    wide = pl.BlockSpec((total, group * head), lambda g, o: (0, g))
    thin = pl.BlockSpec((total, head), lambda g, o: (0, g))
    return pl.pallas_call(
        functools.partial(attend_back_kernel, blocks, group, scale * math.log2(math.e), scale),
        grid_spec=pltpu.PrefetchScalarGridSpec(
            num_scalar_prefetch=1,
            grid=(k_heads,),
            in_specs=[
                wide,
                pl.BlockSpec((total, head), lambda g, o: (0, q_heads + g)),
                thin,
                wide,
                wide,
                wide,
                pl.BlockSpec((total, 1), lambda g, o: (0, 0)),
                pl.BlockSpec((1, total), lambda g, o: (0, 0)),
            ],
            out_specs=[wide, thin, thin],
        ),
        out_shape=[
            jax.ShapeDtypeStruct((total, q_heads * head), f32),
            jax.ShapeDtypeStruct((total, k_heads * head), f32),
            jax.ShapeDtypeStruct((total, k_heads * head), f32),
        ],
        compiler_params=params(),
        cost_estimate=cost(10 * total * total * q_heads * head, total * q_heads * head * 20),
    )(order, rot, rot, val, out_grad, out, logs, seg_col, seg_row)


def feed_kernel(count, kept, weight, down, *refs):
    norm, cot = refs[:count], refs[count : 2 * count]
    hidden, gate_out, up_out, norm_all, cot_all, norm_grad, out, low_held, cot_held = refs[
        2 * count + kept :
    ]
    pick(norm, low_held)
    pick(cot, cot_held)
    units = down.shape[0]
    low = low_held[...]
    norm_all[...] = low
    cot_all[...] = cot_held[...]
    gate = dot(low, weight[:, :units])
    upper = dot(low, weight[:, units:])
    sigma = 1.0 / (1.0 + jnp.exp(-gate))
    silu = gate * sigma
    hid = (silu * upper).astype(bf16)
    hidden[...] = hid
    back = dot_nt(cot_held[...], down[...])
    gate_grad = (back * upper * sigma * (1.0 + gate * (1.0 - sigma))).astype(bf16)
    up_grad = (back * silu).astype(bf16)
    gate_out[...] = gate_grad
    up_out[...] = up_grad
    norm_grad[...] = (
        dot_nt(gate_grad, weight[:, :units]) + dot_nt(up_grad, weight[:, units:])
    ).astype(bf16)
    out[...] = dot(hid, down[...]).astype(bf16)


def feed(norm, cot, weight, down, first, blocks, before):
    count = len(norm)
    block, width = norm[0].shape
    total = block * blocks
    units = down.shape[0]
    kept = [units, units, units, width, width]
    return pl.pallas_call(
        functools.partial(feed_kernel, count, len(before)),
        grid=(count,),
        in_specs=[fixed_block(*weight.shape), fixed_block(*down.shape)]
        + [fixed_block(block, width)] * (2 * count)
        + [pl.BlockSpec(memory_space=pl.ANY)] * len(before),
        out_specs=[row_block(block, n, first) for n in kept] + [row_block(block, width)] * 2,
        out_shape=[jax.ShapeDtypeStruct((total, n), bf16) for n in kept]
        + [jax.ShapeDtypeStruct((block * count, width), bf16)] * 2,
        scratch_shapes=[pltpu.VMEM((block, width), bf16)] * 2,
        input_output_aliases={2 + 2 * count + i: i for i in range(len(before))},
        compiler_params=params(),
        cost_estimate=cost(
            12 * block * count * down.size, 6 * down.size + block * count * width * 16,
            block * count * units,
        ),
    )(weight, down, *norm, *cot, *before)


def branch_kernel(count, weight, *refs):
    branch, (out_grad, branch_all, held) = refs[:count], refs[count:]
    pick(branch, held)
    low = held[...]
    branch_all[...] = low
    out_grad[...] = dot_nt(low, weight[...]).astype(bf16)


def branch_back(branch, weight):
    count = len(branch)
    block, width = branch[0].shape
    total = block * count
    return pl.pallas_call(
        functools.partial(branch_kernel, count),
        grid=(count,),
        in_specs=[fixed_block(*weight.shape)] + [fixed_block(block, width)] * count,
        out_specs=[row_block(block, weight.shape[0]), row_block(block, width)],
        out_shape=[
            jax.ShapeDtypeStruct((total, weight.shape[0]), bf16),
            jax.ShapeDtypeStruct((total, width), bf16),
        ],
        scratch_shapes=[pltpu.VMEM((block, width), bf16)],
        compiler_params=params(),
        cost_estimate=cost(2 * total * weight.size, 2 * weight.size + total * width * 6),
    )(weight, *branch)


def unproject_kernel(
    q_heads, k_heads, count, query_grad, key_grad, val_grad, lin, cosine, sine, gains, weight, *refs
):
    tok, (query_out, pair_out, norm_grad, gain_sum, head_sum, held) = refs[:count], refs[count:]
    pick(tok, held)
    head = cosine.shape[1]
    cos_, sin_ = cosine[...], sine[...]
    sums = [jnp.zeros((1, head), f32), jnp.zeros((1, head), f32)]
    for index in range(q_heads + k_heads):
        which = 0 if index < q_heads else 1
        ref, result, spot = (
            (query_grad, query_out, index) if which == 0 else (key_grad, pair_out, index - q_heads)
        )
        turned = ref[:, spot * head : (spot + 1) * head]
        grad = turned * cos_ - half_turn(turned) * sin_
        rows = lin[:, index * head : (index + 1) * head]
        scale = inverse_root(rows)
        sums[which] = sums[which] + jnp.sum(grad * rows * scale, axis=0, keepdims=True)
        result[:, spot * head : (spot + 1) * head] = norm_back(
            grad * gains[which : which + 1, :], rows, scale
        ).astype(bf16)
    pair_out[:, k_heads * head :] = val_grad[...].astype(bf16)
    normed_grad = dot_nt(query_out[...], weight[:, : q_heads * head]) + dot_nt(
        pair_out[...], weight[:, q_heads * head :]
    )
    norm_grad[...] = normed_grad.astype(bf16)
    rows = held[...].astype(f32)
    gain_part = jnp.sum(normed_grad * rows * inverse_root(rows), axis=0, keepdims=True)

    @pl.when(pl.program_id(0) == 0)
    def _():
        gain_sum[...] = jnp.zeros_like(gain_sum)
        head_sum[...] = jnp.zeros_like(head_sum)

    gain_sum[...] += gain_part
    head_sum[...] += jnp.concatenate(sums, axis=0)


def unproject(query_grad, key_grad, val_grad, lin, cosine, sine, gains, weight, tok, q_heads, k_heads):
    count = len(tok)
    block, width = tok[0].shape
    total = block * count
    head = cosine.shape[1]
    q_width, kv_width = q_heads * head, 2 * k_heads * head
    return pl.pallas_call(
        functools.partial(unproject_kernel, q_heads, k_heads, count),
        grid=(count,),
        in_specs=[
            row_block(block, q_width),
            row_block(block, k_heads * head),
            row_block(block, k_heads * head),
            row_block(block, (q_heads + k_heads) * head),
            row_block(block, head),
            row_block(block, head),
            fixed_block(2, head),
            fixed_block(*weight.shape),
        ]
        + [fixed_block(block, width)] * count,
        out_specs=[
            row_block(block, q_width), row_block(block, kv_width), row_block(block, width),
            fixed_block(1, width), fixed_block(2, head),
        ],
        out_shape=[
            jax.ShapeDtypeStruct((total, q_width), bf16),
            jax.ShapeDtypeStruct((total, kv_width), bf16),
            jax.ShapeDtypeStruct((total, width), bf16),
            jax.ShapeDtypeStruct((1, width), f32),
            jax.ShapeDtypeStruct((2, head), f32),
        ],
        scratch_shapes=[pltpu.VMEM((block, width), bf16)],
        compiler_params=params(),
        cost_estimate=cost(2 * total * weight.size, 2 * weight.size + total * width * 16),
    )(query_grad, key_grad, val_grad, lin, cosine, sine, gains, weight, *tok)


def place_kernel(count, outs, moves, scalars, *refs):
    inputs, results = refs[:count], refs[count:]
    values = [scalars[i] for i in range(scalars.shape[0])]
    for source, index, rows, columns, target, spot in moves:
        piece = inputs[source][index + (slice(rows[0], rows[1]), slice(columns[0], columns[1]))]
        row, column = spot(*values)
        results[target][
            pl.ds(pl.multiple_of(row, 16), rows[1] - rows[0]),
            pl.ds(pl.multiple_of(column, 128), columns[1] - columns[0]),
        ] = piece.astype(results[target].dtype)


def place(scalars, inputs, out_shapes, moves):
    moved = sum(item.size * 2 for item in inputs) + sum(
        math.prod(shape) * (4 if kind == f32 else 2) for shape, kind in out_shapes
    )
    whole = pl.BlockSpec(memory_space=pltpu.VMEM)
    return pl.pallas_call(
        functools.partial(place_kernel, len(inputs), len(out_shapes), moves),
        in_specs=[pl.BlockSpec(memory_space=pltpu.SMEM)] + [whole] * len(inputs),
        out_specs=[whole] * len(out_shapes),
        out_shape=[jax.ShapeDtypeStruct(shape, kind) for shape, kind in out_shapes],
        compiler_params=params(),
        cost_estimate=cost(0, moved),
    )(scalars, *inputs)


def cut_kernel(sizes, scalars, *refs):
    inputs, (own, near, piece) = refs[: len(sizes)], refs[len(sizes) :]
    mine, y = scalars[0], scalars[1]
    half = piece.shape[1]
    begin = 0
    for ref, size in zip(inputs, sizes):
        lanes = lambda i: pl.ds(pl.multiple_of((mine ^ i) * size, 128), size)
        rows = pl.ds(pl.multiple_of(y * half, 16), half)
        own[:, begin : begin + size] = ref[:, lanes(0)]
        near[:, begin : begin + size] = ref[:, lanes(1)]
        piece[0, :, begin : begin + size] = ref[rows, lanes(2)]
        piece[1, :, begin : begin + size] = ref[rows, lanes(3)]
        begin += size


def cut(scalars, inputs, sizes):
    rows = inputs[0].shape[0]
    wide = sum(sizes)
    whole = pl.BlockSpec(memory_space=pltpu.VMEM)
    shapes = [(rows, wide), (rows, wide), (2, rows // 2, wide)]
    return pl.pallas_call(
        functools.partial(cut_kernel, sizes),
        in_specs=[pl.BlockSpec(memory_space=pltpu.SMEM)] + [whole] * len(inputs),
        out_specs=[whole] * 3,
        out_shape=[jax.ShapeDtypeStruct(shape, bf16) for shape in shapes],
        compiler_params=params(),
        cost_estimate=cost(0, 4 * sum(item.size for item in inputs)),
    )(scalars, *inputs)


def ring_kernel(layout, plan, count, sets, chunks, *refs):
    local = [refs[i * count : (i + 1) * count] for i in range(sets)]
    arrived = refs[sets * count : len(refs) - len(plan)]
    results = refs[len(refs) - len(plan) :]
    for result, (which, halves, adds) in zip(results, plan):
        for source, block, lane, size, to_block, to_lane in layout:
            for at, half in enumerate(halves):
                value = local[which][source][block, 0, half, :, lane : lane + size].astype(f32)
                for index, held in adds:
                    if half in held:
                        value = value + arrived[index][
                            to_block, held.index(half), :, to_lane : to_lane + size
                        ].astype(f32)
                result[to_block, at, :, to_lane : to_lane + size] = value.astype(bf16)


def ring_step(shares, layout, blocks, chunks, plan, arrived):
    lines, lanes = shares[0].shape[3], blocks[1]
    specs = []
    for which in range(len(chunks)):
        for share in shares:
            shape = (share.shape[0], 1) + share.shape[2:]
            specs.append(
                pl.BlockSpec(shape, lambda i, c, which=which: (0, c[which], 0, 0, 0))
            )
    whole = lambda shape: pl.BlockSpec(shape, lambda i, c: (0,) * len(shape))
    shapes = [(blocks[0], len(halves), lines, lanes) for _, halves, _ in plan]
    return pl.pallas_call(
        functools.partial(ring_kernel, layout, plan, len(shares), len(chunks)),
        grid_spec=pltpu.PrefetchScalarGridSpec(
            num_scalar_prefetch=1,
            grid=(1,),
            in_specs=specs + [whole(item.shape) for item in arrived],
            out_specs=[whole(shape) for shape in shapes],
        ),
        out_shape=[jax.ShapeDtypeStruct(shape, bf16) for shape in shapes],
        compiler_params=params(),
        cost_estimate=cost(0, 6 * sum(math.prod(shape) for shape in shapes)),
    )(jnp.stack(chunks).astype(jnp.int32), *shares * len(chunks), *arrived)


def split_kernel(pieces, scalars, chunk, own, near, far):
    mine = scalars[0]
    for i, (result, spot) in enumerate([(own, 0), (near, 0), (far, 0), (near, 1)]):
        begin = 0
        for block, lane, size in pieces(mine ^ i):
            result[spot, :, :, begin : begin + size] = chunk[
                block, :, :, pl.ds(pl.multiple_of(lane, 128), size)
            ]
            begin += size


def split(scalars, chunk, pieces, wide):
    whole = pl.BlockSpec(memory_space=pltpu.VMEM)
    lines = chunk.shape[1:3]
    shapes = [(1, *lines, wide), (2, *lines, wide), (1, *lines, wide)]
    return pl.pallas_call(
        functools.partial(split_kernel, pieces),
        in_specs=[pl.BlockSpec(memory_space=pltpu.SMEM), whole],
        out_specs=[whole] * 3,
        out_shape=[jax.ShapeDtypeStruct(shape, bf16) for shape in shapes],
        compiler_params=params(),
        cost_estimate=cost(0, 4 * chunk.size),
    )(scalars, chunk)


def pack_kernel(layout, *refs):
    inputs, result = refs[:-1], refs[-1]
    for source, block, lane, size, to_block, to_lane in layout:
        result[to_block, :, :, to_lane : to_lane + size] = inputs[source][
            block, :, :, lane : lane + size
        ]


def pack(inputs, layout, shape):
    whole = pl.BlockSpec(memory_space=pltpu.VMEM)
    return pl.pallas_call(
        functools.partial(pack_kernel, layout),
        in_specs=[whole] * len(inputs),
        out_specs=whole,
        out_shape=jax.ShapeDtypeStruct(shape, bf16),
        compiler_params=params(),
        cost_estimate=cost(0, 4 * math.prod(shape)),
    )(*inputs)


class Moves:
    def __init__(self):
        self.shards = lax.axis_size("shard")
        self.reps = lax.axis_size("rep")
        self.mine = lax.axis_index("shard")
        self.direct = self.shards == 4 and self.reps == 8
        self.flip = self.mine if self.direct else jnp.int32(0)
        rep = lax.axis_index("rep")
        self.bits = {1: rep % 2, 2: (rep // 2) % 2, 4: rep // 4}
        self.pos = jnp.where(rep % 2 == 0, rep // 2, 7 - rep // 2)
        self.ring = [0, 2, 4, 6, 7, 5, 3, 1]
        self.scalars = jnp.stack([self.mine, self.bits[1], self.pos]).astype(jnp.int32)

    def up(self, item):
        ring = self.ring
        return lax.ppermute(item, "rep", [(ring[i], ring[(i + 1) % 8]) for i in range(8)])

    def down(self, item):
        ring = self.ring
        return lax.ppermute(item, "rep", [(ring[(i + 1) % 8], ring[i]) for i in range(8)])

    def swap(self, item, mask):
        return lax.ppermute(item, "shard", [(i, i ^ mask) for i in range(4)])

    def cross_rep(self, item, mask):
        return lax.ppermute(item, "rep", [(i, i ^ mask) for i in range(8)])

    def gather(self, item):
        if not self.direct:
            rows = item.shape[0]
            whole = lax.all_gather(item, "shard", axis=0, tiled=True)
            return [whole[i * rows : (i + 1) * rows] for i in range(self.shards)]
        far = self.swap(item, 2)
        near = self.swap(item, 1)
        cross = self.swap(far, 1)
        return [item, near, far, cross]

    def scatter(self, near_part, far_part):
        if not self.direct:
            item = jnp.concatenate([near_part, far_part], axis=0).astype(f32)
            return lax.psum_scatter(item, "shard", scatter_dimension=0, tiled=True)
        rows = near_part.shape[0] // 2
        far = self.swap(far_part[:rows] + self.swap(far_part[rows:], 1), 2)
        near = self.swap(near_part[rows:], 1)
        return near_part[:rows].astype(f32) + near.astype(f32) + far.astype(f32)

    def ring_scatter(self, shares, layout, blocks):
        step = functools.partial(ring_step, shares, layout, blocks)
        chunk = lambda offset: (self.pos + offset) % 8
        both = (0, 1)
        u, d = step([chunk(4)], [(0, (0,), []), (0, (1,), [])], [])
        u, d = self.up(u), self.down(d)
        plan = [(0, both, [(0, (0,))]), (1, both, [(1, (1,))])]
        u, d = step([chunk(3), chunk(5)], plan, [u, d])
        u, d = self.up(u), self.down(d)
        plan = [(0, both, [(0, both)]), (1, both, [(1, both)])]
        u, d = step([chunk(2), chunk(6)], plan, [u, d])
        u, d = self.up(u), self.down(d)
        u, d = step([chunk(1), chunk(7)], plan, [u, d])
        u, d = self.up(u), self.down(d)
        return step([chunk(0)], [(0, both, [(0, both), (1, both)])], [u, d])[0]

    def ring_gather(self, item):
        u1, d1 = self.up(item), self.down(item)
        u2, d2 = self.up(u1), self.down(d1)
        u3, d3 = self.up(u2), self.down(d2)
        u4, d4 = self.up(u3[:, :1]), self.down(d3[:, 1:])
        return [
            (item, 0, None), (u1, -1, None), (d1, 1, None), (u2, -2, None), (d2, 2, None),
            (u3, -3, None), (d3, 3, None), (u4, 4, 0), (d4, 4, 1),
        ]

    def exchange(self, chunk, pieces, wide):
        own, near, far = split(self.scalars, chunk, pieces, wide)
        near = self.swap(near, 1)
        far = self.swap(jnp.concatenate([far, near[1:]], axis=0), 2)
        return own, near, far


class Fetch:
    def __init__(self, moves, own, near, piece, spot, shape):
        self.moves, self.own, self.near, self.piece = moves, own, near, piece
        self.spot, self.shape = spot, shape

    def start(self, *before):
        self.here = self.moves.swap(after(self.piece, *before), 2)
        self.there = self.moves.cross_rep(self.here, 1)

    def finish(self):
        moves, here, there, spot = self.moves, self.here, self.there, self.spot
        rows, width = self.own.shape
        half = rows // 2
        near = moves.swap(self.near, 1)
        inputs = [self.own, near, here, moves.swap(here[1], 1), there, moves.swap(there[1], 1)]
        todo = [
            (0, (), (0, rows), (0, width), 0, lambda shard, *_: spot(shard, 0)),
            (1, (), (0, rows), (0, width), 0, lambda shard, *_: spot(shard ^ 1, 0)),
            (2, (0,), (0, half), (0, width), 0, lambda shard, y, *_: spot(shard ^ 2, y * half)),
            (3, (), (0, half), (0, width), 0, lambda shard, y, *_: spot(shard ^ 3, y * half)),
            (4, (0,), (0, half), (0, width), 0, lambda shard, y, *_: spot(shard ^ 2, (1 - y) * half)),
            (5, (), (0, half), (0, width), 0, lambda shard, y, *_: spot(shard ^ 3, (1 - y) * half)),
        ]
        return place(moves.scalars, inputs, [(self.shape, bf16)], todo)[0]


def after(item, *others):
    return lax.optimization_barrier((item, *others))[0]


def per_device(
    tokens, segments, grad_out, attention_gain, query_weight, key_matrix, value_matrix, query_gain,
    key_gain, output_weight, mlp_gain, gate_weight, up_weight, down_weight,
):
    moves = Moves()
    shards, mine, direct = moves.shards, moves.mine, moves.direct
    rows, width = tokens.shape[1:]
    total = rows * shards
    slice_width = attention_gain.shape[0]
    head_slice = query_gain.shape[0]
    head = head_slice * shards
    k_heads = key_matrix.shape[1] // head // shards
    q_heads = query_weight.shape[1] // head // shards
    q_width, k_width = q_heads * head, k_heads * head
    units = down_weight.shape[0]
    own_tokens = tokens[0]
    cot = grad_out[0]

    small = jnp.concatenate(
        [attention_gain, mlp_gain, query_gain, key_gain, segments[0].astype(bf16)]
    )[None]
    small = jnp.concatenate(moves.gather(small), axis=0)
    if direct:
        whole = jnp.where(mine % 2 == 0, small, small[jnp.array([1, 0, 3, 2])])
        whole = jnp.where(mine // 2 == 0, whole, whole[jnp.array([2, 3, 0, 1])])
    else:
        whole = small
    cuts = [slice_width, 2 * slice_width, 2 * slice_width + head_slice, 2 * slice_width + 2 * head_slice]
    input_gain = whole[:, : cuts[0]].reshape(1, width).astype(f32)
    second_gain = whole[:, cuts[0] : cuts[1]].reshape(1, width).astype(f32)
    head_gains = jnp.stack(
        [whole[:, cuts[1] : cuts[2]].reshape(head), whole[:, cuts[2] : cuts[3]].reshape(head)]
    ).astype(f32)
    segs = small[:, cuts[3] :].reshape(total).astype(f32)
    index = jnp.arange(shards, dtype=jnp.int32) ^ moves.flip
    places = (index[:, None] * rows + jnp.arange(rows, dtype=jnp.int32)[None]).reshape(total)
    firsts = jnp.sum((segs < 0.5).astype(jnp.int32))
    seconds = jnp.sum((segs < 1.5).astype(jnp.int32))
    opening = jnp.where(segs < 0.5, 0, jnp.where(segs < 1.5, firsts, seconds))
    freqs = theta_base ** (-(jnp.arange(head // 2, dtype=f32) * 2.0) / head)
    angles = (places - opening).astype(f32)[:, None] * freqs
    cosine, sine = jnp.cos(angles), jnp.sin(angles)
    cosine = jnp.concatenate([cosine, cosine], axis=1)
    sine = jnp.concatenate([-sine, sine], axis=1)
    seg_col, seg_row = segs[:, None], segs[None, :]
    order = moves.flip.astype(jnp.int32)[None]

    all_tokens = all_cot = None
    if direct:
        by_rows = lambda source, line: (source * slice_width + line, 0)
        qkv = Fetch(
            moves,
            *cut(moves.scalars, [query_weight, key_matrix, value_matrix], [q_width, k_width, k_width]),
            by_rows,
            (width, q_width + 2 * k_width),
        )
        outer = lambda i, begin, n: lax.dynamic_slice(
            output_weight, ((mine ^ i) * q_width + begin, 0), (n, slice_width)
        )
        half = q_width // 2
        output = Fetch(
            moves,
            outer(0, 0, q_width),
            outer(1, 0, q_width),
            jnp.stack([outer(2, moves.bits[1] * half, half), outer(3, moves.bits[1] * half, half)]),
            lambda source, line: (line, source * slice_width),
            (q_width, width),
        )
        both = Fetch(
            moves,
            *cut(moves.scalars, [gate_weight, up_weight], [units, units]),
            by_rows,
            (width, 2 * units),
        )
        qkv.start()
        all_tokens = moves.gather(after(own_tokens, qkv.here))
        output.start(all_tokens[2], qkv.there)
        qkv_weight = qkv.finish()
        both.start(output.here)
        out_weight = output.finish()
        all_cot = moves.gather(after(cot, both.here))
    else:
        spread = lambda item: lax.all_to_all(item, "shard", split_axis=1, concat_axis=0, tiled=True)
        qkv_weight = jnp.concatenate(
            [spread(query_weight), spread(key_matrix), spread(value_matrix)], axis=1
        )
        out_weight = lax.all_to_all(output_weight, "shard", split_axis=0, concat_axis=1, tiled=True)
        feed_weight = jnp.concatenate([spread(gate_weight), spread(up_weight)], axis=1)

    if not direct:
        all_tokens, all_cot = moves.gather(own_tokens), moves.gather(cot)
    normed_one, lin, rot, val = project(
        all_tokens, input_gain, qkv_weight, cosine, sine, head_gains, q_heads, k_heads
    )
    attended, attended_low, logs = attend(order, rot, val, seg_col, seg_row, q_heads, k_heads, head, shards)
    inputs = own_tokens.astype(f32)
    split = total // 2
    if direct:
        feed_weight = both.finish()
        attended_low = after(attended_low, both.here)
    far_part = dot(attended_low[split:], out_weight).astype(bf16)
    near_part = dot(attended_low[:split], out_weight).astype(bf16)
    residual_one = inputs + moves.scatter(near_part, far_part)
    residual_scale = inverse_root(residual_one)
    normed_two = moves.gather((residual_one * residual_scale * second_gain).astype(bf16))

    *kept, norm_grad, out_part = feed(
        normed_two, all_cot, feed_weight, down_weight, 0, shards, []
    )
    hidden, gate_grad, up_grad, normed_two, all_cot = kept
    share_down = dot_tn(hidden, all_cot).astype(bf16)
    share_gate = dot_tn(normed_two, gate_grad).astype(bf16)
    share_up = dot_tn(normed_two, up_grad).astype(bf16)
    normed_grad_two = moves.scatter(norm_grad[:split], norm_grad[split:])
    mlp_gain_part = jnp.sum(normed_grad_two * residual_one * residual_scale, axis=0)
    residual_grad = cot.astype(f32) + norm_back(
        normed_grad_two * second_gain, residual_one, residual_scale
    )
    branch_grad = moves.gather(residual_grad.astype(bf16))

    out_part = after(out_part, *branch_grad)
    layer_out = (residual_one + moves.scatter(out_part[:split], out_part[split:])).astype(bf16)

    out_grad, branch_grad = branch_back(branch_grad, out_weight)
    share_out = dot_tn(attended_low, branch_grad).astype(bf16)
    query_grad, key_grad, val_grad = attend_back(
        order, rot, val, out_grad, attended, logs, seg_col, seg_row, q_heads, k_heads, head, shards
    )
    query_lin_grad, pair_lin_grad, norm_one_part, gain_part, head_part = unproject(
        query_grad, key_grad, val_grad, lin, cosine, sine, head_gains, qkv_weight, all_tokens,
        q_heads, k_heads,
    )
    share_query = dot_tn(normed_one, query_lin_grad).astype(bf16)
    share_pair = dot_tn(normed_one, pair_lin_grad).astype(bf16)
    normed_grad_one = moves.scatter(norm_one_part[:split], norm_one_part[split:])
    grad_tokens = residual_grad + norm_back(normed_grad_one * input_gain, inputs, inverse_root(inputs))

    gains = jnp.concatenate([gain_part[0], mlp_gain_part, head_part.reshape(2 * head)])[None]
    if direct:
        gains = gains + moves.swap(gains, 1)
        gains = gains + moves.swap(gains, 2)
        for mask in (1, 2, 4):
            gains = gains + moves.cross_rep(gains, mask)
    else:
        gains = lax.psum(gains, ("shard", "rep"))
    gains = gains[0]

    def own_part(begin, size):
        return lax.dynamic_slice_in_dim(gains, begin + mine * size, size, 0)

    grad_attention_gain = own_part(0, slice_width)
    grad_mlp_gain = own_part(width, slice_width)
    grad_query_gain = own_part(2 * width, head_slice)
    grad_key_gain = own_part(2 * width + head, head_slice)

    if direct:
        lines = slice_width // 16
        rest = 2 * units - width
        as_chunks = lambda share: share.reshape(-1, 8, 2, lines, share.shape[1])
        spot_of = lambda values, offset: lax.rem(values[2] + (offset + 8), 8) * (2 * lines)

        downs = units // slice_width
        blocks = (6 + downs, width)
        layout = []
        for i in range(4):
            layout += [
                (0, i, 0, units, i, 0),
                (1, i, 0, width - units, i, units),
                (1, i, width - units, rest, 4 + i // 2, (i % 2) * rest),
            ]
        layout += [(2, b, 0, width, 6 + b, 0) for b in range(downs)]
        chunk = moves.ring_scatter(
            [as_chunks(share_gate), as_chunks(share_up), as_chunks(share_down)], layout, blocks
        )
        own, near, far = moves.exchange(
            chunk, lambda at: [(at, 0, width), (4 + at // 2, (at % 2) * rest, rest)], 2 * units
        )
        layout = []
        for i, (source, index) in enumerate([(0, 0), (1, 0), (2, 0), (2, 1)]):
            layout += [
                (source, index, 0, width, i, 0),
                (source, index, width, rest, 4 + i // 2, (i % 2) * rest),
            ]
        layout += [(3, 6 + b, 0, width, 6 + b, 0) for b in range(downs)]
        parts = moves.ring_gather(
            pack([own, near, far, chunk], layout, (blocks[0], 2, lines, width))
        )
        todo = []
        for source, (part, offset, half) in enumerate(parts):
            for h in range(part.shape[1]):
                line = ((half or 0) + h) * lines
                for i in range(4):

                    def at(*values, i=i, line=line, offset=offset, begin=0):
                        return spot_of(values, offset) + line, (values[0] ^ i) * units + begin

                    first = width - units
                    todo += [
                        (source, (i, h), (0, lines), (0, units), 0, at),
                        (source, (i, h), (0, lines), (units, width), 1, at),
                        (
                            source, (4 + i // 2, h), (0, lines),
                            ((i % 2) * rest, (i % 2) * rest + rest), 1,
                            functools.partial(at, begin=first),
                        ),
                    ]
                for b in range(downs):

                    def at(*values, b=b, line=line, offset=offset):
                        return b * slice_width + spot_of(values, offset) + line, 0

                    todo.append((source, (6 + b, h), (0, lines), (0, width), 2, at))
        shapes = [((slice_width, units * 4), f32)] * 2 + [((units, width), f32)]
        grad_gate, grad_up, grad_down = place(
            moves.scalars, [part for part, _, _ in parts], shapes, todo
        )

        outs = q_width // slice_width
        pair = 2 * k_width
        wide = q_width + pair
        layout = []
        for i in range(4):
            layout += [(0, i, 0, q_width, i, 0), (1, i, 0, pair, i, q_width)]
        layout += [(2, b, 0, width, 4 + b, 0) for b in range(outs)]
        chunk = moves.ring_scatter(
            [as_chunks(share_query), as_chunks(share_pair), as_chunks(share_out)],
            layout,
            (4 + outs, width),
        )
        own, near, far = moves.exchange(
            chunk,
            lambda at: [(at, 0, wide)] + [(4 + b, at * slice_width, slice_width) for b in range(outs)],
            wide + outs * slice_width,
        )
        wide_all = wide + outs * slice_width
        layout = [
            (source, index, 0, wide_all, i, 0)
            for i, (source, index) in enumerate([(0, 0), (1, 0), (2, 0), (2, 1)])
        ]
        parts = moves.ring_gather(pack([own, near, far], layout, (4, 2, lines, wide_all)))
        todo = []
        for source, (part, offset, half) in enumerate(parts):
            for h in range(part.shape[1]):
                line = ((half or 0) + h) * lines
                for i in range(4):
                    begin = 0
                    for target, size in enumerate([q_width, k_width, k_width]):

                        def at(*values, i=i, line=line, offset=offset, size=size):
                            return spot_of(values, offset) + line, (values[0] ^ i) * size

                        todo.append((source, (i, h), (0, lines), (begin, begin + size), target, at))
                        begin += size
                    for b in range(outs):

                        def at(*values, i=i, b=b, line=line, offset=offset):
                            first = (values[0] ^ i) * q_width + b * slice_width
                            return first + spot_of(values, offset) + line, 0

                        todo.append(
                            (source, (i, h), (0, lines), (begin, begin + slice_width), 3, at)
                        )
                        begin += slice_width
        shapes = [((slice_width, size * 4), f32) for size in (q_width, k_width, k_width)]
        shapes.append(((q_width * 4, slice_width), f32))
        grad_query, grad_key, grad_value, grad_output = place(
            moves.scalars, [part for part, _, _ in parts], shapes, todo
        )
    else:

        def finish(share):
            part = lax.all_to_all(share, "shard", split_axis=0, concat_axis=1, tiled=True)
            return lax.psum(part, "rep").astype(f32)

        grad_down = lax.psum(share_down, "rep").astype(f32)
        grad_gate = finish(share_gate)
        grad_up = finish(share_up)
        grad_output = lax.psum(
            lax.all_to_all(share_out, "shard", split_axis=1, concat_axis=0, tiled=True), "rep"
        ).astype(f32)
        grad_query = finish(share_query)
        grad_key = finish(share_pair[:, :k_width])
        grad_value = finish(share_pair[:, k_width:])

    return (
        layer_out[None], grad_tokens[None], grad_attention_gain, grad_query, grad_key, grad_value,
        grad_query_gain, grad_key_gain, grad_output, grad_mlp_gain, grad_gate, grad_up, grad_down,
    )


def solution(mesh):
    rows_over = P("shard", None)
    return jax.shard_map(
        per_device,
        mesh=mesh,
        in_specs=(
            P("rep", "shard", None), P("rep", "shard"), P("rep", "shard", None), P("shard"), rows_over,
            rows_over, rows_over, P("shard"), P("shard"), P(None, "shard"), P("shard"), rows_over,
            rows_over, rows_over,
        ),
        out_specs=(
            P("rep", "shard", None), P("rep", "shard", None), P("shard"), rows_over, rows_over,
            rows_over, P("shard"), P("shard"), P(None, "shard"), P("shard"), rows_over, rows_over,
            rows_over,
        ),
        check_vma=False,
    )
```

```python
import functools
import math

import jax
import jax.numpy as jnp
from jax import lax
from jax.experimental import pallas as pl
from jax.experimental.pallas import tpu as pltpu
from jax.sharding import PartitionSpec as P

eps_norm = 1e-06
theta_base = 1000000.0
f32 = jnp.float32
bf16 = jnp.bfloat16
vmem_bytes = 32 * 1024 * 1024
vmem_wide = 52 * 1024 * 1024


def dot(left, right):
    return lax.dot_general(left, right, (((1,), (0,)), ((), ())), preferred_element_type=f32)


def dot_nt(left, right):
    return lax.dot_general(left, right, (((1,), (1,)), ((), ())), preferred_element_type=f32)


def dot_tn(left, right):
    return lax.dot_general(left, right, (((0,), (0,)), ((), ())), preferred_element_type=f32)


def inverse_root(rows):
    return lax.rsqrt(jnp.mean(rows * rows, axis=-1, keepdims=True) + eps_norm)


def norm_back(grad, rows, scale):
    return scale * grad - rows * (scale * scale * scale) * jnp.mean(
        grad * rows, axis=-1, keepdims=True
    )


def params(limit=vmem_bytes):
    return pltpu.CompilerParams(vmem_limit_bytes=limit)


def cost(flops, moved, trans=0):
    return pl.CostEstimate(flops=int(flops), bytes_accessed=int(moved), transcendentals=int(trans))


def half_turn(rows):
    return pltpu.roll(rows, rows.shape[-1] // 2, axis=1)


def pick(refs, held):
    for k, ref in enumerate(refs):

        @pl.when(pl.program_id(0) == k)
        def _(ref=ref):
            held[...] = ref[...]


def project_kernel(
    q_heads, k_heads, count, gain, weight, cosine, sine, gains, *refs
):
    tok, (normed, lin, rot, val, held) = refs[:count], refs[count:]
    pick(tok, held)
    rows = held[...].astype(f32)
    low = (rows * inverse_root(rows) * gain[...]).astype(bf16)
    normed[...] = low
    head = cosine.shape[1]
    full = dot(low, weight[...])
    cos_, sin_ = cosine[...], sine[...]
    for index in range(q_heads + k_heads):
        part = full[:, index * head : (index + 1) * head]
        lin[:, index * head : (index + 1) * head] = part
        which = 0 if index < q_heads else 1
        unit = part * inverse_root(part) * gains[which : which + 1, :]
        rot[:, index * head : (index + 1) * head] = (unit * cos_ + half_turn(unit) * sin_).astype(
            bf16
        )
    val[...] = full[:, (q_heads + k_heads) * head :].astype(bf16)


def row_block(rows, columns, first=0):
    return pl.BlockSpec((rows, columns), lambda i: (i + first, 0))


def fixed_block(rows, columns):
    return pl.BlockSpec((rows, columns), lambda i: (0, 0))


def project(tok, gain, weight, cosine, sine, gains, q_heads, k_heads):
    count = len(tok)
    block, width = tok[0].shape
    total = block * count
    head = cosine.shape[1]
    qk = (q_heads + k_heads) * head
    kv = k_heads * head
    return pl.pallas_call(
        functools.partial(project_kernel, q_heads, k_heads, count),
        grid=(count,),
        in_specs=[
            fixed_block(1, width),
            fixed_block(*weight.shape),
            row_block(block, head),
            row_block(block, head),
            fixed_block(2, head),
        ]
        + [fixed_block(block, width)] * count,
        out_specs=[row_block(block, n) for n in (width, qk, qk, kv)],
        out_shape=[
            jax.ShapeDtypeStruct((total, width), bf16),
            jax.ShapeDtypeStruct((total, qk), f32),
            jax.ShapeDtypeStruct((total, qk), bf16),
            jax.ShapeDtypeStruct((total, kv), bf16),
        ],
        scratch_shapes=[pltpu.VMEM((block, width), bf16)],
        compiler_params=params(vmem_wide),
        cost_estimate=cost(2 * total * weight.size, 2 * weight.size + total * width * 12),
    )(gain, weight, cosine, sine, gains, *tok)


def allowed_pairs(j, k, start_q, start_k, block, seg_col, seg_row):
    own = seg_col[pl.ds(start_q, block), :]
    other = seg_row[:, pl.ds(start_k, block)]
    allowed = own == other
    if j == k:
        at_q = lax.broadcasted_iota(jnp.int32, (block, block), 0)
        at_k = lax.broadcasted_iota(jnp.int32, (block, block), 1)
        allowed = allowed & (at_q >= at_k)
    return allowed


def attend_kernel(blocks, group, factor, order, query, key, val, seg_col, seg_row, out, low, logs):
    total, head = key.shape
    block = total // blocks
    flip = order[0]
    start = [pl.multiple_of((jnp.int32(i) ^ flip) * block, block) for i in range(blocks)]
    ones = jnp.ones((block, head), bf16)
    for j in range(blocks):
        stacked = jnp.concatenate(
            [query[pl.ds(start[j], block), h * head : (h + 1) * head] for h in range(group)], axis=0
        )
        acc = jnp.zeros((group * block, 2 * head), f32)
        for k in range(j + 1):
            raw = dot_nt(stacked, key[pl.ds(start[k], block), :])
            allowed = allowed_pairs(j, k, start[j], start[k], block, seg_col, seg_row)
            allowed = jnp.concatenate([allowed] * group, axis=0)
            probs = jnp.where(allowed, jnp.exp2(raw * factor), 0.0).astype(bf16)
            both = jnp.concatenate([val[pl.ds(start[k], block), :], ones], axis=1)
            acc = acc + dot(probs, both)
        sums = acc[:, head:]
        result = acc[:, :head] / sums
        log_sums = jnp.log2(sums)
        for h in range(group):
            out[pl.ds(start[j], block), h * head : (h + 1) * head] = result[
                h * block : (h + 1) * block
            ]
            low[pl.ds(start[j], block), h * head : (h + 1) * head] = result[
                h * block : (h + 1) * block
            ].astype(bf16)
            logs[pl.ds(start[j], block), h * head : (h + 1) * head] = log_sums[
                h * block : (h + 1) * block
            ]


def attend(order, rot, val, seg_col, seg_row, q_heads, k_heads, head, blocks):
    total = rot.shape[0]
    group = q_heads // k_heads
    factor = head**-0.5 * math.log2(math.e)
    wide = pl.BlockSpec((total, group * head), lambda g, o: (0, g))
    return pl.pallas_call(
        functools.partial(attend_kernel, blocks, group, factor),
        grid_spec=pltpu.PrefetchScalarGridSpec(
            num_scalar_prefetch=1,
            grid=(k_heads,),
            in_specs=[
                wide,
                pl.BlockSpec((total, head), lambda g, o: (0, q_heads + g)),
                pl.BlockSpec((total, head), lambda g, o: (0, g)),
                pl.BlockSpec((total, 1), lambda g, o: (0, 0)),
                pl.BlockSpec((1, total), lambda g, o: (0, 0)),
            ],
            out_specs=[wide, wide, wide],
        ),
        out_shape=[jax.ShapeDtypeStruct((total, q_heads * head), kind) for kind in (f32, bf16, f32)],
        compiler_params=params(),
        cost_estimate=cost(4 * total * total * q_heads * head, total * q_heads * head * 12),
    )(order, rot, rot, val, seg_col, seg_row)


def attend_back_kernel(
    blocks, group, factor, scale, order, query, key, val, out_grad, out, logs, seg_col, seg_row,
    query_grad, key_grad, val_grad,
):
    total, head = key.shape
    block = total // blocks
    flip = order[0]
    start = [pl.multiple_of((jnp.int32(i) ^ flip) * block, block) for i in range(blocks)]

    def heads_of(ref, at):
        return jnp.concatenate(
            [ref[pl.ds(at, block), h * head : (h + 1) * head] for h in range(group)], axis=0
        )

    deltas = []
    for j in range(blocks):
        product = heads_of(out_grad, start[j]).astype(f32) * heads_of(out, start[j])
        deltas.append(jnp.sum(product, axis=1, keepdims=True))
    sums = [None] * blocks
    for k in range(blocks):
        key_block = key[pl.ds(start[k], block), :]
        val_block = val[pl.ds(start[k], block), :]
        key_sum = jnp.zeros((block, head), f32)
        val_sum = jnp.zeros((block, head), f32)
        for j in range(k, blocks):
            stacked = heads_of(query, start[j])
            grads = heads_of(out_grad, start[j])
            logged = heads_of(logs, start[j])
            logged = jnp.concatenate([logged] * (block // head), axis=1)
            raw = dot_nt(stacked, key_block)
            allowed = allowed_pairs(j, k, start[j], start[k], block, seg_col, seg_row)
            allowed = jnp.concatenate([allowed] * group, axis=0)
            probs = jnp.where(allowed, jnp.exp2(raw * factor - logged), 0.0)
            prob_grad = dot_nt(grads, val_block)
            score_grad = (probs * (prob_grad - deltas[j]) * scale).astype(bf16)
            val_sum = val_sum + dot_tn(probs.astype(bf16), grads)
            key_sum = key_sum + dot_tn(score_grad, stacked)
            piece = dot(score_grad, key_block)
            sums[j] = piece if k == 0 else sums[j] + piece
        key_grad[pl.ds(start[k], block), :] = key_sum
        val_grad[pl.ds(start[k], block), :] = val_sum
        for h in range(group):
            query_grad[pl.ds(start[k], block), h * head : (h + 1) * head] = sums[k][
                h * block : (h + 1) * block
            ]


def attend_back(order, rot, val, out_grad, out, logs, seg_col, seg_row, q_heads, k_heads, head, blocks):
    total = rot.shape[0]
    group = q_heads // k_heads
    scale = head**-0.5
    wide = pl.BlockSpec((total, group * head), lambda g, o: (0, g))
    thin = pl.BlockSpec((total, head), lambda g, o: (0, g))
    return pl.pallas_call(
        functools.partial(attend_back_kernel, blocks, group, scale * math.log2(math.e), scale),
        grid_spec=pltpu.PrefetchScalarGridSpec(
            num_scalar_prefetch=1,
            grid=(k_heads,),
            in_specs=[
                wide,
                pl.BlockSpec((total, head), lambda g, o: (0, q_heads + g)),
                thin,
                wide,
                wide,
                wide,
                pl.BlockSpec((total, 1), lambda g, o: (0, 0)),
                pl.BlockSpec((1, total), lambda g, o: (0, 0)),
            ],
            out_specs=[wide, thin, thin],
        ),
        out_shape=[
            jax.ShapeDtypeStruct((total, q_heads * head), f32),
            jax.ShapeDtypeStruct((total, k_heads * head), f32),
            jax.ShapeDtypeStruct((total, k_heads * head), f32),
        ],
        compiler_params=params(),
        cost_estimate=cost(10 * total * total * q_heads * head, total * q_heads * head * 20),
    )(order, rot, rot, val, out_grad, out, logs, seg_col, seg_row)


def feed_kernel(count, kept, weight, down, *refs):
    norm, cot = refs[:count], refs[count : 2 * count]
    hidden, gate_out, up_out, norm_all, cot_all, norm_grad, out, low_held, cot_held = refs[
        2 * count + kept :
    ]
    pick(norm, low_held)
    pick(cot, cot_held)
    units = down.shape[0]
    low = low_held[...]
    norm_all[...] = low
    cot_all[...] = cot_held[...]
    gate = dot(low, weight[:, :units])
    upper = dot(low, weight[:, units:])
    sigma = 1.0 / (1.0 + jnp.exp(-gate))
    silu = gate * sigma
    hid = (silu * upper).astype(bf16)
    hidden[...] = hid
    back = dot_nt(cot_held[...], down[...])
    gate_grad = (back * upper * sigma * (1.0 + gate * (1.0 - sigma))).astype(bf16)
    up_grad = (back * silu).astype(bf16)
    gate_out[...] = gate_grad
    up_out[...] = up_grad
    norm_grad[...] = (
        dot_nt(gate_grad, weight[:, :units]) + dot_nt(up_grad, weight[:, units:])
    ).astype(bf16)
    out[...] = dot(hid, down[...]).astype(bf16)


def feed(norm, cot, weight, down, first, blocks, before):
    count = len(norm)
    block, width = norm[0].shape
    total = block * blocks
    units = down.shape[0]
    kept = [units, units, units, width, width]
    return pl.pallas_call(
        functools.partial(feed_kernel, count, len(before)),
        grid=(count,),
        in_specs=[fixed_block(*weight.shape), fixed_block(*down.shape)]
        + [fixed_block(block, width)] * (2 * count)
        + [pl.BlockSpec(memory_space=pl.ANY)] * len(before),
        out_specs=[row_block(block, n, first) for n in kept] + [row_block(block, width)] * 2,
        out_shape=[jax.ShapeDtypeStruct((total, n), bf16) for n in kept]
        + [jax.ShapeDtypeStruct((block * count, width), bf16)] * 2,
        scratch_shapes=[pltpu.VMEM((block, width), bf16)] * 2,
        input_output_aliases={2 + 2 * count + i: i for i in range(len(before))},
        compiler_params=params(vmem_wide),
        cost_estimate=cost(
            12 * block * count * down.size, 6 * down.size + block * count * width * 16,
            block * count * units,
        ),
    )(weight, down, *norm, *cot, *before)


def branch_kernel(count, weight, *refs):
    branch, (out_grad, branch_all, held) = refs[:count], refs[count:]
    pick(branch, held)
    low = held[...]
    branch_all[...] = low
    out_grad[...] = dot_nt(low, weight[...]).astype(bf16)


def branch_back(branch, weight):
    count = len(branch)
    block, width = branch[0].shape
    total = block * count
    return pl.pallas_call(
        functools.partial(branch_kernel, count),
        grid=(count,),
        in_specs=[fixed_block(*weight.shape)] + [fixed_block(block, width)] * count,
        out_specs=[row_block(block, weight.shape[0]), row_block(block, width)],
        out_shape=[
            jax.ShapeDtypeStruct((total, weight.shape[0]), bf16),
            jax.ShapeDtypeStruct((total, width), bf16),
        ],
        scratch_shapes=[pltpu.VMEM((block, width), bf16)],
        compiler_params=params(),
        cost_estimate=cost(2 * total * weight.size, 2 * weight.size + total * width * 6),
    )(weight, *branch)


def unproject_kernel(
    q_heads, k_heads, count, query_grad, key_grad, val_grad, lin, cosine, sine, gains, weight, *refs
):
    tok, (query_out, pair_out, norm_grad, gain_sum, head_sum, held) = refs[:count], refs[count:]
    pick(tok, held)
    head = cosine.shape[1]
    cos_, sin_ = cosine[...], sine[...]
    sums = [jnp.zeros((1, head), f32), jnp.zeros((1, head), f32)]
    for index in range(q_heads + k_heads):
        which = 0 if index < q_heads else 1
        ref, result, spot = (
            (query_grad, query_out, index) if which == 0 else (key_grad, pair_out, index - q_heads)
        )
        turned = ref[:, spot * head : (spot + 1) * head]
        grad = turned * cos_ - half_turn(turned) * sin_
        rows = lin[:, index * head : (index + 1) * head]
        scale = inverse_root(rows)
        sums[which] = sums[which] + jnp.sum(grad * rows * scale, axis=0, keepdims=True)
        result[:, spot * head : (spot + 1) * head] = norm_back(
            grad * gains[which : which + 1, :], rows, scale
        ).astype(bf16)
    pair_out[:, k_heads * head :] = val_grad[...].astype(bf16)
    normed_grad = dot_nt(query_out[...], weight[:, : q_heads * head]) + dot_nt(
        pair_out[...], weight[:, q_heads * head :]
    )
    norm_grad[...] = normed_grad.astype(bf16)
    rows = held[...].astype(f32)
    gain_part = jnp.sum(normed_grad * rows * inverse_root(rows), axis=0, keepdims=True)

    @pl.when(pl.program_id(0) == 0)
    def _():
        gain_sum[...] = jnp.zeros_like(gain_sum)
        head_sum[...] = jnp.zeros_like(head_sum)

    gain_sum[...] += gain_part
    head_sum[...] += jnp.concatenate(sums, axis=0)


def unproject(query_grad, key_grad, val_grad, lin, cosine, sine, gains, weight, tok, q_heads, k_heads):
    count = len(tok)
    block, width = tok[0].shape
    total = block * count
    head = cosine.shape[1]
    q_width, kv_width = q_heads * head, 2 * k_heads * head
    return pl.pallas_call(
        functools.partial(unproject_kernel, q_heads, k_heads, count),
        grid=(count,),
        in_specs=[
            row_block(block, q_width),
            row_block(block, k_heads * head),
            row_block(block, k_heads * head),
            row_block(block, (q_heads + k_heads) * head),
            row_block(block, head),
            row_block(block, head),
            fixed_block(2, head),
            fixed_block(*weight.shape),
        ]
        + [fixed_block(block, width)] * count,
        out_specs=[
            row_block(block, q_width), row_block(block, kv_width), row_block(block, width),
            fixed_block(1, width), fixed_block(2, head),
        ],
        out_shape=[
            jax.ShapeDtypeStruct((total, q_width), bf16),
            jax.ShapeDtypeStruct((total, kv_width), bf16),
            jax.ShapeDtypeStruct((total, width), bf16),
            jax.ShapeDtypeStruct((1, width), f32),
            jax.ShapeDtypeStruct((2, head), f32),
        ],
        scratch_shapes=[pltpu.VMEM((block, width), bf16)],
        compiler_params=params(),
        cost_estimate=cost(2 * total * weight.size, 2 * weight.size + total * width * 16),
    )(query_grad, key_grad, val_grad, lin, cosine, sine, gains, weight, *tok)


def place_kernel(count, outs, moves, scalars, *refs):
    inputs, results = refs[:count], refs[count:]
    values = [scalars[i] for i in range(scalars.shape[0])]
    for source, index, rows, columns, target, spot in moves:
        piece = inputs[source][index + (slice(rows[0], rows[1]), slice(columns[0], columns[1]))]
        row, column = spot(*values)
        results[target][
            pl.ds(pl.multiple_of(row, 16), rows[1] - rows[0]),
            pl.ds(pl.multiple_of(column, 128), columns[1] - columns[0]),
        ] = piece.astype(results[target].dtype)


def place(scalars, inputs, out_shapes, moves):
    moved = sum(item.size * 2 for item in inputs) + sum(
        math.prod(shape) * (4 if kind == f32 else 2) for shape, kind in out_shapes
    )
    whole = pl.BlockSpec(memory_space=pltpu.VMEM)
    return pl.pallas_call(
        functools.partial(place_kernel, len(inputs), len(out_shapes), moves),
        in_specs=[pl.BlockSpec(memory_space=pltpu.SMEM)] + [whole] * len(inputs),
        out_specs=[whole] * len(out_shapes),
        out_shape=[jax.ShapeDtypeStruct(shape, kind) for shape, kind in out_shapes],
        compiler_params=params(),
        cost_estimate=cost(0, moved),
    )(scalars, *inputs)


def cut_kernel(sizes, which, scalars, *refs):
    inputs, (own, near, piece) = refs[: len(sizes)], refs[len(sizes) :]
    mine, part = scalars[0], scalars[which]
    half = piece.shape[1]
    begin = 0
    for ref, size in zip(inputs, sizes):
        lanes = lambda i: pl.ds(pl.multiple_of((mine ^ i) * size, 128), size)
        rows = pl.ds(pl.multiple_of(part * half, 16), half)
        own[:, begin : begin + size] = ref[:, lanes(0)]
        near[:, begin : begin + size] = ref[:, lanes(1)]
        piece[0, :, begin : begin + size] = ref[rows, lanes(2)]
        piece[1, :, begin : begin + size] = ref[rows, lanes(3)]
        begin += size


def cut(scalars, inputs, sizes, parts):
    rows = inputs[0].shape[0]
    wide = sum(sizes)
    whole = pl.BlockSpec(memory_space=pltpu.VMEM)
    shapes = [(rows, wide), (rows, wide), (2, rows // parts, wide)]
    return pl.pallas_call(
        functools.partial(cut_kernel, sizes, parts // 2 if parts == 2 else 3),
        in_specs=[pl.BlockSpec(memory_space=pltpu.SMEM)] + [whole] * len(inputs),
        out_specs=[whole] * 3,
        out_shape=[jax.ShapeDtypeStruct(shape, bf16) for shape in shapes],
        compiler_params=params(),
        cost_estimate=cost(0, 4 * sum(item.size for item in inputs)),
    )(scalars, *inputs)


def ring_kernel(layout, plan, count, sets, chunks, *refs):
    local = [refs[i * count : (i + 1) * count] for i in range(sets)]
    arrived = refs[sets * count : len(refs) - len(plan)]
    results = refs[len(refs) - len(plan) :]
    for result, (which, halves, adds) in zip(results, plan):
        for source, block, lane, size, to_block, to_lane in layout:
            for at, half in enumerate(halves):
                value = local[which][source][block, 0, half, :, lane : lane + size].astype(f32)
                for index, held in adds:
                    if half in held:
                        value = value + arrived[index][
                            to_block, held.index(half), :, to_lane : to_lane + size
                        ].astype(f32)
                result[to_block, at, :, to_lane : to_lane + size] = value.astype(bf16)


def ring_step(shares, layout, blocks, chunks, plan, arrived):
    lines, lanes = shares[0].shape[3], blocks[1]
    specs = []
    for which in range(len(chunks)):
        for share in shares:
            shape = (share.shape[0], 1) + share.shape[2:]
            specs.append(
                pl.BlockSpec(shape, lambda i, c, which=which: (0, c[which], 0, 0, 0))
            )
    whole = lambda shape: pl.BlockSpec(shape, lambda i, c: (0,) * len(shape))
    shapes = [(blocks[0], len(halves), lines, lanes) for _, halves, _ in plan]
    return pl.pallas_call(
        functools.partial(ring_kernel, layout, plan, len(shares), len(chunks)),
        grid_spec=pltpu.PrefetchScalarGridSpec(
            num_scalar_prefetch=1,
            grid=(1,),
            in_specs=specs + [whole(item.shape) for item in arrived],
            out_specs=[whole(shape) for shape in shapes],
        ),
        out_shape=[jax.ShapeDtypeStruct(shape, bf16) for shape in shapes],
        compiler_params=params(),
        cost_estimate=cost(0, 6 * sum(math.prod(shape) for shape in shapes)),
    )(jnp.stack(chunks).astype(jnp.int32), *shares * len(chunks), *arrived)


def split_kernel(pieces, scalars, chunk, own, near, far):
    mine = scalars[0]
    for i, (result, spot) in enumerate([(own, 0), (near, 0), (far, 0), (near, 1)]):
        begin = 0
        for block, lane, size in pieces(mine ^ i):
            result[spot, :, :, begin : begin + size] = chunk[
                block, :, :, pl.ds(pl.multiple_of(lane, 128), size)
            ]
            begin += size


def split(scalars, chunk, pieces, wide):
    whole = pl.BlockSpec(memory_space=pltpu.VMEM)
    lines = chunk.shape[1:3]
    shapes = [(1, *lines, wide), (2, *lines, wide), (1, *lines, wide)]
    return pl.pallas_call(
        functools.partial(split_kernel, pieces),
        in_specs=[pl.BlockSpec(memory_space=pltpu.SMEM), whole],
        out_specs=[whole] * 3,
        out_shape=[jax.ShapeDtypeStruct(shape, bf16) for shape in shapes],
        compiler_params=params(),
        cost_estimate=cost(0, 4 * chunk.size),
    )(scalars, chunk)


def pack_kernel(layout, *refs):
    inputs, result = refs[:-1], refs[-1]
    for source, block, lane, size, to_block, to_lane in layout:
        result[to_block, :, :, to_lane : to_lane + size] = inputs[source][
            block, :, :, lane : lane + size
        ]


def pack(inputs, layout, shape):
    whole = pl.BlockSpec(memory_space=pltpu.VMEM)
    return pl.pallas_call(
        functools.partial(pack_kernel, layout),
        in_specs=[whole] * len(inputs),
        out_specs=whole,
        out_shape=jax.ShapeDtypeStruct(shape, bf16),
        compiler_params=params(),
        cost_estimate=cost(0, 4 * math.prod(shape)),
    )(*inputs)


class Moves:
    def __init__(self):
        self.shards = lax.axis_size("shard")
        self.reps = lax.axis_size("rep")
        self.mine = lax.axis_index("shard")
        self.direct = self.shards == 4 and self.reps == 8
        self.flip = self.mine if self.direct else jnp.int32(0)
        rep = lax.axis_index("rep")
        self.bits = {1: rep % 2, 2: (rep // 2) % 2, 4: rep // 4}
        self.pos = jnp.where(rep % 2 == 0, rep // 2, 7 - rep // 2)
        self.ring = [0, 2, 4, 6, 7, 5, 3, 1]
        self.quarter = self.bits[1] * 2 + self.bits[2]
        self.scalars = jnp.stack([self.mine, self.bits[1], self.pos, self.quarter]).astype(jnp.int32)

    def up(self, item):
        ring = self.ring
        return lax.ppermute(item, "rep", [(ring[i], ring[(i + 1) % 8]) for i in range(8)])

    def down(self, item):
        ring = self.ring
        return lax.ppermute(item, "rep", [(ring[(i + 1) % 8], ring[i]) for i in range(8)])

    def swap(self, item, mask):
        return lax.ppermute(item, "shard", [(i, i ^ mask) for i in range(4)])

    def cross_rep(self, item, mask):
        return lax.ppermute(item, "rep", [(i, i ^ mask) for i in range(8)])

    def gather(self, item):
        if not self.direct:
            rows = item.shape[0]
            whole = lax.all_gather(item, "shard", axis=0, tiled=True)
            return [whole[i * rows : (i + 1) * rows] for i in range(self.shards)]
        far = self.swap(item, 2)
        near = self.swap(item, 1)
        cross = self.swap(far, 1)
        return [item, near, far, cross]

    def scatter(self, near_part, far_part):
        if not self.direct:
            item = jnp.concatenate([near_part, far_part], axis=0).astype(f32)
            return lax.psum_scatter(item, "shard", scatter_dimension=0, tiled=True)
        rows = near_part.shape[0] // 2
        far = self.swap(far_part[:rows] + self.swap(far_part[rows:], 1), 2)
        near = self.swap(near_part[rows:], 1)
        return near_part[:rows].astype(f32) + near.astype(f32) + far.astype(f32)

    def ring_scatter(self, shares, layout, blocks):
        return RingSum(self, shares, layout, blocks)

    def ring_gather(self, item):
        u1, d1 = self.up(item), self.down(item)
        u2, d2 = self.up(u1), self.down(d1)
        u3, d3 = self.up(u2), self.down(d2)
        u4, d4 = self.up(u3[:, :1]), self.down(d3[:, 1:])
        return [
            (item, 0, None), (u1, -1, None), (d1, 1, None), (u2, -2, None), (d2, 2, None),
            (u3, -3, None), (d3, 3, None), (u4, 4, 0), (d4, 4, 1),
        ]

    def exchange(self, chunk, pieces, wide):
        own, near, far = split(self.scalars, chunk, pieces, wide)
        near = self.swap(near, 1)
        far = self.swap(jnp.concatenate([far, near[1:]], axis=0), 2)
        return own, near, far


class RingSum:
    def __init__(self, moves, shares, layout, blocks):
        self.moves = moves
        self.step = functools.partial(ring_step, shares, layout, blocks)
        self.send(*self.step([self.chunk(4)], [(0, (0,), []), (0, (1,), [])], []))
        self.at = 4

    def chunk(self, offset):
        return (self.moves.pos + offset) % 8

    def send(self, u, d):
        self.sent = u
        self.arrived = [self.moves.up(u), self.moves.down(d)]

    def advance(self, *before):
        self.at -= 1
        both = (0, 1)
        u, d = self.arrived
        u = after(u, *before) if before else u
        held = [(0,), (1,)] if self.at == 3 else [both, both]
        plan = [(0, both, [(0, held[0])]), (1, both, [(1, held[1])])]
        self.send(*self.step([self.chunk(self.at), self.chunk(8 - self.at)], plan, [u, d]))

    def finish(self, *before):
        both = (0, 1)
        u, d = self.arrived
        u = after(u, *before) if before else u
        return self.step([self.chunk(0)], [(0, both, [(0, both), (1, both)])], [u, d])[0]


class Fetch:
    def __init__(self, moves, own, near, piece, spot, shape):
        self.moves, self.own, self.near, self.piece = moves, own, near, piece
        self.spot, self.shape = spot, shape

    def start(self, *before):
        self.here = self.moves.swap(after(self.piece, *before), 2)
        self.there = self.moves.cross_rep(self.here, 1)

    def finish(self):
        moves, here, there, spot = self.moves, self.here, self.there, self.spot
        rows, width = self.own.shape
        half = rows // 2
        near = moves.swap(self.near, 1)
        inputs = [self.own, near, here, moves.swap(here[1], 1), there, moves.swap(there[1], 1)]
        todo = [
            (0, (), (0, rows), (0, width), 0, lambda shard, *_: spot(shard, 0)),
            (1, (), (0, rows), (0, width), 0, lambda shard, *_: spot(shard ^ 1, 0)),
            (2, (0,), (0, half), (0, width), 0, lambda shard, y, *_: spot(shard ^ 2, y * half)),
            (3, (), (0, half), (0, width), 0, lambda shard, y, *_: spot(shard ^ 3, y * half)),
            (4, (0,), (0, half), (0, width), 0, lambda shard, y, *_: spot(shard ^ 2, (1 - y) * half)),
            (5, (), (0, half), (0, width), 0, lambda shard, y, *_: spot(shard ^ 3, (1 - y) * half)),
        ]
        return place(moves.scalars, inputs, [(self.shape, bf16)], todo)[0]


class DeepFetch(Fetch):
    def start(self, *before):
        moves = self.moves
        self.here = moves.swap(after(self.piece, *before), 2)
        pair = jnp.concatenate([self.here, moves.cross_rep(self.here, 1)], axis=0)
        self.parts = [pair, moves.cross_rep(pair, 2)]

    def finish(self):
        moves, spot = self.moves, self.spot
        first, second = self.parts
        rows, width = self.own.shape
        size = rows // 4
        cross = moves.swap(jnp.stack([first[1], first[3], second[1], second[3]]), 1)
        inputs = [self.own, moves.swap(self.near, 1), first, second, cross]
        todo = [
            (0, (), (0, rows), (0, width), 0, lambda shard, *_: spot(shard, 0)),
            (1, (), (0, rows), (0, width), 0, lambda shard, *_: spot(shard ^ 1, 0)),
        ]
        for i, (source, index, mask) in enumerate([(2, 0, 0), (2, 2, 2), (3, 0, 1), (3, 2, 3)]):
            for which, where, at in ((2, source, index), (3, 4, i)):

                def to(shard, y, pos, quarter, which=which, mask=mask):
                    return spot(shard ^ which, (quarter ^ mask) * size)

                todo.append((where, (at,), (0, size), (0, width), 0, to))
        return place(moves.scalars, inputs, [(self.shape, bf16)], todo)[0]


def after(item, *others):
    return lax.optimization_barrier((item, *others))[0]


def per_device(
    tokens, segments, grad_out, attention_gain, query_weight, key_matrix, value_matrix, query_gain,
    key_gain, output_weight, mlp_gain, gate_weight, up_weight, down_weight,
):
    moves = Moves()
    shards, mine, direct = moves.shards, moves.mine, moves.direct
    rows, width = tokens.shape[1:]
    total = rows * shards
    slice_width = attention_gain.shape[0]
    head_slice = query_gain.shape[0]
    head = head_slice * shards
    k_heads = key_matrix.shape[1] // head // shards
    q_heads = query_weight.shape[1] // head // shards
    q_width, k_width = q_heads * head, k_heads * head
    units = down_weight.shape[0]
    own_tokens = tokens[0]
    cot = grad_out[0]

    if direct:
        by_rows = lambda source, line: (source * slice_width + line, 0)
        qkv = Fetch(
            moves,
            *cut(moves.scalars, [query_weight, key_matrix, value_matrix], [q_width, k_width, k_width], 2),
            by_rows,
            (width, q_width + 2 * k_width),
        )
        qkv.start()
        attention_gain = after(attention_gain, qkv.here)
    small = jnp.concatenate(
        [attention_gain, mlp_gain, query_gain, key_gain, segments[0].astype(bf16)]
    )[None]
    small = jnp.concatenate(moves.gather(small), axis=0)
    if direct:
        whole = jnp.where(mine % 2 == 0, small, small[jnp.array([1, 0, 3, 2])])
        whole = jnp.where(mine // 2 == 0, whole, whole[jnp.array([2, 3, 0, 1])])
    else:
        whole = small
    cuts = [slice_width, 2 * slice_width, 2 * slice_width + head_slice, 2 * slice_width + 2 * head_slice]
    input_gain = whole[:, : cuts[0]].reshape(1, width).astype(f32)
    second_gain = whole[:, cuts[0] : cuts[1]].reshape(1, width).astype(f32)
    head_gains = jnp.stack(
        [whole[:, cuts[1] : cuts[2]].reshape(head), whole[:, cuts[2] : cuts[3]].reshape(head)]
    ).astype(f32)
    segs = small[:, cuts[3] :].reshape(total).astype(f32)
    index = jnp.arange(shards, dtype=jnp.int32) ^ moves.flip
    places = (index[:, None] * rows + jnp.arange(rows, dtype=jnp.int32)[None]).reshape(total)
    firsts = jnp.sum((segs < 0.5).astype(jnp.int32))
    seconds = jnp.sum((segs < 1.5).astype(jnp.int32))
    opening = jnp.where(segs < 0.5, 0, jnp.where(segs < 1.5, firsts, seconds))
    freqs = theta_base ** (-(jnp.arange(head // 2, dtype=f32) * 2.0) / head)
    angles = (places - opening).astype(f32)[:, None] * freqs
    cosine, sine = jnp.cos(angles), jnp.sin(angles)
    cosine = jnp.concatenate([cosine, cosine], axis=1)
    sine = jnp.concatenate([-sine, sine], axis=1)
    seg_col, seg_row = segs[:, None], segs[None, :]
    order = moves.flip.astype(jnp.int32)[None]

    all_tokens = all_cot = None
    if direct:
        outer = lambda i, begin, n: lax.dynamic_slice(
            output_weight, ((mine ^ i) * q_width + begin, 0), (n, slice_width)
        )
        half = q_width // 2
        output = Fetch(
            moves,
            outer(0, 0, q_width),
            outer(1, 0, q_width),
            jnp.stack([outer(2, moves.bits[1] * half, half), outer(3, moves.bits[1] * half, half)]),
            lambda source, line: (line, source * slice_width),
            (q_width, width),
        )
        both = DeepFetch(
            moves,
            *cut(moves.scalars, [gate_weight, up_weight], [units, units], 4),
            by_rows,
            (width, 2 * units),
        )
        all_tokens = moves.gather(after(own_tokens, qkv.here))
        output.start(all_tokens[2], qkv.there)
        qkv_weight = qkv.finish()
        both.start(output.here)
        out_weight = output.finish()
        all_cot = moves.gather(after(cot, both.here))
    else:
        spread = lambda item: lax.all_to_all(item, "shard", split_axis=1, concat_axis=0, tiled=True)
        qkv_weight = jnp.concatenate(
            [spread(query_weight), spread(key_matrix), spread(value_matrix)], axis=1
        )
        out_weight = lax.all_to_all(output_weight, "shard", split_axis=0, concat_axis=1, tiled=True)
        feed_weight = jnp.concatenate([spread(gate_weight), spread(up_weight)], axis=1)

    if not direct:
        all_tokens, all_cot = moves.gather(own_tokens), moves.gather(cot)
    normed_one, lin, rot, val = project(
        all_tokens, input_gain, qkv_weight, cosine, sine, head_gains, q_heads, k_heads
    )
    attended, attended_low, logs = attend(order, rot, val, seg_col, seg_row, q_heads, k_heads, head, shards)
    inputs = own_tokens.astype(f32)
    split = total // 2
    if direct:
        feed_weight = both.finish()
        attended_low = after(attended_low, both.here)
    far_part = dot(attended_low[split:], out_weight).astype(bf16)
    near_part = dot(attended_low[:split], out_weight).astype(bf16)
    residual_one = inputs + moves.scatter(near_part, far_part)
    residual_scale = inverse_root(residual_one)
    normed_two = moves.gather((residual_one * residual_scale * second_gain).astype(bf16))

    *kept, norm_grad, out_part = feed(
        normed_two, all_cot, feed_weight, down_weight, 0, shards, []
    )
    hidden, gate_grad, up_grad, normed_two, all_cot = kept
    if direct:
        crossed = norm_grad[2 * rows : 3 * rows] + moves.swap(norm_grad[3 * rows :], 1)
        hidden, gate_grad = after(hidden, crossed), after(gate_grad, crossed)
        up_grad = after(up_grad, crossed)
        near_grad = norm_grad[:rows].astype(f32) + moves.swap(norm_grad[rows : 2 * rows], 1).astype(f32)
        normed_grad_two = near_grad + moves.swap(crossed, 2).astype(f32)
    else:
        normed_grad_two = moves.scatter(norm_grad[:split], norm_grad[split:])
    share_down = dot_tn(hidden, all_cot).astype(bf16)
    share_gate = dot_tn(normed_two, gate_grad).astype(bf16)
    share_up = dot_tn(normed_two, up_grad).astype(bf16)
    mlp_gain_part = jnp.sum(normed_grad_two * residual_one * residual_scale, axis=0)
    residual_grad = cot.astype(f32) + norm_back(
        normed_grad_two * second_gain, residual_one, residual_scale
    )
    branch_low = residual_grad.astype(bf16)
    branch_grad = moves.gather(branch_low)
    if direct:
        lines = slice_width // 16
        rest = 2 * units - width
        as_chunks = lambda share: share.reshape(-1, 8, 2, lines, share.shape[1])
        spot_of = lambda values, offset: lax.rem(values[2] + (offset + 8), 8) * (2 * lines)

        downs = units // slice_width
        blocks = (6 + downs, width)
        layout = []
        for i in range(4):
            layout += [
                (0, i, 0, units, i, 0),
                (1, i, 0, width - units, i, units),
                (1, i, width - units, rest, 4 + i // 2, (i % 2) * rest),
            ]
        layout += [(2, b, 0, width, 6 + b, 0) for b in range(downs)]
        ring = moves.ring_scatter(
            [as_chunks(share_gate), as_chunks(share_up), as_chunks(share_down)], layout, blocks
        )
        ring.advance(branch_low)

    out_part = after(out_part, *branch_grad)
    layer_out = (residual_one + moves.scatter(out_part[:split], out_part[split:])).astype(bf16)

    far_branch = branch_grad[2]
    out_grad, branch_grad = branch_back(branch_grad, out_weight)
    share_out = dot_tn(attended_low, branch_grad).astype(bf16)
    if direct:
        ring.advance(far_branch)
        out_grad = after(out_grad, ring.sent)
    query_grad, key_grad, val_grad = attend_back(
        order, rot, val, out_grad, attended, logs, seg_col, seg_row, q_heads, k_heads, head, shards
    )
    if direct:
        ring.advance(query_grad)
        query_grad = after(query_grad, ring.sent)
    query_lin_grad, pair_lin_grad, norm_one_part, gain_part, head_part = unproject(
        query_grad, key_grad, val_grad, lin, cosine, sine, head_gains, qkv_weight, all_tokens,
        q_heads, k_heads,
    )
    share_query = dot_tn(normed_one, query_lin_grad).astype(bf16)
    share_pair = dot_tn(normed_one, pair_lin_grad).astype(bf16)
    normed_grad_one = moves.scatter(norm_one_part[:split], norm_one_part[split:])
    grad_tokens = residual_grad + norm_back(normed_grad_one * input_gain, inputs, inverse_root(inputs))

    gains = jnp.concatenate([gain_part[0], mlp_gain_part, head_part.reshape(2 * head)])[None]
    if direct:
        gains = gains + moves.swap(gains, 1)
        gains = gains + moves.swap(gains, 2)
        for mask in (1, 2, 4):
            gains = gains + moves.cross_rep(gains, mask)
    else:
        gains = lax.psum(gains, ("shard", "rep"))
    gains = gains[0]

    def own_part(begin, size):
        return lax.dynamic_slice_in_dim(gains, begin + mine * size, size, 0)

    grad_attention_gain = own_part(0, slice_width)
    grad_mlp_gain = own_part(width, slice_width)
    grad_query_gain = own_part(2 * width, head_slice)
    grad_key_gain = own_part(2 * width + head, head_slice)

    if direct:
        chunk = ring.finish()
        own, near, far = moves.exchange(
            chunk, lambda at: [(at, 0, width), (4 + at // 2, (at % 2) * rest, rest)], 2 * units
        )
        layout = []
        for i, (source, index) in enumerate([(0, 0), (1, 0), (2, 0), (2, 1)]):
            layout += [
                (source, index, 0, width, i, 0),
                (source, index, width, rest, 4 + i // 2, (i % 2) * rest),
            ]
        layout += [(3, 6 + b, 0, width, 6 + b, 0) for b in range(downs)]
        parts = moves.ring_gather(
            pack([own, near, far, chunk], layout, (blocks[0], 2, lines, width))
        )
        todo = []
        for source, (part, offset, half) in enumerate(parts):
            for h in range(part.shape[1]):
                line = ((half or 0) + h) * lines
                for i in range(4):

                    def at(*values, i=i, line=line, offset=offset, begin=0):
                        return spot_of(values, offset) + line, (values[0] ^ i) * units + begin

                    first = width - units
                    todo += [
                        (source, (i, h), (0, lines), (0, units), 0, at),
                        (source, (i, h), (0, lines), (units, width), 1, at),
                        (
                            source, (4 + i // 2, h), (0, lines),
                            ((i % 2) * rest, (i % 2) * rest + rest), 1,
                            functools.partial(at, begin=first),
                        ),
                    ]
                for b in range(downs):

                    def at(*values, b=b, line=line, offset=offset):
                        return b * slice_width + spot_of(values, offset) + line, 0

                    todo.append((source, (6 + b, h), (0, lines), (0, width), 2, at))
        shapes = [((slice_width, units * 4), f32)] * 2 + [((units, width), f32)]
        grad_gate, grad_up, grad_down = place(
            moves.scalars, [part for part, _, _ in parts], shapes, todo
        )

        first_near, first_packed = near, parts[0][0]

        outs = q_width // slice_width
        pair = 2 * k_width
        wide = q_width + pair
        layout = []
        for i in range(4):
            layout += [(0, i, 0, q_width, i, 0), (1, i, 0, pair, i, q_width)]
        layout += [(2, b, 0, width, 4 + b, 0) for b in range(outs)]
        ring = moves.ring_scatter(
            [as_chunks(share_query), as_chunks(share_pair), as_chunks(share_out)],
            layout,
            (4 + outs, width),
        )
        ring.advance(first_near)
        ring.advance(first_packed)
        ring.advance()
        chunk = ring.finish()
        own, near, far = moves.exchange(
            chunk,
            lambda at: [(at, 0, wide)] + [(4 + b, at * slice_width, slice_width) for b in range(outs)],
            wide + outs * slice_width,
        )
        wide_all = wide + outs * slice_width
        layout = [
            (source, index, 0, wide_all, i, 0)
            for i, (source, index) in enumerate([(0, 0), (1, 0), (2, 0), (2, 1)])
        ]
        parts = moves.ring_gather(pack([own, near, far], layout, (4, 2, lines, wide_all)))
        todo = []
        for source, (part, offset, half) in enumerate(parts):
            for h in range(part.shape[1]):
                line = ((half or 0) + h) * lines
                for i in range(4):
                    begin = 0
                    for target, size in enumerate([q_width, k_width, k_width]):

                        def at(*values, i=i, line=line, offset=offset, size=size):
                            return spot_of(values, offset) + line, (values[0] ^ i) * size

                        todo.append((source, (i, h), (0, lines), (begin, begin + size), target, at))
                        begin += size
                    for b in range(outs):

                        def at(*values, i=i, b=b, line=line, offset=offset):
                            first = (values[0] ^ i) * q_width + b * slice_width
                            return first + spot_of(values, offset) + line, 0

                        todo.append(
                            (source, (i, h), (0, lines), (begin, begin + slice_width), 3, at)
                        )
                        begin += slice_width
        shapes = [((slice_width, size * 4), f32) for size in (q_width, k_width, k_width)]
        shapes.append(((q_width * 4, slice_width), f32))
        grad_query, grad_key, grad_value, grad_output = place(
            moves.scalars, [part for part, _, _ in parts], shapes, todo
        )
    else:

        def finish(share):
            part = lax.all_to_all(share, "shard", split_axis=0, concat_axis=1, tiled=True)
            return lax.psum(part, "rep").astype(f32)

        grad_down = lax.psum(share_down, "rep").astype(f32)
        grad_gate = finish(share_gate)
        grad_up = finish(share_up)
        grad_output = lax.psum(
            lax.all_to_all(share_out, "shard", split_axis=1, concat_axis=0, tiled=True), "rep"
        ).astype(f32)
        grad_query = finish(share_query)
        grad_key = finish(share_pair[:, :k_width])
        grad_value = finish(share_pair[:, k_width:])

    return (
        layer_out[None], grad_tokens[None], grad_attention_gain, grad_query, grad_key, grad_value,
        grad_query_gain, grad_key_gain, grad_output, grad_mlp_gain, grad_gate, grad_up, grad_down,
    )


def solution(mesh):
    rows_over = P("shard", None)
    return jax.shard_map(
        per_device,
        mesh=mesh,
        in_specs=(
            P("rep", "shard", None), P("rep", "shard"), P("rep", "shard", None), P("shard"), rows_over,
            rows_over, rows_over, P("shard"), P("shard"), P(None, "shard"), P("shard"), rows_over,
            rows_over, rows_over,
        ),
        out_specs=(
            P("rep", "shard", None), P("rep", "shard", None), P("shard"), rows_over, rows_over,
            rows_over, P("shard"), P("shard"), P(None, "shard"), P("shard"), rows_over, rows_over,
            rows_over,
        ),
        check_vma=False,
    )
```

```python
import functools
import math

import jax
import jax.numpy as jnp
from jax import lax
from jax.experimental import pallas as pl
from jax.experimental.pallas import tpu as pltpu
from jax.sharding import PartitionSpec as P

eps_norm = 1e-06
theta_base = 1000000.0
f32 = jnp.float32
bf16 = jnp.bfloat16
vmem_bytes = 32 * 1024 * 1024
vmem_wide = 42 * 1024 * 1024


def dot(left, right):
    return lax.dot_general(left, right, (((1,), (0,)), ((), ())), preferred_element_type=f32)


def dot_nt(left, right):
    return lax.dot_general(left, right, (((1,), (1,)), ((), ())), preferred_element_type=f32)


def dot_tn(left, right):
    return lax.dot_general(left, right, (((0,), (0,)), ((), ())), preferred_element_type=f32)


def inverse_root(rows):
    return lax.rsqrt(jnp.mean(rows * rows, axis=-1, keepdims=True) + eps_norm)


def norm_back(grad, rows, scale):
    return scale * grad - rows * (scale * scale * scale) * jnp.mean(
        grad * rows, axis=-1, keepdims=True
    )


def params(limit=vmem_bytes):
    return pltpu.CompilerParams(vmem_limit_bytes=limit)


def cost(flops, moved, trans=0):
    return pl.CostEstimate(flops=int(flops), bytes_accessed=int(moved), transcendentals=int(trans))


def half_turn(rows):
    return pltpu.roll(rows, rows.shape[-1] // 2, axis=1)


def pick(refs, held):
    for k, ref in enumerate(refs):

        @pl.when(pl.program_id(0) == k)
        def _(ref=ref):
            held[...] = ref[...]


def project_kernel(
    q_heads, k_heads, count, gain, weight, cosine, sine, gains, *refs
):
    tok, (normed, lin, rot, val, held) = refs[:count], refs[count:]
    pick(tok, held)
    rows = held[...].astype(f32)
    low = (rows * inverse_root(rows) * gain[...]).astype(bf16)
    normed[...] = low
    head = cosine.shape[1]
    full = dot(low, weight[...])
    cos_, sin_ = cosine[...], sine[...]
    for index in range(q_heads + k_heads):
        part = full[:, index * head : (index + 1) * head]
        lin[:, index * head : (index + 1) * head] = part
        which = 0 if index < q_heads else 1
        unit = part * inverse_root(part) * gains[which : which + 1, :]
        rot[:, index * head : (index + 1) * head] = (unit * cos_ + half_turn(unit) * sin_).astype(
            bf16
        )
    val[...] = full[:, (q_heads + k_heads) * head :].astype(bf16)


def row_block(rows, columns, first=0):
    return pl.BlockSpec((rows, columns), lambda i: (i + first, 0))


def fixed_block(rows, columns):
    return pl.BlockSpec((rows, columns), lambda i: (0, 0))


def project(tok, gain, weight, cosine, sine, gains, q_heads, k_heads):
    count = len(tok)
    block, width = tok[0].shape
    total = block * count
    head = cosine.shape[1]
    qk = (q_heads + k_heads) * head
    kv = k_heads * head
    return pl.pallas_call(
        functools.partial(project_kernel, q_heads, k_heads, count),
        grid=(count,),
        in_specs=[
            fixed_block(1, width),
            fixed_block(*weight.shape),
            row_block(block, head),
            row_block(block, head),
            fixed_block(2, head),
        ]
        + [fixed_block(block, width)] * count,
        out_specs=[row_block(block, n) for n in (width, qk, qk, kv)],
        out_shape=[
            jax.ShapeDtypeStruct((total, width), bf16),
            jax.ShapeDtypeStruct((total, qk), f32),
            jax.ShapeDtypeStruct((total, qk), bf16),
            jax.ShapeDtypeStruct((total, kv), bf16),
        ],
        scratch_shapes=[pltpu.VMEM((block, width), bf16)],
        compiler_params=params(vmem_wide),
        cost_estimate=cost(2 * total * weight.size, 2 * weight.size + total * width * 12),
    )(gain, weight, cosine, sine, gains, *tok)


def allowed_pairs(j, k, start_q, start_k, block, seg_col, seg_row):
    own = seg_col[pl.ds(start_q, block), :]
    other = seg_row[:, pl.ds(start_k, block)]
    allowed = own == other
    if j == k:
        at_q = lax.broadcasted_iota(jnp.int32, (block, block), 0)
        at_k = lax.broadcasted_iota(jnp.int32, (block, block), 1)
        allowed = allowed & (at_q >= at_k)
    return allowed


def attend_kernel(blocks, group, factor, order, query, key, val, seg_col, seg_row, out, low, logs):
    total, head = key.shape
    block = total // blocks
    flip = order[0]
    start = [pl.multiple_of((jnp.int32(i) ^ flip) * block, block) for i in range(blocks)]
    ones = jnp.ones((block, head), bf16)
    for j in range(blocks):
        stacked = jnp.concatenate(
            [query[pl.ds(start[j], block), h * head : (h + 1) * head] for h in range(group)], axis=0
        )
        acc = jnp.zeros((group * block, 2 * head), f32)
        for k in range(j + 1):
            raw = dot_nt(stacked, key[pl.ds(start[k], block), :])
            allowed = allowed_pairs(j, k, start[j], start[k], block, seg_col, seg_row)
            allowed = jnp.concatenate([allowed] * group, axis=0)
            probs = jnp.where(allowed, jnp.exp2(raw * factor), 0.0).astype(bf16)
            both = jnp.concatenate([val[pl.ds(start[k], block), :], ones], axis=1)
            acc = acc + dot(probs, both)
        sums = acc[:, head:]
        result = acc[:, :head] / sums
        log_sums = jnp.log2(sums)
        for h in range(group):
            out[pl.ds(start[j], block), h * head : (h + 1) * head] = result[
                h * block : (h + 1) * block
            ]
            low[pl.ds(start[j], block), h * head : (h + 1) * head] = result[
                h * block : (h + 1) * block
            ].astype(bf16)
            logs[pl.ds(start[j], block), h * head : (h + 1) * head] = log_sums[
                h * block : (h + 1) * block
            ]


def attend(order, rot, val, seg_col, seg_row, q_heads, k_heads, head, blocks):
    total = rot.shape[0]
    group = q_heads // k_heads
    factor = head**-0.5 * math.log2(math.e)
    wide = pl.BlockSpec((total, group * head), lambda g, o: (0, g))
    return pl.pallas_call(
        functools.partial(attend_kernel, blocks, group, factor),
        grid_spec=pltpu.PrefetchScalarGridSpec(
            num_scalar_prefetch=1,
            grid=(k_heads,),
            in_specs=[
                wide,
                pl.BlockSpec((total, head), lambda g, o: (0, q_heads + g)),
                pl.BlockSpec((total, head), lambda g, o: (0, g)),
                pl.BlockSpec((total, 1), lambda g, o: (0, 0)),
                pl.BlockSpec((1, total), lambda g, o: (0, 0)),
            ],
            out_specs=[wide, wide, wide],
        ),
        out_shape=[jax.ShapeDtypeStruct((total, q_heads * head), kind) for kind in (f32, bf16, f32)],
        compiler_params=params(),
        cost_estimate=cost(4 * total * total * q_heads * head, total * q_heads * head * 12),
    )(order, rot, rot, val, seg_col, seg_row)


def attend_back_kernel(
    blocks, group, factor, scale, order, query, key, val, out_grad, out, logs, seg_col, seg_row,
    query_grad, key_grad, val_grad,
):
    total, head = key.shape
    block = total // blocks
    flip = order[0]
    start = [pl.multiple_of((jnp.int32(i) ^ flip) * block, block) for i in range(blocks)]

    def heads_of(ref, at):
        return jnp.concatenate(
            [ref[pl.ds(at, block), h * head : (h + 1) * head] for h in range(group)], axis=0
        )

    deltas = []
    for j in range(blocks):
        product = heads_of(out_grad, start[j]).astype(f32) * heads_of(out, start[j])
        deltas.append(jnp.sum(product, axis=1, keepdims=True))
    sums = [None] * blocks
    for k in range(blocks):
        key_block = key[pl.ds(start[k], block), :]
        val_block = val[pl.ds(start[k], block), :]
        key_sum = jnp.zeros((block, head), f32)
        val_sum = jnp.zeros((block, head), f32)
        for j in range(k, blocks):
            stacked = heads_of(query, start[j])
            grads = heads_of(out_grad, start[j])
            logged = heads_of(logs, start[j])
            logged = jnp.concatenate([logged] * (block // head), axis=1)
            raw = dot_nt(stacked, key_block)
            allowed = allowed_pairs(j, k, start[j], start[k], block, seg_col, seg_row)
            allowed = jnp.concatenate([allowed] * group, axis=0)
            probs = jnp.where(allowed, jnp.exp2(raw * factor - logged), 0.0)
            prob_grad = dot_nt(grads, val_block)
            score_grad = (probs * (prob_grad - deltas[j]) * scale).astype(bf16)
            val_sum = val_sum + dot_tn(probs.astype(bf16), grads)
            key_sum = key_sum + dot_tn(score_grad, stacked)
            piece = dot(score_grad, key_block)
            sums[j] = piece if k == 0 else sums[j] + piece
        key_grad[pl.ds(start[k], block), :] = key_sum
        val_grad[pl.ds(start[k], block), :] = val_sum
        for h in range(group):
            query_grad[pl.ds(start[k], block), h * head : (h + 1) * head] = sums[k][
                h * block : (h + 1) * block
            ]


def attend_back(order, rot, val, out_grad, out, logs, seg_col, seg_row, q_heads, k_heads, head, blocks):
    total = rot.shape[0]
    group = q_heads // k_heads
    scale = head**-0.5
    wide = pl.BlockSpec((total, group * head), lambda g, o: (0, g))
    thin = pl.BlockSpec((total, head), lambda g, o: (0, g))
    return pl.pallas_call(
        functools.partial(attend_back_kernel, blocks, group, scale * math.log2(math.e), scale),
        grid_spec=pltpu.PrefetchScalarGridSpec(
            num_scalar_prefetch=1,
            grid=(k_heads,),
            in_specs=[
                wide,
                pl.BlockSpec((total, head), lambda g, o: (0, q_heads + g)),
                thin,
                wide,
                wide,
                wide,
                pl.BlockSpec((total, 1), lambda g, o: (0, 0)),
                pl.BlockSpec((1, total), lambda g, o: (0, 0)),
            ],
            out_specs=[wide, thin, thin],
        ),
        out_shape=[
            jax.ShapeDtypeStruct((total, q_heads * head), f32),
            jax.ShapeDtypeStruct((total, k_heads * head), f32),
            jax.ShapeDtypeStruct((total, k_heads * head), f32),
        ],
        compiler_params=params(),
        cost_estimate=cost(10 * total * total * q_heads * head, total * q_heads * head * 20),
    )(order, rot, rot, val, out_grad, out, logs, seg_col, seg_row)


def feed_kernel(count, kept, weight, down, *refs):
    norm, cot = refs[:count], refs[count : 2 * count]
    hidden, gate_out, up_out, norm_all, cot_all, out, *norm_grad, low_held, cot_held = refs[
        2 * count + kept :
    ]
    pick(norm, low_held)
    pick(cot, cot_held)
    units = down.shape[0]
    low = low_held[...]
    norm_all[...] = low
    cot_all[...] = cot_held[...]
    gate = dot(low, weight[:, :units])
    upper = dot(low, weight[:, units:])
    sigma = 1.0 / (1.0 + jnp.exp(-gate))
    silu = gate * sigma
    hid = (silu * upper).astype(bf16)
    hidden[...] = hid
    back = dot_nt(cot_held[...], down[...])
    gate_grad = (back * upper * sigma * (1.0 + gate * (1.0 - sigma))).astype(bf16)
    up_grad = (back * silu).astype(bf16)
    gate_out[...] = gate_grad
    up_out[...] = up_grad
    back_low = (
        dot_nt(gate_grad, weight[:, :units]) + dot_nt(up_grad, weight[:, units:])
    ).astype(bf16)
    for k, ref in enumerate(norm_grad):

        @pl.when(pl.program_id(0) == k)
        def _(ref=ref):
            ref[...] = back_low

    out[...] = dot(hid, down[...]).astype(bf16)


def feed(norm, cot, weight, down, first, blocks, before):
    count = len(norm)
    block, width = norm[0].shape
    total = block * blocks
    units = down.shape[0]
    kept = [units, units, units, width, width]
    return pl.pallas_call(
        functools.partial(feed_kernel, count, len(before)),
        grid=(count,),
        in_specs=[fixed_block(*weight.shape), fixed_block(*down.shape)]
        + [fixed_block(block, width)] * (2 * count)
        + [pl.BlockSpec(memory_space=pl.ANY)] * len(before),
        out_specs=[row_block(block, n, first) for n in kept] + [row_block(block, width)]
        + [fixed_block(block, width)] * count,
        out_shape=[jax.ShapeDtypeStruct((total, n), bf16) for n in kept]
        + [jax.ShapeDtypeStruct((block * count, width), bf16)]
        + [jax.ShapeDtypeStruct((block, width), bf16)] * count,
        scratch_shapes=[pltpu.VMEM((block, width), bf16)] * 2,
        input_output_aliases={2 + 2 * count + i: i for i in range(len(before))},
        compiler_params=params(vmem_wide),
        cost_estimate=cost(
            12 * block * count * down.size, 6 * down.size + block * count * width * 16,
            block * count * units,
        ),
    )(weight, down, *norm, *cot, *before)


def branch_kernel(count, weight, *refs):
    branch, (out_grad, branch_all, held) = refs[:count], refs[count:]
    pick(branch, held)
    low = held[...]
    branch_all[...] = low
    out_grad[...] = dot_nt(low, weight[...]).astype(bf16)


def branch_back(branch, weight):
    count = len(branch)
    block, width = branch[0].shape
    total = block * count
    return pl.pallas_call(
        functools.partial(branch_kernel, count),
        grid=(count,),
        in_specs=[fixed_block(*weight.shape)] + [fixed_block(block, width)] * count,
        out_specs=[row_block(block, weight.shape[0]), row_block(block, width)],
        out_shape=[
            jax.ShapeDtypeStruct((total, weight.shape[0]), bf16),
            jax.ShapeDtypeStruct((total, width), bf16),
        ],
        scratch_shapes=[pltpu.VMEM((block, width), bf16)],
        compiler_params=params(),
        cost_estimate=cost(2 * total * weight.size, 2 * weight.size + total * width * 6),
    )(weight, *branch)


def unproject_kernel(
    q_heads, k_heads, count, query_grad, key_grad, val_grad, lin, cosine, sine, gains, weight, *refs
):
    tok, (query_out, pair_out, norm_grad, gain_sum, head_sum, held) = refs[:count], refs[count:]
    pick(tok, held)
    head = cosine.shape[1]
    cos_, sin_ = cosine[...], sine[...]
    sums = [jnp.zeros((1, head), f32), jnp.zeros((1, head), f32)]
    for index in range(q_heads + k_heads):
        which = 0 if index < q_heads else 1
        ref, result, spot = (
            (query_grad, query_out, index) if which == 0 else (key_grad, pair_out, index - q_heads)
        )
        turned = ref[:, spot * head : (spot + 1) * head]
        grad = turned * cos_ - half_turn(turned) * sin_
        rows = lin[:, index * head : (index + 1) * head]
        scale = inverse_root(rows)
        sums[which] = sums[which] + jnp.sum(grad * rows * scale, axis=0, keepdims=True)
        result[:, spot * head : (spot + 1) * head] = norm_back(
            grad * gains[which : which + 1, :], rows, scale
        ).astype(bf16)
    pair_out[:, k_heads * head :] = val_grad[...].astype(bf16)
    normed_grad = dot_nt(query_out[...], weight[:, : q_heads * head]) + dot_nt(
        pair_out[...], weight[:, q_heads * head :]
    )
    norm_grad[...] = normed_grad.astype(bf16)
    rows = held[...].astype(f32)
    gain_part = jnp.sum(normed_grad * rows * inverse_root(rows), axis=0, keepdims=True)

    @pl.when(pl.program_id(0) == 0)
    def _():
        gain_sum[...] = jnp.zeros_like(gain_sum)
        head_sum[...] = jnp.zeros_like(head_sum)

    gain_sum[...] += gain_part
    head_sum[...] += jnp.concatenate(sums, axis=0)


def unproject(query_grad, key_grad, val_grad, lin, cosine, sine, gains, weight, tok, q_heads, k_heads):
    count = len(tok)
    block, width = tok[0].shape
    total = block * count
    head = cosine.shape[1]
    q_width, kv_width = q_heads * head, 2 * k_heads * head
    return pl.pallas_call(
        functools.partial(unproject_kernel, q_heads, k_heads, count),
        grid=(count,),
        in_specs=[
            row_block(block, q_width),
            row_block(block, k_heads * head),
            row_block(block, k_heads * head),
            row_block(block, (q_heads + k_heads) * head),
            row_block(block, head),
            row_block(block, head),
            fixed_block(2, head),
            fixed_block(*weight.shape),
        ]
        + [fixed_block(block, width)] * count,
        out_specs=[
            row_block(block, q_width), row_block(block, kv_width), row_block(block, width),
            fixed_block(1, width), fixed_block(2, head),
        ],
        out_shape=[
            jax.ShapeDtypeStruct((total, q_width), bf16),
            jax.ShapeDtypeStruct((total, kv_width), bf16),
            jax.ShapeDtypeStruct((total, width), bf16),
            jax.ShapeDtypeStruct((1, width), f32),
            jax.ShapeDtypeStruct((2, head), f32),
        ],
        scratch_shapes=[pltpu.VMEM((block, width), bf16)],
        compiler_params=params(),
        cost_estimate=cost(2 * total * weight.size, 2 * weight.size + total * width * 16),
    )(query_grad, key_grad, val_grad, lin, cosine, sine, gains, weight, *tok)


def place_kernel(count, outs, moves, scalars, *refs):
    inputs, results = refs[:count], refs[count:]
    values = [scalars[i] for i in range(scalars.shape[0])]
    for source, index, rows, columns, target, spot in moves:
        piece = inputs[source][index + (slice(rows[0], rows[1]), slice(columns[0], columns[1]))]
        row, column = spot(*values)
        results[target][
            pl.ds(pl.multiple_of(row, 16), rows[1] - rows[0]),
            pl.ds(pl.multiple_of(column, 128), columns[1] - columns[0]),
        ] = piece.astype(results[target].dtype)


def place(scalars, inputs, out_shapes, moves):
    moved = sum(item.size * 2 for item in inputs) + sum(
        math.prod(shape) * (4 if kind == f32 else 2) for shape, kind in out_shapes
    )
    whole = pl.BlockSpec(memory_space=pltpu.VMEM)
    return pl.pallas_call(
        functools.partial(place_kernel, len(inputs), len(out_shapes), moves),
        in_specs=[pl.BlockSpec(memory_space=pltpu.SMEM)] + [whole] * len(inputs),
        out_specs=[whole] * len(out_shapes),
        out_shape=[jax.ShapeDtypeStruct(shape, kind) for shape, kind in out_shapes],
        compiler_params=params(),
        cost_estimate=cost(0, moved),
    )(scalars, *inputs)


def cut_kernel(sizes, which, scalars, *refs):
    inputs, (own, near, piece) = refs[: len(sizes)], refs[len(sizes) :]
    mine, part = scalars[0], scalars[which]
    half = piece.shape[1]
    begin = 0
    for ref, size in zip(inputs, sizes):
        lanes = lambda i: pl.ds(pl.multiple_of((mine ^ i) * size, 128), size)
        rows = pl.ds(pl.multiple_of(part * half, 16), half)
        own[:, begin : begin + size] = ref[:, lanes(0)]
        near[:, begin : begin + size] = ref[:, lanes(1)]
        piece[0, :, begin : begin + size] = ref[rows, lanes(2)]
        piece[1, :, begin : begin + size] = ref[rows, lanes(3)]
        begin += size


def cut(scalars, inputs, sizes, parts):
    rows = inputs[0].shape[0]
    wide = sum(sizes)
    whole = pl.BlockSpec(memory_space=pltpu.VMEM)
    shapes = [(rows, wide), (rows, wide), (2, rows // parts, wide)]
    return pl.pallas_call(
        functools.partial(cut_kernel, sizes, parts // 2 if parts == 2 else 3),
        in_specs=[pl.BlockSpec(memory_space=pltpu.SMEM)] + [whole] * len(inputs),
        out_specs=[whole] * 3,
        out_shape=[jax.ShapeDtypeStruct(shape, bf16) for shape in shapes],
        compiler_params=params(),
        cost_estimate=cost(0, 4 * sum(item.size for item in inputs)),
    )(scalars, *inputs)


def ring_kernel(layout, plan, count, sets, chunks, *refs):
    local = [refs[i * count : (i + 1) * count] for i in range(sets)]
    arrived = refs[sets * count : len(refs) - len(plan)]
    results = refs[len(refs) - len(plan) :]
    for result, (which, halves, adds) in zip(results, plan):
        for source, block, lane, size, to_block, to_lane in layout:
            for at, half in enumerate(halves):
                value = local[which][source][block, 0, half, :, lane : lane + size].astype(f32)
                for index, held in adds:
                    if half in held:
                        value = value + arrived[index][
                            to_block, held.index(half), :, to_lane : to_lane + size
                        ].astype(f32)
                result[to_block, at, :, to_lane : to_lane + size] = value.astype(bf16)


def ring_step(shares, layout, blocks, chunks, plan, arrived):
    lines, lanes = shares[0].shape[3], blocks[1]
    specs = []
    for which in range(len(chunks)):
        for share in shares:
            shape = (share.shape[0], 1) + share.shape[2:]
            specs.append(
                pl.BlockSpec(shape, lambda i, c, which=which: (0, c[which], 0, 0, 0))
            )
    whole = lambda shape: pl.BlockSpec(shape, lambda i, c: (0,) * len(shape))
    shapes = [(blocks[0], len(halves), lines, lanes) for _, halves, _ in plan]
    return pl.pallas_call(
        functools.partial(ring_kernel, layout, plan, len(shares), len(chunks)),
        grid_spec=pltpu.PrefetchScalarGridSpec(
            num_scalar_prefetch=1,
            grid=(1,),
            in_specs=specs + [whole(item.shape) for item in arrived],
            out_specs=[whole(shape) for shape in shapes],
        ),
        out_shape=[jax.ShapeDtypeStruct(shape, bf16) for shape in shapes],
        compiler_params=params(),
        cost_estimate=cost(0, 6 * sum(math.prod(shape) for shape in shapes)),
    )(jnp.stack(chunks).astype(jnp.int32), *shares * len(chunks), *arrived)


def split_kernel(pieces, scalars, chunk, own, near, far):
    mine = scalars[0]
    for i, (result, spot) in enumerate([(own, 0), (near, 0), (far, 0), (near, 1)]):
        begin = 0
        for block, lane, size in pieces(mine ^ i):
            result[spot, :, :, begin : begin + size] = chunk[
                block, :, :, pl.ds(pl.multiple_of(lane, 128), size)
            ]
            begin += size


def split(scalars, chunk, pieces, wide):
    whole = pl.BlockSpec(memory_space=pltpu.VMEM)
    lines = chunk.shape[1:3]
    shapes = [(1, *lines, wide), (2, *lines, wide), (1, *lines, wide)]
    return pl.pallas_call(
        functools.partial(split_kernel, pieces),
        in_specs=[pl.BlockSpec(memory_space=pltpu.SMEM), whole],
        out_specs=[whole] * 3,
        out_shape=[jax.ShapeDtypeStruct(shape, bf16) for shape in shapes],
        compiler_params=params(),
        cost_estimate=cost(0, 4 * chunk.size),
    )(scalars, chunk)


def pack_kernel(layout, *refs):
    inputs, result = refs[:-1], refs[-1]
    for source, block, lane, size, to_block, to_lane in layout:
        result[to_block, :, :, to_lane : to_lane + size] = inputs[source][
            block, :, :, lane : lane + size
        ]


def pack(inputs, layout, shape):
    whole = pl.BlockSpec(memory_space=pltpu.VMEM)
    return pl.pallas_call(
        functools.partial(pack_kernel, layout),
        in_specs=[whole] * len(inputs),
        out_specs=whole,
        out_shape=jax.ShapeDtypeStruct(shape, bf16),
        compiler_params=params(),
        cost_estimate=cost(0, 4 * math.prod(shape)),
    )(*inputs)


class Moves:
    def __init__(self):
        self.shards = lax.axis_size("shard")
        self.reps = lax.axis_size("rep")
        self.mine = lax.axis_index("shard")
        self.direct = self.shards == 4 and self.reps == 8
        self.flip = self.mine if self.direct else jnp.int32(0)
        rep = lax.axis_index("rep")
        self.bits = {1: rep % 2, 2: (rep // 2) % 2, 4: rep // 4}
        self.pos = jnp.where(rep % 2 == 0, rep // 2, 7 - rep // 2)
        self.ring = [0, 2, 4, 6, 7, 5, 3, 1]
        self.quarter = self.bits[1] * 2 + self.bits[2]
        self.scalars = jnp.stack([self.mine, self.bits[1], self.pos, self.quarter]).astype(jnp.int32)

    def up(self, item):
        ring = self.ring
        return lax.ppermute(item, "rep", [(ring[i], ring[(i + 1) % 8]) for i in range(8)])

    def down(self, item):
        ring = self.ring
        return lax.ppermute(item, "rep", [(ring[(i + 1) % 8], ring[i]) for i in range(8)])

    def swap(self, item, mask):
        return lax.ppermute(item, "shard", [(i, i ^ mask) for i in range(4)])

    def cross_rep(self, item, mask):
        return lax.ppermute(item, "rep", [(i, i ^ mask) for i in range(8)])

    def gather(self, item):
        if not self.direct:
            rows = item.shape[0]
            whole = lax.all_gather(item, "shard", axis=0, tiled=True)
            return [whole[i * rows : (i + 1) * rows] for i in range(self.shards)]
        far = self.swap(item, 2)
        near = self.swap(item, 1)
        cross = self.swap(far, 1)
        return [item, near, far, cross]

    def scatter(self, near_part, far_part):
        if not self.direct:
            item = jnp.concatenate([near_part, far_part], axis=0).astype(f32)
            return lax.psum_scatter(item, "shard", scatter_dimension=0, tiled=True)
        rows = near_part.shape[0] // 2
        far = self.swap(far_part[:rows] + self.swap(far_part[rows:], 1), 2)
        near = self.swap(near_part[rows:], 1)
        return near_part[:rows].astype(f32) + near.astype(f32) + far.astype(f32)

    def ring_scatter(self, shares, layout, blocks):
        return RingSum(self, shares, layout, blocks)

    def ring_gather(self, item, *before):
        u1, d1 = self.up(item), self.down(item)
        u2, d2 = self.up(u1), self.down(d1)
        u3, d3 = self.up(u2), self.down(d2)
        last = after(u3, *before) if before else u3
        u4, d4 = self.up(last[:, :1]), self.down(d3[:, 1:])
        return [
            (item, 0, None), (u1, -1, None), (d1, 1, None), (u2, -2, None), (d2, 2, None),
            (u3, -3, None), (d3, 3, None), (u4, 4, 0), (d4, 4, 1),
        ]

    def exchange(self, chunk, pieces, wide):
        own, near, far = split(self.scalars, chunk, pieces, wide)
        near = self.swap(near, 1)
        far = self.swap(jnp.concatenate([far, near[1:]], axis=0), 2)
        return own, near, far


class RingSum:
    def __init__(self, moves, shares, layout, blocks):
        self.moves = moves
        self.step = functools.partial(ring_step, shares, layout, blocks)
        self.send(*self.step([self.chunk(4)], [(0, (0,), []), (0, (1,), [])], []))
        self.at = 4

    def chunk(self, offset):
        return (self.moves.pos + offset) % 8

    def send(self, u, d):
        self.sent = u
        self.arrived = [self.moves.up(u), self.moves.down(d)]

    def advance(self, *before):
        self.at -= 1
        both = (0, 1)
        u, d = self.arrived
        u = after(u, *before) if before else u
        held = [(0,), (1,)] if self.at == 3 else [both, both]
        plan = [(0, both, [(0, held[0])]), (1, both, [(1, held[1])])]
        self.send(*self.step([self.chunk(self.at), self.chunk(8 - self.at)], plan, [u, d]))

    def finish(self, *before):
        both = (0, 1)
        u, d = self.arrived
        u = after(u, *before) if before else u
        return self.step([self.chunk(0)], [(0, both, [(0, both), (1, both)])], [u, d])[0]


class Fetch:
    def __init__(self, moves, own, near, piece, spot, shape):
        self.moves, self.own, self.near, self.piece = moves, own, near, piece
        self.spot, self.shape = spot, shape

    def start(self, *before):
        self.here = self.moves.swap(after(self.piece, *before), 2)
        self.there = self.moves.cross_rep(self.here, 1)

    def finish(self):
        moves, here, there, spot = self.moves, self.here, self.there, self.spot
        rows, width = self.own.shape
        half = rows // 2
        near = moves.swap(self.near, 1)
        inputs = [self.own, near, here, moves.swap(here[1], 1), there, moves.swap(there[1], 1)]
        todo = [
            (0, (), (0, rows), (0, width), 0, lambda shard, *_: spot(shard, 0)),
            (1, (), (0, rows), (0, width), 0, lambda shard, *_: spot(shard ^ 1, 0)),
            (2, (0,), (0, half), (0, width), 0, lambda shard, y, *_: spot(shard ^ 2, y * half)),
            (3, (), (0, half), (0, width), 0, lambda shard, y, *_: spot(shard ^ 3, y * half)),
            (4, (0,), (0, half), (0, width), 0, lambda shard, y, *_: spot(shard ^ 2, (1 - y) * half)),
            (5, (), (0, half), (0, width), 0, lambda shard, y, *_: spot(shard ^ 3, (1 - y) * half)),
        ]
        return place(moves.scalars, inputs, [(self.shape, bf16)], todo)[0]


class DeepFetch(Fetch):
    def start(self, *before):
        moves = self.moves
        self.here = moves.swap(after(self.piece, *before), 2)
        pair = jnp.concatenate([self.here, moves.cross_rep(self.here, 1)], axis=0)
        self.parts = [pair, moves.cross_rep(pair, 2)]

    def finish(self):
        moves, spot = self.moves, self.spot
        first, second = self.parts
        rows, width = self.own.shape
        size = rows // 4
        cross = moves.swap(jnp.stack([first[1], first[3], second[1], second[3]]), 1)
        inputs = [self.own, moves.swap(self.near, 1), first, second, cross]
        todo = [
            (0, (), (0, rows), (0, width), 0, lambda shard, *_: spot(shard, 0)),
            (1, (), (0, rows), (0, width), 0, lambda shard, *_: spot(shard ^ 1, 0)),
        ]
        for i, (source, index, mask) in enumerate([(2, 0, 0), (2, 2, 2), (3, 0, 1), (3, 2, 3)]):
            for which, where, at in ((2, source, index), (3, 4, i)):

                def to(shard, y, pos, quarter, which=which, mask=mask):
                    return spot(shard ^ which, (quarter ^ mask) * size)

                todo.append((where, (at,), (0, size), (0, width), 0, to))
        return place(moves.scalars, inputs, [(self.shape, bf16)], todo)[0]


def after(item, *others):
    return lax.optimization_barrier((item, *others))[0]


def per_device(
    tokens, segments, grad_out, attention_gain, query_weight, key_matrix, value_matrix, query_gain,
    key_gain, output_weight, mlp_gain, gate_weight, up_weight, down_weight,
):
    moves = Moves()
    shards, mine, direct = moves.shards, moves.mine, moves.direct
    rows, width = tokens.shape[1:]
    total = rows * shards
    slice_width = attention_gain.shape[0]
    head_slice = query_gain.shape[0]
    head = head_slice * shards
    k_heads = key_matrix.shape[1] // head // shards
    q_heads = query_weight.shape[1] // head // shards
    q_width, k_width = q_heads * head, k_heads * head
    units = down_weight.shape[0]
    own_tokens = tokens[0]
    cot = grad_out[0]

    if direct:
        by_rows = lambda source, line: (source * slice_width + line, 0)
        qkv = Fetch(
            moves,
            *cut(moves.scalars, [query_weight, key_matrix, value_matrix], [q_width, k_width, k_width], 2),
            by_rows,
            (width, q_width + 2 * k_width),
        )
        qkv.start()
        attention_gain = after(attention_gain, qkv.piece)
    small = jnp.concatenate(
        [attention_gain, mlp_gain, query_gain, key_gain, segments[0].astype(bf16)]
    )[None]
    small = jnp.concatenate(moves.gather(small), axis=0)
    if direct:
        whole = jnp.where(mine % 2 == 0, small, small[jnp.array([1, 0, 3, 2])])
        whole = jnp.where(mine // 2 == 0, whole, whole[jnp.array([2, 3, 0, 1])])
    else:
        whole = small
    cuts = [slice_width, 2 * slice_width, 2 * slice_width + head_slice, 2 * slice_width + 2 * head_slice]
    input_gain = whole[:, : cuts[0]].reshape(1, width).astype(f32)
    second_gain = whole[:, cuts[0] : cuts[1]].reshape(1, width).astype(f32)
    head_gains = jnp.stack(
        [whole[:, cuts[1] : cuts[2]].reshape(head), whole[:, cuts[2] : cuts[3]].reshape(head)]
    ).astype(f32)
    segs = small[:, cuts[3] :].reshape(total).astype(f32)
    index = jnp.arange(shards, dtype=jnp.int32) ^ moves.flip
    places = (index[:, None] * rows + jnp.arange(rows, dtype=jnp.int32)[None]).reshape(total)
    firsts = jnp.sum((segs < 0.5).astype(jnp.int32))
    seconds = jnp.sum((segs < 1.5).astype(jnp.int32))
    opening = jnp.where(segs < 0.5, 0, jnp.where(segs < 1.5, firsts, seconds))
    freqs = theta_base ** (-(jnp.arange(head // 2, dtype=f32) * 2.0) / head)
    angles = (places - opening).astype(f32)[:, None] * freqs
    cosine, sine = jnp.cos(angles), jnp.sin(angles)
    cosine = jnp.concatenate([cosine, cosine], axis=1)
    sine = jnp.concatenate([-sine, sine], axis=1)
    seg_col, seg_row = segs[:, None], segs[None, :]
    order = moves.flip.astype(jnp.int32)[None]

    all_tokens = all_cot = None
    if direct:
        outer = lambda i, begin, n: lax.dynamic_slice(
            output_weight, ((mine ^ i) * q_width + begin, 0), (n, slice_width)
        )
        half = q_width // 2
        output = Fetch(
            moves,
            outer(0, 0, q_width),
            outer(1, 0, q_width),
            jnp.stack([outer(2, moves.bits[1] * half, half), outer(3, moves.bits[1] * half, half)]),
            lambda source, line: (line, source * slice_width),
            (q_width, width),
        )
        both = DeepFetch(
            moves,
            *cut(moves.scalars, [gate_weight, up_weight], [units, units], 4),
            by_rows,
            (width, 2 * units),
        )
        all_tokens = moves.gather(after(own_tokens, qkv.here))
        output.start(all_tokens[2], qkv.there)
        qkv_weight = qkv.finish()
        both.start(output.here)
        out_weight = output.finish()
        all_cot = moves.gather(after(cot, both.here))
    else:
        spread = lambda item: lax.all_to_all(item, "shard", split_axis=1, concat_axis=0, tiled=True)
        qkv_weight = jnp.concatenate(
            [spread(query_weight), spread(key_matrix), spread(value_matrix)], axis=1
        )
        out_weight = lax.all_to_all(output_weight, "shard", split_axis=0, concat_axis=1, tiled=True)
        feed_weight = jnp.concatenate([spread(gate_weight), spread(up_weight)], axis=1)

    if not direct:
        all_tokens, all_cot = moves.gather(own_tokens), moves.gather(cot)
    normed_one, lin, rot, val = project(
        all_tokens, input_gain, qkv_weight, cosine, sine, head_gains, q_heads, k_heads
    )
    if direct:
        rot = after(rot, both.here)
    attended, attended_low, logs = attend(order, rot, val, seg_col, seg_row, q_heads, k_heads, head, shards)
    inputs = own_tokens.astype(f32)
    split = total // 2
    if direct:
        feed_weight = both.finish()
        attended_low = after(attended_low, all_cot[2])
    far_part = dot(attended_low[split:], out_weight).astype(bf16)
    near_part = dot(attended_low[:split], out_weight).astype(bf16)
    residual_one = inputs + moves.scatter(near_part, far_part)
    residual_scale = inverse_root(residual_one)
    normed_two = moves.gather((residual_one * residual_scale * second_gain).astype(bf16))

    hidden, gate_grad, up_grad, normed_two, all_cot, out_part, *norm_grad = feed(
        normed_two, all_cot, feed_weight, down_weight, 0, shards, []
    )
    if direct:
        crossed = norm_grad[2] + moves.swap(norm_grad[3], 1)
        hidden, gate_grad = after(hidden, crossed), after(gate_grad, crossed)
        up_grad = after(up_grad, crossed)
        near_grad = norm_grad[0].astype(f32) + moves.swap(norm_grad[1], 1).astype(f32)
        far_grad = moves.swap(crossed, 2)
    else:
        norm_grad = jnp.concatenate(norm_grad, axis=0)
        normed_grad_two = moves.scatter(norm_grad[:split], norm_grad[split:])
    share_down = dot_tn(hidden, all_cot).astype(bf16)
    share_gate = dot_tn(normed_two, gate_grad).astype(bf16)
    share_up = dot_tn(normed_two, up_grad).astype(bf16)
    if direct:
        lines = slice_width // 16
        rest = 2 * units - width
        as_chunks = lambda share: share.reshape(-1, 8, 2, lines, share.shape[1])
        spot_of = lambda values, offset: lax.rem(values[2] + (offset + 8), 8) * (2 * lines)

        downs = units // slice_width
        blocks = (6 + downs, width)
        layout = []
        for i in range(4):
            layout += [
                (0, i, 0, units, i, 0),
                (1, i, 0, width - units, i, units),
                (1, i, width - units, rest, 4 + i // 2, (i % 2) * rest),
            ]
        layout += [(2, b, 0, width, 6 + b, 0) for b in range(downs)]
        ring = moves.ring_scatter(
            [as_chunks(share_gate), as_chunks(share_up), as_chunks(share_down)], layout, blocks
        )
        normed_grad_two = near_grad + after(far_grad, ring.sent).astype(f32)
    mlp_gain_part = jnp.sum(normed_grad_two * residual_one * residual_scale, axis=0)
    residual_grad = cot.astype(f32) + norm_back(
        normed_grad_two * second_gain, residual_one, residual_scale
    )
    branch_low = residual_grad.astype(bf16)
    if direct:
        ring.advance(branch_low)
        far_branch = after(moves.swap(branch_low, 2), ring.sent)
        branch_grad = [
            branch_low, moves.swap(branch_low, 1), far_branch, moves.swap(far_branch, 1),
        ]
    else:
        branch_grad = moves.gather(branch_low)
    out_part = after(out_part, *branch_grad)
    layer_out = (residual_one + moves.scatter(out_part[:split], out_part[split:])).astype(bf16)

    out_grad, branch_grad = branch_back(branch_grad, out_weight)
    share_out = dot_tn(attended_low, branch_grad).astype(bf16)
    if direct:
        ring.advance(out_grad)
        out_grad = after(out_grad, ring.sent)
    query_grad, key_grad, val_grad = attend_back(
        order, rot, val, out_grad, attended, logs, seg_col, seg_row, q_heads, k_heads, head, shards
    )
    if direct:
        ring.advance(query_grad)
        query_grad = after(query_grad, ring.sent)
    query_lin_grad, pair_lin_grad, norm_one_part, gain_part, head_part = unproject(
        query_grad, key_grad, val_grad, lin, cosine, sine, head_gains, qkv_weight, all_tokens,
        q_heads, k_heads,
    )
    share_query = dot_tn(normed_one, query_lin_grad).astype(bf16)
    share_pair = dot_tn(normed_one, pair_lin_grad).astype(bf16)
    normed_grad_one = moves.scatter(norm_one_part[:split], norm_one_part[split:])
    grad_tokens = residual_grad + norm_back(normed_grad_one * input_gain, inputs, inverse_root(inputs))

    gains = jnp.concatenate([gain_part[0], mlp_gain_part, head_part.reshape(2 * head)])[None]
    if direct:
        gains = gains + moves.swap(gains, 1)
        gains = gains + moves.swap(gains, 2)
        for mask in (1, 2, 4):
            gains = gains + moves.cross_rep(gains, mask)
    else:
        gains = lax.psum(gains, ("shard", "rep"))
    gains = gains[0]

    def own_part(begin, size):
        return lax.dynamic_slice_in_dim(gains, begin + mine * size, size, 0)

    grad_attention_gain = own_part(0, slice_width)
    grad_mlp_gain = own_part(width, slice_width)
    grad_query_gain = own_part(2 * width, head_slice)
    grad_key_gain = own_part(2 * width + head, head_slice)

    if direct:
        chunk = ring.finish()
        own, near, far = moves.exchange(
            chunk, lambda at: [(at, 0, width), (4 + at // 2, (at % 2) * rest, rest)], 2 * units
        )
        layout = []
        for i, (source, index) in enumerate([(0, 0), (1, 0), (2, 0), (2, 1)]):
            layout += [
                (source, index, 0, width, i, 0),
                (source, index, width, rest, 4 + i // 2, (i % 2) * rest),
            ]
        layout += [(3, 6 + b, 0, width, 6 + b, 0) for b in range(downs)]
        parts = moves.ring_gather(
            pack([own, near, far, chunk], layout, (blocks[0], 2, lines, width))
        )
        todo = []
        for source, (part, offset, half) in enumerate(parts):
            for h in range(part.shape[1]):
                line = ((half or 0) + h) * lines
                for i in range(4):

                    def at(*values, i=i, line=line, offset=offset, begin=0):
                        return spot_of(values, offset) + line, (values[0] ^ i) * units + begin

                    first = width - units
                    todo += [
                        (source, (i, h), (0, lines), (0, units), 0, at),
                        (source, (i, h), (0, lines), (units, width), 1, at),
                        (
                            source, (4 + i // 2, h), (0, lines),
                            ((i % 2) * rest, (i % 2) * rest + rest), 1,
                            functools.partial(at, begin=first),
                        ),
                    ]
                for b in range(downs):

                    def at(*values, b=b, line=line, offset=offset):
                        return b * slice_width + spot_of(values, offset) + line, 0

                    todo.append((source, (6 + b, h), (0, lines), (0, width), 2, at))
        shapes = [((slice_width, units * 4), f32)] * 2 + [((units, width), f32)]
        grad_gate, grad_up, grad_down = place(
            moves.scalars, [part for part, _, _ in parts], shapes, todo
        )

        first_near, first_packed, first_last = near, parts[0][0], parts[-1][0]

        outs = q_width // slice_width
        pair = 2 * k_width
        wide = q_width + pair
        layout = []
        for i in range(4):
            layout += [(0, i, 0, q_width, i, 0), (1, i, 0, pair, i, q_width)]
        layout += [(2, b, 0, width, 4 + b, 0) for b in range(outs)]
        ring = moves.ring_scatter(
            [as_chunks(share_query), as_chunks(share_pair), as_chunks(share_out)],
            layout,
            (4 + outs, width),
        )
        ring.advance(first_near)
        ring.advance(first_packed)
        ring.advance()
        chunk = ring.finish()
        own, near, far = moves.exchange(
            chunk,
            lambda at: [(at, 0, wide)] + [(4 + b, at * slice_width, slice_width) for b in range(outs)],
            wide + outs * slice_width,
        )
        wide_all = wide + outs * slice_width
        layout = [
            (source, index, 0, wide_all, i, 0)
            for i, (source, index) in enumerate([(0, 0), (1, 0), (2, 0), (2, 1)])
        ]
        parts = moves.ring_gather(pack([own, near, far], layout, (4, 2, lines, wide_all)), first_last)
        todo = []
        for source, (part, offset, half) in enumerate(parts):
            for h in range(part.shape[1]):
                line = ((half or 0) + h) * lines
                for i in range(4):
                    begin = 0
                    for target, size in enumerate([q_width, k_width, k_width]):

                        def at(*values, i=i, line=line, offset=offset, size=size):
                            return spot_of(values, offset) + line, (values[0] ^ i) * size

                        todo.append((source, (i, h), (0, lines), (begin, begin + size), target, at))
                        begin += size
                    for b in range(outs):

                        def at(*values, i=i, b=b, line=line, offset=offset):
                            first = (values[0] ^ i) * q_width + b * slice_width
                            return first + spot_of(values, offset) + line, 0

                        todo.append(
                            (source, (i, h), (0, lines), (begin, begin + slice_width), 3, at)
                        )
                        begin += slice_width
        shapes = [((slice_width, size * 4), f32) for size in (q_width, k_width, k_width)]
        shapes.append(((q_width * 4, slice_width), f32))
        grad_query, grad_key, grad_value, grad_output = place(
            moves.scalars, [part for part, _, _ in parts], shapes, todo
        )
    else:

        def finish(share):
            part = lax.all_to_all(share, "shard", split_axis=0, concat_axis=1, tiled=True)
            return lax.psum(part, "rep").astype(f32)

        grad_down = lax.psum(share_down, "rep").astype(f32)
        grad_gate = finish(share_gate)
        grad_up = finish(share_up)
        grad_output = lax.psum(
            lax.all_to_all(share_out, "shard", split_axis=1, concat_axis=0, tiled=True), "rep"
        ).astype(f32)
        grad_query = finish(share_query)
        grad_key = finish(share_pair[:, :k_width])
        grad_value = finish(share_pair[:, k_width:])

    return (
        layer_out[None], grad_tokens[None], grad_attention_gain, grad_query, grad_key, grad_value,
        grad_query_gain, grad_key_gain, grad_output, grad_mlp_gain, grad_gate, grad_up, grad_down,
    )


def solution(mesh):
    rows_over = P("shard", None)
    return jax.shard_map(
        per_device,
        mesh=mesh,
        in_specs=(
            P("rep", "shard", None), P("rep", "shard"), P("rep", "shard", None), P("shard"), rows_over,
            rows_over, rows_over, P("shard"), P("shard"), P(None, "shard"), P("shard"), rows_over,
            rows_over, rows_over,
        ),
        out_specs=(
            P("rep", "shard", None), P("rep", "shard", None), P("shard"), rows_over, rows_over,
            rows_over, P("shard"), P("shard"), P(None, "shard"), P("shard"), rows_over, rows_over,
            rows_over,
        ),
        check_vma=False,
    )
```

```python
import functools
import math

import jax
import jax.numpy as jnp
from jax import lax
from jax.experimental import pallas as pl
from jax.experimental.pallas import tpu as pltpu
from jax.sharding import PartitionSpec as P

eps_norm = 1e-06
theta_base = 1000000.0
f32 = jnp.float32
bf16 = jnp.bfloat16
vmem_bytes = 24 * 1024 * 1024
vmem_wide = 42 * 1024 * 1024
vmem_feed = 48 * 1024 * 1024


def dot(left, right):
    return lax.dot_general(left, right, (((1,), (0,)), ((), ())), preferred_element_type=f32)


def dot_nt(left, right):
    return lax.dot_general(left, right, (((1,), (1,)), ((), ())), preferred_element_type=f32)


def dot_tn(left, right):
    return lax.dot_general(left, right, (((0,), (0,)), ((), ())), preferred_element_type=f32)


def inverse_root(rows):
    return lax.rsqrt(jnp.mean(rows * rows, axis=-1, keepdims=True) + eps_norm)


def norm_back(grad, rows, scale):
    return scale * grad - rows * (scale * scale * scale) * jnp.mean(
        grad * rows, axis=-1, keepdims=True
    )


def params(limit=vmem_bytes):
    return pltpu.CompilerParams(vmem_limit_bytes=limit)


def cost(flops, moved, trans=0):
    return pl.CostEstimate(flops=int(flops), bytes_accessed=int(moved), transcendentals=int(trans))


def half_turn(rows):
    return pltpu.roll(rows, rows.shape[-1] // 2, axis=1)


def pick(refs, held):
    rows = refs[0].shape[0]
    count = held.shape[0] // rows
    for k in range(len(refs) // count):

        @pl.when(pl.program_id(0) == k)
        def _(k=k):
            for i in range(count):
                held[i * rows : (i + 1) * rows, :] = refs[k * count + i][...]


def project_kernel(
    q_heads, k_heads, count, gain, weight, cosine, sine, gains, *refs
):
    tok, (normed, lin, rot, val, held) = refs[:count], refs[count:]
    pick(tok, held)
    rows = held[...].astype(f32)
    low = (rows * inverse_root(rows) * gain[...]).astype(bf16)
    normed[...] = low
    head = cosine.shape[1]
    full = dot(low, weight[...])
    cos_, sin_ = cosine[...], sine[...]
    for index in range(q_heads + k_heads):
        part = full[:, index * head : (index + 1) * head]
        lin[:, index * head : (index + 1) * head] = part
        which = 0 if index < q_heads else 1
        unit = part * inverse_root(part) * gains[which : which + 1, :]
        rot[:, index * head : (index + 1) * head] = (unit * cos_ + half_turn(unit) * sin_).astype(
            bf16
        )
    val[...] = full[:, (q_heads + k_heads) * head :].astype(bf16)


def row_block(rows, columns, first=0):
    return pl.BlockSpec((rows, columns), lambda i: (i + first, 0))


def fixed_block(rows, columns):
    return pl.BlockSpec((rows, columns), lambda i: (0, 0))


def once_block(rows, columns):
    return pl.BlockSpec((rows, columns), lambda i: (0, 0), pipeline_mode=pl.Buffered(1))


def project(tok, gain, weight, cosine, sine, gains, q_heads, k_heads):
    count = len(tok)
    block, width = tok[0].shape
    total = block * count
    head = cosine.shape[1]
    qk = (q_heads + k_heads) * head
    kv = k_heads * head
    return pl.pallas_call(
        functools.partial(project_kernel, q_heads, k_heads, count),
        grid=(count,),
        in_specs=[
            fixed_block(1, width),
            fixed_block(*weight.shape),
            row_block(block, head),
            row_block(block, head),
            fixed_block(2, head),
        ]
        + [fixed_block(block, width)] * count,
        out_specs=[row_block(block, n) for n in (width, qk, qk, kv)],
        out_shape=[
            jax.ShapeDtypeStruct((total, width), bf16),
            jax.ShapeDtypeStruct((total, qk), f32),
            jax.ShapeDtypeStruct((total, qk), bf16),
            jax.ShapeDtypeStruct((total, kv), bf16),
        ],
        scratch_shapes=[pltpu.VMEM((block, width), bf16)],
        compiler_params=params(vmem_wide),
        cost_estimate=cost(2 * total * weight.size, 2 * weight.size + total * width * 12),
    )(gain, weight, cosine, sine, gains, *tok)


def allowed_pairs(j, k, start_q, start_k, block, seg_col, seg_row):
    own = seg_col[pl.ds(start_q, block), :]
    other = seg_row[:, pl.ds(start_k, block)]
    allowed = own == other
    if j == k:
        at_q = lax.broadcasted_iota(jnp.int32, (block, block), 0)
        at_k = lax.broadcasted_iota(jnp.int32, (block, block), 1)
        allowed = allowed & (at_q >= at_k)
    return allowed


def attend_kernel(blocks, group, factor, order, query, key, val, seg_col, seg_row, out, low, logs):
    total, head = key.shape
    block = total // blocks
    flip = order[0]
    start = [pl.multiple_of((jnp.int32(i) ^ flip) * block, block) for i in range(blocks)]
    ones = jnp.ones((block, head), bf16)
    for j in range(blocks):
        stacked = jnp.concatenate(
            [query[pl.ds(start[j], block), h * head : (h + 1) * head] for h in range(group)], axis=0
        )
        acc = jnp.zeros((group * block, 2 * head), f32)
        for k in range(j + 1):
            raw = dot_nt(stacked, key[pl.ds(start[k], block), :])
            allowed = allowed_pairs(j, k, start[j], start[k], block, seg_col, seg_row)
            allowed = jnp.concatenate([allowed] * group, axis=0)
            probs = jnp.where(allowed, jnp.exp2(raw * factor), 0.0).astype(bf16)
            both = jnp.concatenate([val[pl.ds(start[k], block), :], ones], axis=1)
            acc = acc + dot(probs, both)
        sums = acc[:, head:]
        result = acc[:, :head] / sums
        log_sums = jnp.log2(sums)
        for h in range(group):
            out[pl.ds(start[j], block), h * head : (h + 1) * head] = result[
                h * block : (h + 1) * block
            ]
            low[pl.ds(start[j], block), h * head : (h + 1) * head] = result[
                h * block : (h + 1) * block
            ].astype(bf16)
            logs[pl.ds(start[j], block), h * head : (h + 1) * head] = log_sums[
                h * block : (h + 1) * block
            ]


def attend(order, rot, val, seg_col, seg_row, q_heads, k_heads, head, blocks):
    total = rot.shape[0]
    group = q_heads // k_heads
    factor = head**-0.5 * math.log2(math.e)
    wide = pl.BlockSpec((total, group * head), lambda g, o: (0, g))
    return pl.pallas_call(
        functools.partial(attend_kernel, blocks, group, factor),
        grid_spec=pltpu.PrefetchScalarGridSpec(
            num_scalar_prefetch=1,
            grid=(k_heads,),
            in_specs=[
                wide,
                pl.BlockSpec((total, head), lambda g, o: (0, q_heads + g)),
                pl.BlockSpec((total, head), lambda g, o: (0, g)),
                pl.BlockSpec((total, 1), lambda g, o: (0, 0)),
                pl.BlockSpec((1, total), lambda g, o: (0, 0)),
            ],
            out_specs=[wide, wide, wide],
        ),
        out_shape=[jax.ShapeDtypeStruct((total, q_heads * head), kind) for kind in (f32, bf16, f32)],
        compiler_params=params(),
        cost_estimate=cost(4 * total * total * q_heads * head, total * q_heads * head * 12),
    )(order, rot, rot, val, seg_col, seg_row)


def attend_back_kernel(
    blocks, group, factor, scale, order, query, key, val, out_grad, out, logs, seg_col, seg_row,
    query_grad, key_grad, val_grad,
):
    total, head = key.shape
    block = total // blocks
    flip = order[0]
    start = [pl.multiple_of((jnp.int32(i) ^ flip) * block, block) for i in range(blocks)]

    def heads_of(ref, at):
        return jnp.concatenate(
            [ref[pl.ds(at, block), h * head : (h + 1) * head] for h in range(group)], axis=0
        )

    deltas = []
    for j in range(blocks):
        product = heads_of(out_grad, start[j]).astype(f32) * heads_of(out, start[j])
        deltas.append(jnp.sum(product, axis=1, keepdims=True))
    sums = [None] * blocks
    for k in range(blocks):
        key_block = key[pl.ds(start[k], block), :]
        val_block = val[pl.ds(start[k], block), :]
        key_sum = jnp.zeros((block, head), f32)
        val_sum = jnp.zeros((block, head), f32)
        for j in range(k, blocks):
            stacked = heads_of(query, start[j])
            grads = heads_of(out_grad, start[j])
            logged = heads_of(logs, start[j])
            logged = jnp.concatenate([logged] * (block // head), axis=1)
            raw = dot_nt(stacked, key_block)
            allowed = allowed_pairs(j, k, start[j], start[k], block, seg_col, seg_row)
            allowed = jnp.concatenate([allowed] * group, axis=0)
            probs = jnp.where(allowed, jnp.exp2(raw * factor - logged), 0.0)
            prob_grad = dot_nt(grads, val_block)
            score_grad = (probs * (prob_grad - deltas[j]) * scale).astype(bf16)
            val_sum = val_sum + dot_tn(probs.astype(bf16), grads)
            key_sum = key_sum + dot_tn(score_grad, stacked)
            piece = dot(score_grad, key_block)
            sums[j] = piece if k == 0 else sums[j] + piece
        key_grad[pl.ds(start[k], block), :] = key_sum
        val_grad[pl.ds(start[k], block), :] = val_sum
        for h in range(group):
            query_grad[pl.ds(start[k], block), h * head : (h + 1) * head] = sums[k][
                h * block : (h + 1) * block
            ]


def attend_back(order, rot, val, out_grad, out, logs, seg_col, seg_row, q_heads, k_heads, head, blocks):
    total = rot.shape[0]
    group = q_heads // k_heads
    scale = head**-0.5
    wide = pl.BlockSpec((total, group * head), lambda g, o: (0, g))
    thin = pl.BlockSpec((total, head), lambda g, o: (0, g))
    return pl.pallas_call(
        functools.partial(attend_back_kernel, blocks, group, scale * math.log2(math.e), scale),
        grid_spec=pltpu.PrefetchScalarGridSpec(
            num_scalar_prefetch=1,
            grid=(k_heads,),
            in_specs=[
                wide,
                pl.BlockSpec((total, head), lambda g, o: (0, q_heads + g)),
                thin,
                wide,
                wide,
                wide,
                pl.BlockSpec((total, 1), lambda g, o: (0, 0)),
                pl.BlockSpec((1, total), lambda g, o: (0, 0)),
            ],
            out_specs=[wide, thin, thin],
        ),
        out_shape=[
            jax.ShapeDtypeStruct((total, q_heads * head), f32),
            jax.ShapeDtypeStruct((total, k_heads * head), f32),
            jax.ShapeDtypeStruct((total, k_heads * head), f32),
        ],
        compiler_params=params(),
        cost_estimate=cost(10 * total * total * q_heads * head, total * q_heads * head * 20),
    )(order, rot, rot, val, out_grad, out, logs, seg_col, seg_row)


def feed_kernel(count, kept, weight, down, *refs):
    norm, cot = refs[:count], refs[count : 2 * count]
    hidden, gate_out, up_out, norm_all, cot_all, out, *norm_grad, low_held, cot_held = refs[
        2 * count + kept :
    ]
    pick(norm, low_held)
    pick(cot, cot_held)
    units = down.shape[0]
    low = low_held[...]
    norm_all[...] = low
    cot_all[...] = cot_held[...]
    gate = dot(low, weight[:, :units])
    upper = dot(low, weight[:, units:])
    sigma = 1.0 / (1.0 + jnp.exp(-gate))
    silu = gate * sigma
    hid = (silu * upper).astype(bf16)
    hidden[...] = hid
    back = dot_nt(cot_held[...], down[...])
    gate_grad = (back * upper * sigma * (1.0 + gate * (1.0 - sigma))).astype(bf16)
    up_grad = (back * silu).astype(bf16)
    gate_out[...] = gate_grad
    up_out[...] = up_grad
    back_low = (
        dot_nt(gate_grad, weight[:, :units]) + dot_nt(up_grad, weight[:, units:])
    ).astype(bf16)
    for k, ref in enumerate(norm_grad):

        @pl.when(pl.program_id(0) == k // 2)
        def _(k=k, ref=ref):
            rows = ref.shape[0]
            ref[...] = back_low[(k % 2) * rows : (k % 2 + 1) * rows]

    out[...] = dot(hid, down[...]).astype(bf16)


def feed(norm, cot, weight, down, first, blocks, before):
    count = len(norm)
    block, width = norm[0].shape
    total = block * blocks
    tall = 2 * block
    units = down.shape[0]
    kept = [units, units, units, width, width]
    return pl.pallas_call(
        functools.partial(feed_kernel, count, len(before)),
        grid=(count // 2,),
        in_specs=[once_block(*weight.shape), once_block(*down.shape)]
        + [once_block(block, width)] * (2 * count)
        + [pl.BlockSpec(memory_space=pl.ANY)] * len(before),
        out_specs=[row_block(tall, n, first) for n in kept] + [row_block(tall, width)]
        + [fixed_block(block, width)] * count,
        out_shape=[jax.ShapeDtypeStruct((total, n), bf16) for n in kept]
        + [jax.ShapeDtypeStruct((block * count, width), bf16)]
        + [jax.ShapeDtypeStruct((block, width), bf16)] * count,
        scratch_shapes=[pltpu.VMEM((tall, width), bf16)] * 2,
        input_output_aliases={2 + 2 * count + i: i for i in range(len(before))},
        compiler_params=params(vmem_feed),
        cost_estimate=cost(
            12 * block * count * down.size, 6 * down.size + block * count * width * 16,
            block * count * units,
        ),
    )(weight, down, *norm, *cot, *before)


def branch_kernel(count, weight, *refs):
    branch, (out_grad, branch_all, held) = refs[:count], refs[count:]
    pick(branch, held)
    low = held[...]
    branch_all[...] = low
    out_grad[...] = dot_nt(low, weight[...]).astype(bf16)


def branch_back(branch, weight):
    count = len(branch)
    block, width = branch[0].shape
    total = block * count
    return pl.pallas_call(
        functools.partial(branch_kernel, count),
        grid=(count,),
        in_specs=[fixed_block(*weight.shape)] + [fixed_block(block, width)] * count,
        out_specs=[row_block(block, weight.shape[0]), row_block(block, width)],
        out_shape=[
            jax.ShapeDtypeStruct((total, weight.shape[0]), bf16),
            jax.ShapeDtypeStruct((total, width), bf16),
        ],
        scratch_shapes=[pltpu.VMEM((block, width), bf16)],
        compiler_params=params(),
        cost_estimate=cost(2 * total * weight.size, 2 * weight.size + total * width * 6),
    )(weight, *branch)


def unproject_kernel(
    q_heads, k_heads, count, query_grad, key_grad, val_grad, lin, cosine, sine, gains, weight, *refs
):
    tok, (query_out, pair_out, norm_grad, gain_sum, head_sum, held) = refs[:count], refs[count:]
    pick(tok, held)
    head = cosine.shape[1]
    cos_, sin_ = cosine[...], sine[...]
    sums = [jnp.zeros((1, head), f32), jnp.zeros((1, head), f32)]
    for index in range(q_heads + k_heads):
        which = 0 if index < q_heads else 1
        ref, result, spot = (
            (query_grad, query_out, index) if which == 0 else (key_grad, pair_out, index - q_heads)
        )
        turned = ref[:, spot * head : (spot + 1) * head]
        grad = turned * cos_ - half_turn(turned) * sin_
        rows = lin[:, index * head : (index + 1) * head]
        scale = inverse_root(rows)
        sums[which] = sums[which] + jnp.sum(grad * rows * scale, axis=0, keepdims=True)
        result[:, spot * head : (spot + 1) * head] = norm_back(
            grad * gains[which : which + 1, :], rows, scale
        ).astype(bf16)
    pair_out[:, k_heads * head :] = val_grad[...].astype(bf16)
    normed_grad = dot_nt(query_out[...], weight[:, : q_heads * head]) + dot_nt(
        pair_out[...], weight[:, q_heads * head :]
    )
    norm_grad[...] = normed_grad.astype(bf16)
    rows = held[...].astype(f32)
    gain_part = jnp.sum(normed_grad * rows * inverse_root(rows), axis=0, keepdims=True)

    @pl.when(pl.program_id(0) == 0)
    def _():
        gain_sum[...] = jnp.zeros_like(gain_sum)
        head_sum[...] = jnp.zeros_like(head_sum)

    gain_sum[...] += gain_part
    head_sum[...] += jnp.concatenate(sums, axis=0)


def unproject(query_grad, key_grad, val_grad, lin, cosine, sine, gains, weight, tok, q_heads, k_heads):
    count = len(tok)
    block, width = tok[0].shape
    total = block * count
    head = cosine.shape[1]
    q_width, kv_width = q_heads * head, 2 * k_heads * head
    return pl.pallas_call(
        functools.partial(unproject_kernel, q_heads, k_heads, count),
        grid=(count,),
        in_specs=[
            row_block(block, q_width),
            row_block(block, k_heads * head),
            row_block(block, k_heads * head),
            row_block(block, (q_heads + k_heads) * head),
            row_block(block, head),
            row_block(block, head),
            fixed_block(2, head),
            fixed_block(*weight.shape),
        ]
        + [fixed_block(block, width)] * count,
        out_specs=[
            row_block(block, q_width), row_block(block, kv_width), row_block(block, width),
            fixed_block(1, width), fixed_block(2, head),
        ],
        out_shape=[
            jax.ShapeDtypeStruct((total, q_width), bf16),
            jax.ShapeDtypeStruct((total, kv_width), bf16),
            jax.ShapeDtypeStruct((total, width), bf16),
            jax.ShapeDtypeStruct((1, width), f32),
            jax.ShapeDtypeStruct((2, head), f32),
        ],
        scratch_shapes=[pltpu.VMEM((block, width), bf16)],
        compiler_params=params(),
        cost_estimate=cost(2 * total * weight.size, 2 * weight.size + total * width * 16),
    )(query_grad, key_grad, val_grad, lin, cosine, sine, gains, weight, *tok)


def place_kernel(count, outs, moves, scalars, *refs):
    inputs, results = refs[:count], refs[count:]
    values = [scalars[i] for i in range(scalars.shape[0])]
    for source, index, rows, columns, target, spot in moves:
        piece = inputs[source][index + (slice(rows[0], rows[1]), slice(columns[0], columns[1]))]
        row, column = spot(*values)
        results[target][
            pl.ds(pl.multiple_of(row, 16), rows[1] - rows[0]),
            pl.ds(pl.multiple_of(column, 128), columns[1] - columns[0]),
        ] = piece.astype(results[target].dtype)


def place(scalars, inputs, out_shapes, moves):
    moved = sum(item.size * 2 for item in inputs) + sum(
        math.prod(shape) * (4 if kind == f32 else 2) for shape, kind in out_shapes
    )
    whole = pl.BlockSpec(memory_space=pltpu.VMEM)
    return pl.pallas_call(
        functools.partial(place_kernel, len(inputs), len(out_shapes), moves),
        in_specs=[pl.BlockSpec(memory_space=pltpu.SMEM)] + [whole] * len(inputs),
        out_specs=[whole] * len(out_shapes),
        out_shape=[jax.ShapeDtypeStruct(shape, kind) for shape, kind in out_shapes],
        compiler_params=params(),
        cost_estimate=cost(0, moved),
    )(scalars, *inputs)


def cut_kernel(sizes, which, scalars, *refs):
    inputs, (own, near, piece) = refs[: len(sizes)], refs[len(sizes) :]
    mine, part = scalars[0], scalars[which]
    half = piece.shape[1]
    begin = 0
    for ref, size in zip(inputs, sizes):
        lanes = lambda i: pl.ds(pl.multiple_of((mine ^ i) * size, 128), size)
        rows = pl.ds(pl.multiple_of(part * half, 16), half)
        own[:, begin : begin + size] = ref[:, lanes(0)]
        near[:, begin : begin + size] = ref[:, lanes(1)]
        piece[0, :, begin : begin + size] = ref[rows, lanes(2)]
        piece[1, :, begin : begin + size] = ref[rows, lanes(3)]
        begin += size


def cut(scalars, inputs, sizes, parts):
    rows = inputs[0].shape[0]
    wide = sum(sizes)
    whole = pl.BlockSpec(memory_space=pltpu.VMEM)
    shapes = [(rows, wide), (rows, wide), (2, rows // parts, wide)]
    return pl.pallas_call(
        functools.partial(cut_kernel, sizes, parts // 2 if parts == 2 else 3),
        in_specs=[pl.BlockSpec(memory_space=pltpu.SMEM)] + [whole] * len(inputs),
        out_specs=[whole] * 3,
        out_shape=[jax.ShapeDtypeStruct(shape, bf16) for shape in shapes],
        compiler_params=params(),
        cost_estimate=cost(0, 4 * sum(item.size for item in inputs)),
    )(scalars, *inputs)


def ring_kernel(layout, plan, count, sets, chunks, *refs):
    local = [refs[i * count : (i + 1) * count] for i in range(sets)]
    arrived = refs[sets * count : len(refs) - len(plan)]
    results = refs[len(refs) - len(plan) :]
    for result, (which, halves, adds) in zip(results, plan):
        for source, block, lane, size, to_block, to_lane in layout:
            for at, half in enumerate(halves):
                value = local[which][source][block, 0, half, :, lane : lane + size].astype(f32)
                for index, held in adds:
                    if half in held:
                        value = value + arrived[index][
                            to_block, held.index(half), :, to_lane : to_lane + size
                        ].astype(f32)
                result[to_block, at, :, to_lane : to_lane + size] = value.astype(bf16)


def ring_step(shares, layout, blocks, chunks, plan, arrived):
    lines, lanes = shares[0].shape[3], blocks[1]
    specs = []
    for which in range(len(chunks)):
        for share in shares:
            shape = (share.shape[0], 1) + share.shape[2:]
            specs.append(
                pl.BlockSpec(shape, lambda i, c, which=which: (0, c[which], 0, 0, 0))
            )
    whole = lambda shape: pl.BlockSpec(shape, lambda i, c: (0,) * len(shape))
    shapes = [(blocks[0], len(halves), lines, lanes) for _, halves, _ in plan]
    return pl.pallas_call(
        functools.partial(ring_kernel, layout, plan, len(shares), len(chunks)),
        grid_spec=pltpu.PrefetchScalarGridSpec(
            num_scalar_prefetch=1,
            grid=(1,),
            in_specs=specs + [whole(item.shape) for item in arrived],
            out_specs=[whole(shape) for shape in shapes],
        ),
        out_shape=[jax.ShapeDtypeStruct(shape, bf16) for shape in shapes],
        compiler_params=params(),
        cost_estimate=cost(0, 6 * sum(math.prod(shape) for shape in shapes)),
    )(jnp.stack(chunks).astype(jnp.int32), *shares * len(chunks), *arrived)


def split_kernel(pieces, scalars, chunk, own, near, far):
    mine = scalars[0]
    for i, (result, spot) in enumerate([(own, 0), (near, 0), (far, 0), (near, 1)]):
        begin = 0
        for block, lane, size in pieces(mine ^ i):
            result[spot, :, :, begin : begin + size] = chunk[
                block, :, :, pl.ds(pl.multiple_of(lane, 128), size)
            ]
            begin += size


def split(scalars, chunk, pieces, wide):
    whole = pl.BlockSpec(memory_space=pltpu.VMEM)
    lines = chunk.shape[1:3]
    shapes = [(1, *lines, wide), (2, *lines, wide), (1, *lines, wide)]
    return pl.pallas_call(
        functools.partial(split_kernel, pieces),
        in_specs=[pl.BlockSpec(memory_space=pltpu.SMEM), whole],
        out_specs=[whole] * 3,
        out_shape=[jax.ShapeDtypeStruct(shape, bf16) for shape in shapes],
        compiler_params=params(),
        cost_estimate=cost(0, 4 * chunk.size),
    )(scalars, chunk)


def pack_kernel(layout, *refs):
    inputs, result = refs[:-1], refs[-1]
    for source, block, lane, size, to_block, to_lane in layout:
        result[to_block, :, :, to_lane : to_lane + size] = inputs[source][
            block, :, :, lane : lane + size
        ]


def pack(inputs, layout, shape):
    whole = pl.BlockSpec(memory_space=pltpu.VMEM)
    return pl.pallas_call(
        functools.partial(pack_kernel, layout),
        in_specs=[whole] * len(inputs),
        out_specs=whole,
        out_shape=jax.ShapeDtypeStruct(shape, bf16),
        compiler_params=params(),
        cost_estimate=cost(0, 4 * math.prod(shape)),
    )(*inputs)


class Moves:
    def __init__(self):
        self.shards = lax.axis_size("shard")
        self.reps = lax.axis_size("rep")
        self.mine = lax.axis_index("shard")
        self.direct = self.shards == 4 and self.reps == 8
        self.flip = self.mine if self.direct else jnp.int32(0)
        rep = lax.axis_index("rep")
        self.bits = {1: rep % 2, 2: (rep // 2) % 2, 4: rep // 4}
        self.pos = jnp.where(rep % 2 == 0, rep // 2, 7 - rep // 2)
        self.ring = [0, 2, 4, 6, 7, 5, 3, 1]
        self.quarter = self.bits[1] * 2 + self.bits[2]
        self.scalars = jnp.stack([self.mine, self.bits[1], self.pos, self.quarter]).astype(jnp.int32)

    def up(self, item):
        ring = self.ring
        return lax.ppermute(item, "rep", [(ring[i], ring[(i + 1) % 8]) for i in range(8)])

    def down(self, item):
        ring = self.ring
        return lax.ppermute(item, "rep", [(ring[(i + 1) % 8], ring[i]) for i in range(8)])

    def swap(self, item, mask):
        return lax.ppermute(item, "shard", [(i, i ^ mask) for i in range(4)])

    def cross_rep(self, item, mask):
        return lax.ppermute(item, "rep", [(i, i ^ mask) for i in range(8)])

    def gather(self, item):
        if not self.direct:
            rows = item.shape[0]
            whole = lax.all_gather(item, "shard", axis=0, tiled=True)
            return [whole[i * rows : (i + 1) * rows] for i in range(self.shards)]
        far = self.swap(item, 2)
        near = self.swap(item, 1)
        cross = self.swap(far, 1)
        return [item, near, far, cross]

    def scatter(self, near_part, far_part):
        if not self.direct:
            item = jnp.concatenate([near_part, far_part], axis=0).astype(f32)
            return lax.psum_scatter(item, "shard", scatter_dimension=0, tiled=True)
        rows = near_part.shape[0] // 2
        far = self.swap(far_part[:rows] + self.swap(far_part[rows:], 1), 2)
        near = self.swap(near_part[rows:], 1)
        return near_part[:rows].astype(f32) + near.astype(f32) + far.astype(f32)

    def ring_scatter(self, shares, layout, blocks):
        return RingSum(self, shares, layout, blocks)

    def ring_gather(self, item, *before):
        u1, d1 = self.up(item), self.down(item)
        u2, d2 = self.up(u1), self.down(d1)
        u3, d3 = self.up(u2), self.down(d2)
        last = after(u3, *before) if before else u3
        u4, d4 = self.up(last[:, :1]), self.down(d3[:, 1:])
        return [
            (item, 0, None), (u1, -1, None), (d1, 1, None), (u2, -2, None), (d2, 2, None),
            (u3, -3, None), (d3, 3, None), (u4, 4, 0), (d4, 4, 1),
        ]

    def exchange(self, chunk, pieces, wide):
        own, near, far = split(self.scalars, chunk, pieces, wide)
        near = self.swap(near, 1)
        far = self.swap(jnp.concatenate([far, near[1:]], axis=0), 2)
        return own, near, far


class RingSum:
    def __init__(self, moves, shares, layout, blocks):
        self.moves = moves
        self.step = functools.partial(ring_step, shares, layout, blocks)
        self.send(*self.step([self.chunk(4)], [(0, (0,), []), (0, (1,), [])], []))
        self.at = 4

    def chunk(self, offset):
        return (self.moves.pos + offset) % 8

    def send(self, u, d):
        self.sent = u
        self.arrived = [self.moves.up(u), self.moves.down(d)]

    def advance(self, *before):
        self.at -= 1
        both = (0, 1)
        u, d = self.arrived
        u = after(u, *before) if before else u
        held = [(0,), (1,)] if self.at == 3 else [both, both]
        plan = [(0, both, [(0, held[0])]), (1, both, [(1, held[1])])]
        self.send(*self.step([self.chunk(self.at), self.chunk(8 - self.at)], plan, [u, d]))

    def finish(self, *before):
        both = (0, 1)
        u, d = self.arrived
        u = after(u, *before) if before else u
        return self.step([self.chunk(0)], [(0, both, [(0, both), (1, both)])], [u, d])[0]


class Fetch:
    def __init__(self, moves, own, near, piece, spot, shape):
        self.moves, self.own, self.near, self.piece = moves, own, near, piece
        self.spot, self.shape = spot, shape

    def start(self, *before):
        self.here = self.moves.swap(after(self.piece, *before), 2)
        self.there = self.moves.cross_rep(self.here, 1)

    def finish(self):
        moves, here, there, spot = self.moves, self.here, self.there, self.spot
        rows, width = self.own.shape
        half = rows // 2
        near = moves.swap(self.near, 1)
        inputs = [self.own, near, here, moves.swap(here[1], 1), there, moves.swap(there[1], 1)]
        todo = [
            (0, (), (0, rows), (0, width), 0, lambda shard, *_: spot(shard, 0)),
            (1, (), (0, rows), (0, width), 0, lambda shard, *_: spot(shard ^ 1, 0)),
            (2, (0,), (0, half), (0, width), 0, lambda shard, y, *_: spot(shard ^ 2, y * half)),
            (3, (), (0, half), (0, width), 0, lambda shard, y, *_: spot(shard ^ 3, y * half)),
            (4, (0,), (0, half), (0, width), 0, lambda shard, y, *_: spot(shard ^ 2, (1 - y) * half)),
            (5, (), (0, half), (0, width), 0, lambda shard, y, *_: spot(shard ^ 3, (1 - y) * half)),
        ]
        return place(moves.scalars, inputs, [(self.shape, bf16)], todo)[0]


class DeepFetch(Fetch):
    def start(self, *before):
        moves = self.moves
        self.here = moves.swap(after(self.piece, *before), 2)
        pair = jnp.concatenate([self.here, moves.cross_rep(self.here, 1)], axis=0)
        self.parts = [pair, moves.cross_rep(pair, 2)]

    def finish(self):
        moves, spot = self.moves, self.spot
        first, second = self.parts
        rows, width = self.own.shape
        size = rows // 4
        cross = moves.swap(jnp.stack([first[1], first[3], second[1], second[3]]), 1)
        inputs = [self.own, moves.swap(self.near, 1), first, second, cross]
        todo = [
            (0, (), (0, rows), (0, width), 0, lambda shard, *_: spot(shard, 0)),
            (1, (), (0, rows), (0, width), 0, lambda shard, *_: spot(shard ^ 1, 0)),
        ]
        for i, (source, index, mask) in enumerate([(2, 0, 0), (2, 2, 2), (3, 0, 1), (3, 2, 3)]):
            for which, where, at in ((2, source, index), (3, 4, i)):

                def to(shard, y, pos, quarter, which=which, mask=mask):
                    return spot(shard ^ which, (quarter ^ mask) * size)

                todo.append((where, (at,), (0, size), (0, width), 0, to))
        return place(moves.scalars, inputs, [(self.shape, bf16)], todo)[0]


def after(item, *others):
    return lax.optimization_barrier((item, *others))[0]


def per_device(
    tokens, segments, grad_out, attention_gain, query_weight, key_matrix, value_matrix, query_gain,
    key_gain, output_weight, mlp_gain, gate_weight, up_weight, down_weight,
):
    moves = Moves()
    shards, mine, direct = moves.shards, moves.mine, moves.direct
    rows, width = tokens.shape[1:]
    total = rows * shards
    slice_width = attention_gain.shape[0]
    head_slice = query_gain.shape[0]
    head = head_slice * shards
    k_heads = key_matrix.shape[1] // head // shards
    q_heads = query_weight.shape[1] // head // shards
    q_width, k_width = q_heads * head, k_heads * head
    units = down_weight.shape[0]
    own_tokens = tokens[0]
    cot = grad_out[0]

    if direct:
        by_rows = lambda source, line: (source * slice_width + line, 0)
        qkv = Fetch(
            moves,
            *cut(moves.scalars, [query_weight, key_matrix, value_matrix], [q_width, k_width, k_width], 2),
            by_rows,
            (width, q_width + 2 * k_width),
        )
        qkv.start()
        attention_gain = after(attention_gain, qkv.piece)
    small = jnp.concatenate(
        [attention_gain, mlp_gain, query_gain, key_gain, segments[0].astype(bf16)]
    )[None]
    small = jnp.concatenate(moves.gather(small), axis=0)
    if direct:
        whole = jnp.where(mine % 2 == 0, small, small[jnp.array([1, 0, 3, 2])])
        whole = jnp.where(mine // 2 == 0, whole, whole[jnp.array([2, 3, 0, 1])])
    else:
        whole = small
    cuts = [slice_width, 2 * slice_width, 2 * slice_width + head_slice, 2 * slice_width + 2 * head_slice]
    input_gain = whole[:, : cuts[0]].reshape(1, width).astype(f32)
    second_gain = whole[:, cuts[0] : cuts[1]].reshape(1, width).astype(f32)
    head_gains = jnp.stack(
        [whole[:, cuts[1] : cuts[2]].reshape(head), whole[:, cuts[2] : cuts[3]].reshape(head)]
    ).astype(f32)
    segs = small[:, cuts[3] :].reshape(total).astype(f32)
    index = jnp.arange(shards, dtype=jnp.int32) ^ moves.flip
    places = (index[:, None] * rows + jnp.arange(rows, dtype=jnp.int32)[None]).reshape(total)
    firsts = jnp.sum((segs < 0.5).astype(jnp.int32))
    seconds = jnp.sum((segs < 1.5).astype(jnp.int32))
    opening = jnp.where(segs < 0.5, 0, jnp.where(segs < 1.5, firsts, seconds))
    freqs = theta_base ** (-(jnp.arange(head // 2, dtype=f32) * 2.0) / head)
    angles = (places - opening).astype(f32)[:, None] * freqs
    cosine, sine = jnp.cos(angles), jnp.sin(angles)
    cosine = jnp.concatenate([cosine, cosine], axis=1)
    sine = jnp.concatenate([-sine, sine], axis=1)
    seg_col, seg_row = segs[:, None], segs[None, :]
    order = moves.flip.astype(jnp.int32)[None]

    all_tokens = all_cot = None
    if direct:
        outer = lambda i, begin, n: lax.dynamic_slice(
            output_weight, ((mine ^ i) * q_width + begin, 0), (n, slice_width)
        )
        half = q_width // 2
        output = Fetch(
            moves,
            outer(0, 0, q_width),
            outer(1, 0, q_width),
            jnp.stack([outer(2, moves.bits[1] * half, half), outer(3, moves.bits[1] * half, half)]),
            lambda source, line: (line, source * slice_width),
            (q_width, width),
        )
        both = DeepFetch(
            moves,
            *cut(moves.scalars, [gate_weight, up_weight], [units, units], 4),
            by_rows,
            (width, 2 * units),
        )
        all_tokens = moves.gather(after(own_tokens, qkv.here))
        output.start(all_tokens[2], qkv.there)
        qkv_weight = qkv.finish()
        both.start(output.here)
        out_weight = output.finish()
        all_cot = moves.gather(after(cot, both.here))
    else:
        spread = lambda item: lax.all_to_all(item, "shard", split_axis=1, concat_axis=0, tiled=True)
        qkv_weight = jnp.concatenate(
            [spread(query_weight), spread(key_matrix), spread(value_matrix)], axis=1
        )
        out_weight = lax.all_to_all(output_weight, "shard", split_axis=0, concat_axis=1, tiled=True)
        feed_weight = jnp.concatenate([spread(gate_weight), spread(up_weight)], axis=1)

    if not direct:
        all_tokens, all_cot = moves.gather(own_tokens), moves.gather(cot)
    normed_one, lin, rot, val = project(
        all_tokens, input_gain, qkv_weight, cosine, sine, head_gains, q_heads, k_heads
    )
    if direct:
        rot = after(rot, both.here)
    attended, attended_low, logs = attend(order, rot, val, seg_col, seg_row, q_heads, k_heads, head, shards)
    inputs = own_tokens.astype(f32)
    split = total // 2
    if direct:
        feed_weight = both.finish()
        attended_low = after(attended_low, all_cot[2])
    far_part = dot(attended_low[split:], out_weight).astype(bf16)
    near_part = dot(attended_low[:split], out_weight).astype(bf16)
    residual_one = inputs + moves.scatter(near_part, far_part)
    residual_scale = inverse_root(residual_one)
    normed_two = moves.gather((residual_one * residual_scale * second_gain).astype(bf16))

    hidden, gate_grad, up_grad, normed_two, all_cot, out_part, *norm_grad = feed(
        normed_two, all_cot, feed_weight, down_weight, 0, shards, []
    )
    if direct:
        crossed = norm_grad[2] + moves.swap(norm_grad[3], 1)
        hidden, gate_grad = after(hidden, crossed), after(gate_grad, crossed)
        up_grad = after(up_grad, crossed)
        near_grad = norm_grad[0].astype(f32) + moves.swap(norm_grad[1], 1).astype(f32)
        far_grad = moves.swap(crossed, 2)
    else:
        norm_grad = jnp.concatenate(norm_grad, axis=0)
        normed_grad_two = moves.scatter(norm_grad[:split], norm_grad[split:])
    share_down = dot_tn(hidden, all_cot).astype(bf16)
    share_gate = dot_tn(normed_two, gate_grad).astype(bf16)
    share_up = dot_tn(normed_two, up_grad).astype(bf16)
    if direct:
        lines = slice_width // 16
        rest = 2 * units - width
        as_chunks = lambda share: share.reshape(-1, 8, 2, lines, share.shape[1])
        spot_of = lambda values, offset: lax.rem(values[2] + (offset + 8), 8) * (2 * lines)

        downs = units // slice_width
        blocks = (6 + downs, width)
        layout = []
        for i in range(4):
            layout += [
                (0, i, 0, units, i, 0),
                (1, i, 0, width - units, i, units),
                (1, i, width - units, rest, 4 + i // 2, (i % 2) * rest),
            ]
        layout += [(2, b, 0, width, 6 + b, 0) for b in range(downs)]
        ring = moves.ring_scatter(
            [as_chunks(share_gate), as_chunks(share_up), as_chunks(share_down)], layout, blocks
        )
        normed_grad_two = near_grad + after(far_grad, ring.sent).astype(f32)
    mlp_gain_part = jnp.sum(normed_grad_two * residual_one * residual_scale, axis=0)
    residual_grad = cot.astype(f32) + norm_back(
        normed_grad_two * second_gain, residual_one, residual_scale
    )
    branch_low = residual_grad.astype(bf16)
    if direct:
        ring.advance(branch_low)
        far_branch = after(moves.swap(branch_low, 2), ring.sent)
        branch_grad = [
            branch_low, moves.swap(branch_low, 1), far_branch, moves.swap(far_branch, 1),
        ]
    else:
        branch_grad = moves.gather(branch_low)
    out_part = after(out_part, *branch_grad)
    layer_out = (residual_one + moves.scatter(out_part[:split], out_part[split:])).astype(bf16)

    out_grad, branch_grad = branch_back(branch_grad, out_weight)
    share_out = dot_tn(attended_low, branch_grad).astype(bf16)
    if direct:
        ring.advance(out_grad)
        out_grad = after(out_grad, ring.sent)
    query_grad, key_grad, val_grad = attend_back(
        order, rot, val, out_grad, attended, logs, seg_col, seg_row, q_heads, k_heads, head, shards
    )
    if direct:
        ring.advance(query_grad)
        query_grad = after(query_grad, ring.sent)
    query_lin_grad, pair_lin_grad, norm_one_part, gain_part, head_part = unproject(
        query_grad, key_grad, val_grad, lin, cosine, sine, head_gains, qkv_weight, all_tokens,
        q_heads, k_heads,
    )
    share_query = dot_tn(normed_one, query_lin_grad).astype(bf16)
    share_pair = dot_tn(normed_one, pair_lin_grad).astype(bf16)
    normed_grad_one = moves.scatter(norm_one_part[:split], norm_one_part[split:])
    grad_tokens = residual_grad + norm_back(normed_grad_one * input_gain, inputs, inverse_root(inputs))

    gains = jnp.concatenate([gain_part[0], mlp_gain_part, head_part.reshape(2 * head)])[None]
    if direct:
        gains = gains + moves.swap(gains, 1)
        gains = gains + moves.swap(gains, 2)
        for mask in (1, 2, 4):
            gains = gains + moves.cross_rep(gains, mask)
    else:
        gains = lax.psum(gains, ("shard", "rep"))
    gains = gains[0]

    def own_part(begin, size):
        return lax.dynamic_slice_in_dim(gains, begin + mine * size, size, 0)

    grad_attention_gain = own_part(0, slice_width)
    grad_mlp_gain = own_part(width, slice_width)
    grad_query_gain = own_part(2 * width, head_slice)
    grad_key_gain = own_part(2 * width + head, head_slice)

    if direct:
        chunk = ring.finish()
        own, near, far = moves.exchange(
            chunk, lambda at: [(at, 0, width), (4 + at // 2, (at % 2) * rest, rest)], 2 * units
        )
        layout = []
        for i, (source, index) in enumerate([(0, 0), (1, 0), (2, 0), (2, 1)]):
            layout += [
                (source, index, 0, width, i, 0),
                (source, index, width, rest, 4 + i // 2, (i % 2) * rest),
            ]
        layout += [(3, 6 + b, 0, width, 6 + b, 0) for b in range(downs)]
        parts = moves.ring_gather(
            pack([own, near, far, chunk], layout, (blocks[0], 2, lines, width))
        )
        todo = []
        for source, (part, offset, half) in enumerate(parts):
            for h in range(part.shape[1]):
                line = ((half or 0) + h) * lines
                for i in range(4):

                    def at(*values, i=i, line=line, offset=offset, begin=0):
                        return spot_of(values, offset) + line, (values[0] ^ i) * units + begin

                    first = width - units
                    todo += [
                        (source, (i, h), (0, lines), (0, units), 0, at),
                        (source, (i, h), (0, lines), (units, width), 1, at),
                        (
                            source, (4 + i // 2, h), (0, lines),
                            ((i % 2) * rest, (i % 2) * rest + rest), 1,
                            functools.partial(at, begin=first),
                        ),
                    ]
                for b in range(downs):

                    def at(*values, b=b, line=line, offset=offset):
                        return b * slice_width + spot_of(values, offset) + line, 0

                    todo.append((source, (6 + b, h), (0, lines), (0, width), 2, at))
        shapes = [((slice_width, units * 4), f32)] * 2 + [((units, width), f32)]
        grad_gate, grad_up, grad_down = place(
            moves.scalars, [part for part, _, _ in parts], shapes, todo
        )

        first_near, first_packed, first_last = near, parts[0][0], parts[-1][0]

        outs = q_width // slice_width
        pair = 2 * k_width
        wide = q_width + pair
        layout = []
        for i in range(4):
            layout += [(0, i, 0, q_width, i, 0), (1, i, 0, pair, i, q_width)]
        layout += [(2, b, 0, width, 4 + b, 0) for b in range(outs)]
        ring = moves.ring_scatter(
            [as_chunks(share_query), as_chunks(share_pair), as_chunks(share_out)],
            layout,
            (4 + outs, width),
        )
        ring.advance(first_near)
        ring.advance(first_packed)
        ring.advance()
        chunk = ring.finish()
        own, near, far = moves.exchange(
            chunk,
            lambda at: [(at, 0, wide)] + [(4 + b, at * slice_width, slice_width) for b in range(outs)],
            wide + outs * slice_width,
        )
        wide_all = wide + outs * slice_width
        layout = [
            (source, index, 0, wide_all, i, 0)
            for i, (source, index) in enumerate([(0, 0), (1, 0), (2, 0), (2, 1)])
        ]
        parts = moves.ring_gather(pack([own, near, far], layout, (4, 2, lines, wide_all)))
        todo = []
        for source, (part, offset, half) in enumerate(parts):
            for h in range(part.shape[1]):
                line = ((half or 0) + h) * lines
                for i in range(4):
                    begin = 0
                    for target, size in enumerate([q_width, k_width, k_width]):

                        def at(*values, i=i, line=line, offset=offset, size=size):
                            return spot_of(values, offset) + line, (values[0] ^ i) * size

                        todo.append((source, (i, h), (0, lines), (begin, begin + size), target, at))
                        begin += size
                    for b in range(outs):

                        def at(*values, i=i, b=b, line=line, offset=offset):
                            first = (values[0] ^ i) * q_width + b * slice_width
                            return first + spot_of(values, offset) + line, 0

                        todo.append(
                            (source, (i, h), (0, lines), (begin, begin + slice_width), 3, at)
                        )
                        begin += slice_width
        shapes = [((slice_width, size * 4), f32) for size in (q_width, k_width, k_width)]
        shapes.append(((q_width * 4, slice_width), f32))
        grad_query, grad_key, grad_value, grad_output = place(
            moves.scalars, [part for part, _, _ in parts], shapes, todo
        )
    else:

        def finish(share):
            part = lax.all_to_all(share, "shard", split_axis=0, concat_axis=1, tiled=True)
            return lax.psum(part, "rep").astype(f32)

        grad_down = lax.psum(share_down, "rep").astype(f32)
        grad_gate = finish(share_gate)
        grad_up = finish(share_up)
        grad_output = lax.psum(
            lax.all_to_all(share_out, "shard", split_axis=1, concat_axis=0, tiled=True), "rep"
        ).astype(f32)
        grad_query = finish(share_query)
        grad_key = finish(share_pair[:, :k_width])
        grad_value = finish(share_pair[:, k_width:])

    return (
        layer_out[None], grad_tokens[None], grad_attention_gain, grad_query, grad_key, grad_value,
        grad_query_gain, grad_key_gain, grad_output, grad_mlp_gain, grad_gate, grad_up, grad_down,
    )


def solution(mesh):
    rows_over = P("shard", None)
    return jax.shard_map(
        per_device,
        mesh=mesh,
        in_specs=(
            P("rep", "shard", None), P("rep", "shard"), P("rep", "shard", None), P("shard"), rows_over,
            rows_over, rows_over, P("shard"), P("shard"), P(None, "shard"), P("shard"), rows_over,
            rows_over, rows_over,
        ),
        out_specs=(
            P("rep", "shard", None), P("rep", "shard", None), P("shard"), rows_over, rows_over,
            rows_over, P("shard"), P("shard"), P(None, "shard"), P("shard"), rows_over, rows_over,
            rows_over,
        ),
        check_vma=False,
    )
```

```python
import functools
import math

import jax
import jax.numpy as jnp
from jax import lax
from jax.experimental import pallas as pl
from jax.experimental.pallas import tpu as pltpu
from jax.sharding import PartitionSpec as P

eps_norm = 1e-06
theta_base = 1000000.0
f32 = jnp.float32
bf16 = jnp.bfloat16
vmem_bytes = 24 * 1024 * 1024
vmem_wide = 42 * 1024 * 1024
vmem_feed = 48 * 1024 * 1024


def dot(left, right):
    return lax.dot_general(left, right, (((1,), (0,)), ((), ())), preferred_element_type=f32)


def dot_nt(left, right):
    return lax.dot_general(left, right, (((1,), (1,)), ((), ())), preferred_element_type=f32)


def dot_tn(left, right):
    return lax.dot_general(left, right, (((0,), (0,)), ((), ())), preferred_element_type=f32)


def inverse_root(rows):
    return lax.rsqrt(jnp.mean(rows * rows, axis=-1, keepdims=True) + eps_norm)


def norm_back(grad, rows, scale):
    return scale * grad - rows * (scale * scale * scale) * jnp.mean(
        grad * rows, axis=-1, keepdims=True
    )


def params(limit=vmem_bytes):
    return pltpu.CompilerParams(vmem_limit_bytes=limit)


def cost(flops, moved, trans=0):
    return pl.CostEstimate(flops=int(flops), bytes_accessed=int(moved), transcendentals=int(trans))


def half_turn(rows):
    return pltpu.roll(rows, rows.shape[-1] // 2, axis=1)


def pick(refs, held):
    rows = refs[0].shape[0]
    count = held.shape[0] // rows
    for k in range(len(refs) // count):

        @pl.when(pl.program_id(0) == k)
        def _(k=k):
            for i in range(count):
                held[i * rows : (i + 1) * rows, :] = refs[k * count + i][...]


def project_kernel(
    q_heads, k_heads, count, gain, weight, cosine, sine, gains, *refs
):
    tok, (normed, lin, rot, val, held) = refs[:count], refs[count:]
    pick(tok, held)
    rows = held[...].astype(f32)
    low = (rows * inverse_root(rows) * gain[...]).astype(bf16)
    normed[...] = low
    head = cosine.shape[1]
    full = dot(low, weight[...])
    cos_, sin_ = cosine[...], sine[...]
    for index in range(q_heads + k_heads):
        part = full[:, index * head : (index + 1) * head]
        lin[:, index * head : (index + 1) * head] = part.astype(bf16)
        which = 0 if index < q_heads else 1
        unit = part * inverse_root(part) * gains[which : which + 1, :]
        rot[:, index * head : (index + 1) * head] = (unit * cos_ + half_turn(unit) * sin_).astype(
            bf16
        )
    val[...] = full[:, (q_heads + k_heads) * head :].astype(bf16)


def row_block(rows, columns, first=0):
    return pl.BlockSpec((rows, columns), lambda i: (i + first, 0))


def fixed_block(rows, columns):
    return pl.BlockSpec((rows, columns), lambda i: (0, 0))


def once_block(rows, columns):
    return pl.BlockSpec((rows, columns), lambda i: (0, 0), pipeline_mode=pl.Buffered(1))


def project(tok, gain, weight, cosine, sine, gains, q_heads, k_heads):
    count = len(tok)
    block, width = tok[0].shape
    total = block * count
    head = cosine.shape[1]
    qk = (q_heads + k_heads) * head
    kv = k_heads * head
    return pl.pallas_call(
        functools.partial(project_kernel, q_heads, k_heads, count),
        grid=(count,),
        in_specs=[
            fixed_block(1, width),
            fixed_block(*weight.shape),
            row_block(block, head),
            row_block(block, head),
            fixed_block(2, head),
        ]
        + [fixed_block(block, width)] * count,
        out_specs=[row_block(block, n) for n in (width, qk, qk, kv)],
        out_shape=[
            jax.ShapeDtypeStruct((total, width), bf16),
            jax.ShapeDtypeStruct((total, qk), bf16),
            jax.ShapeDtypeStruct((total, qk), bf16),
            jax.ShapeDtypeStruct((total, kv), bf16),
        ],
        scratch_shapes=[pltpu.VMEM((block, width), bf16)],
        compiler_params=params(vmem_wide),
        cost_estimate=cost(2 * total * weight.size, 2 * weight.size + total * width * 12),
    )(gain, weight, cosine, sine, gains, *tok)


def allowed_pairs(j, k, start_q, start_k, block, seg_col, seg_row):
    own = seg_col[pl.ds(start_q, block), :]
    other = seg_row[:, pl.ds(start_k, block)]
    allowed = own == other
    if j == k:
        at_q = lax.broadcasted_iota(jnp.int32, (block, block), 0)
        at_k = lax.broadcasted_iota(jnp.int32, (block, block), 1)
        allowed = allowed & (at_q >= at_k)
    return allowed


def attend_kernel(blocks, group, factor, order, query, key, val, seg_col, seg_row, out, low, logs):
    total, head = key.shape
    block = total // blocks
    flip = order[0]
    start = [pl.multiple_of((jnp.int32(i) ^ flip) * block, block) for i in range(blocks)]
    ones = jnp.ones((block, head), bf16)
    for j in range(blocks):
        stacked = jnp.concatenate(
            [query[pl.ds(start[j], block), h * head : (h + 1) * head] for h in range(group)], axis=0
        )
        acc = jnp.zeros((group * block, 2 * head), f32)
        for k in range(j + 1):
            raw = dot_nt(stacked, key[pl.ds(start[k], block), :])
            allowed = allowed_pairs(j, k, start[j], start[k], block, seg_col, seg_row)
            allowed = jnp.concatenate([allowed] * group, axis=0)
            probs = jnp.where(allowed, jnp.exp2(raw * factor), 0.0).astype(bf16)
            both = jnp.concatenate([val[pl.ds(start[k], block), :], ones], axis=1)
            acc = acc + dot(probs, both)
        sums = acc[:, head:]
        result = acc[:, :head] / sums
        log_sums = jnp.log2(sums)
        for h in range(group):
            out[pl.ds(start[j], block), h * head : (h + 1) * head] = result[
                h * block : (h + 1) * block
            ]
            low[pl.ds(start[j], block), h * head : (h + 1) * head] = result[
                h * block : (h + 1) * block
            ].astype(bf16)
            logs[pl.ds(start[j], block), h * head : (h + 1) * head] = log_sums[
                h * block : (h + 1) * block
            ]


def attend(order, rot, val, seg_col, seg_row, q_heads, k_heads, head, blocks):
    total = rot.shape[0]
    group = q_heads // k_heads
    factor = head**-0.5 * math.log2(math.e)
    wide = pl.BlockSpec((total, group * head), lambda g, o: (0, g))
    return pl.pallas_call(
        functools.partial(attend_kernel, blocks, group, factor),
        grid_spec=pltpu.PrefetchScalarGridSpec(
            num_scalar_prefetch=1,
            grid=(k_heads,),
            in_specs=[
                wide,
                pl.BlockSpec((total, head), lambda g, o: (0, q_heads + g)),
                pl.BlockSpec((total, head), lambda g, o: (0, g)),
                pl.BlockSpec((total, 1), lambda g, o: (0, 0)),
                pl.BlockSpec((1, total), lambda g, o: (0, 0)),
            ],
            out_specs=[wide, wide, wide],
        ),
        out_shape=[jax.ShapeDtypeStruct((total, q_heads * head), kind) for kind in (f32, bf16, f32)],
        compiler_params=params(),
        cost_estimate=cost(4 * total * total * q_heads * head, total * q_heads * head * 12),
    )(order, rot, rot, val, seg_col, seg_row)


def attend_back_kernel(
    blocks, group, factor, scale, order, query, key, val, out_grad, out, logs, seg_col, seg_row,
    query_grad, key_grad, val_grad,
):
    total, head = key.shape
    block = total // blocks
    flip = order[0]
    start = [pl.multiple_of((jnp.int32(i) ^ flip) * block, block) for i in range(blocks)]

    def heads_of(ref, at):
        return jnp.concatenate(
            [ref[pl.ds(at, block), h * head : (h + 1) * head] for h in range(group)], axis=0
        )

    deltas = []
    for j in range(blocks):
        product = heads_of(out_grad, start[j]).astype(f32) * heads_of(out, start[j])
        deltas.append(jnp.sum(product, axis=1, keepdims=True))
    sums = [None] * blocks
    for k in range(blocks):
        key_block = key[pl.ds(start[k], block), :]
        val_block = val[pl.ds(start[k], block), :]
        key_sum = jnp.zeros((block, head), f32)
        val_sum = jnp.zeros((block, head), f32)
        for j in range(k, blocks):
            stacked = heads_of(query, start[j])
            grads = heads_of(out_grad, start[j])
            logged = heads_of(logs, start[j])
            logged = jnp.concatenate([logged] * (block // head), axis=1)
            raw = dot_nt(stacked, key_block)
            allowed = allowed_pairs(j, k, start[j], start[k], block, seg_col, seg_row)
            allowed = jnp.concatenate([allowed] * group, axis=0)
            probs = jnp.where(allowed, jnp.exp2(raw * factor - logged), 0.0)
            prob_grad = dot_nt(grads, val_block)
            score_grad = (probs * (prob_grad - deltas[j]) * scale).astype(bf16)
            val_sum = val_sum + dot_tn(probs.astype(bf16), grads)
            key_sum = key_sum + dot_tn(score_grad, stacked)
            piece = dot(score_grad, key_block)
            sums[j] = piece if k == 0 else sums[j] + piece
        key_grad[pl.ds(start[k], block), :] = key_sum
        val_grad[pl.ds(start[k], block), :] = val_sum
        for h in range(group):
            query_grad[pl.ds(start[k], block), h * head : (h + 1) * head] = sums[k][
                h * block : (h + 1) * block
            ]


def attend_back(order, rot, val, out_grad, out, logs, seg_col, seg_row, q_heads, k_heads, head, blocks):
    total = rot.shape[0]
    group = q_heads // k_heads
    scale = head**-0.5
    wide = pl.BlockSpec((total, group * head), lambda g, o: (0, g))
    thin = pl.BlockSpec((total, head), lambda g, o: (0, g))
    return pl.pallas_call(
        functools.partial(attend_back_kernel, blocks, group, scale * math.log2(math.e), scale),
        grid_spec=pltpu.PrefetchScalarGridSpec(
            num_scalar_prefetch=1,
            grid=(k_heads,),
            in_specs=[
                wide,
                pl.BlockSpec((total, head), lambda g, o: (0, q_heads + g)),
                thin,
                wide,
                wide,
                wide,
                pl.BlockSpec((total, 1), lambda g, o: (0, 0)),
                pl.BlockSpec((1, total), lambda g, o: (0, 0)),
            ],
            out_specs=[wide, thin, thin],
        ),
        out_shape=[
            jax.ShapeDtypeStruct((total, q_heads * head), f32),
            jax.ShapeDtypeStruct((total, k_heads * head), f32),
            jax.ShapeDtypeStruct((total, k_heads * head), f32),
        ],
        compiler_params=params(),
        cost_estimate=cost(10 * total * total * q_heads * head, total * q_heads * head * 20),
    )(order, rot, rot, val, out_grad, out, logs, seg_col, seg_row)


def feed_kernel(count, kept, weight, down, *refs):
    norm, cot = refs[:count], refs[count : 2 * count]
    hidden, gate_out, up_out, norm_all, cot_all, out, *norm_grad, low_held, cot_held = refs[
        2 * count + kept :
    ]
    pick(norm, low_held)
    pick(cot, cot_held)
    units = down.shape[0]
    low = low_held[...]
    norm_all[...] = low
    cot_all[...] = cot_held[...]
    gate = dot(low, weight[:, :units])
    upper = dot(low, weight[:, units:])
    sigma = 1.0 / (1.0 + jnp.exp(-gate))
    silu = gate * sigma
    hid = (silu * upper).astype(bf16)
    hidden[...] = hid
    back = dot_nt(cot_held[...], down[...])
    gate_grad = (back * upper * sigma * (1.0 + gate * (1.0 - sigma))).astype(bf16)
    up_grad = (back * silu).astype(bf16)
    gate_out[...] = gate_grad
    up_out[...] = up_grad
    back_low = (
        dot_nt(gate_grad, weight[:, :units]) + dot_nt(up_grad, weight[:, units:])
    ).astype(bf16)
    for k, ref in enumerate(norm_grad):

        @pl.when(pl.program_id(0) == k // 2)
        def _(k=k, ref=ref):
            rows = ref.shape[0]
            ref[...] = back_low[(k % 2) * rows : (k % 2 + 1) * rows]

    out[...] = dot(hid, down[...]).astype(bf16)


def feed(norm, cot, weight, down, first, blocks, before):
    count = len(norm)
    block, width = norm[0].shape
    total = block * blocks
    tall = 2 * block
    units = down.shape[0]
    kept = [units, units, units, width, width]
    return pl.pallas_call(
        functools.partial(feed_kernel, count, len(before)),
        grid=(count // 2,),
        in_specs=[once_block(*weight.shape), once_block(*down.shape)]
        + [once_block(block, width)] * (2 * count)
        + [pl.BlockSpec(memory_space=pl.ANY)] * len(before),
        out_specs=[row_block(tall, n, first) for n in kept] + [row_block(tall, width)]
        + [fixed_block(block, width)] * count,
        out_shape=[jax.ShapeDtypeStruct((total, n), bf16) for n in kept]
        + [jax.ShapeDtypeStruct((block * count, width), bf16)]
        + [jax.ShapeDtypeStruct((block, width), bf16)] * count,
        scratch_shapes=[pltpu.VMEM((tall, width), bf16)] * 2,
        input_output_aliases={2 + 2 * count + i: i for i in range(len(before))},
        compiler_params=params(vmem_feed),
        cost_estimate=cost(
            12 * block * count * down.size, 6 * down.size + block * count * width * 16,
            block * count * units,
        ),
    )(weight, down, *norm, *cot, *before)


def branch_kernel(count, weight, *refs):
    branch, (out_grad, branch_all, held) = refs[:count], refs[count:]
    pick(branch, held)
    low = held[...]
    branch_all[...] = low
    out_grad[...] = dot_nt(low, weight[...]).astype(bf16)


def branch_back(branch, weight):
    count = len(branch)
    block, width = branch[0].shape
    total = block * count
    return pl.pallas_call(
        functools.partial(branch_kernel, count),
        grid=(count,),
        in_specs=[fixed_block(*weight.shape)] + [fixed_block(block, width)] * count,
        out_specs=[row_block(block, weight.shape[0]), row_block(block, width)],
        out_shape=[
            jax.ShapeDtypeStruct((total, weight.shape[0]), bf16),
            jax.ShapeDtypeStruct((total, width), bf16),
        ],
        scratch_shapes=[pltpu.VMEM((block, width), bf16)],
        compiler_params=params(),
        cost_estimate=cost(2 * total * weight.size, 2 * weight.size + total * width * 6),
    )(weight, *branch)


def unproject_kernel(
    q_heads, k_heads, count, query_grad, key_grad, val_grad, lin, cosine, sine, gains, weight, *refs
):
    tok, (query_out, pair_out, norm_grad, gain_sum, head_sum, held) = refs[:count], refs[count:]
    pick(tok, held)
    head = cosine.shape[1]
    cos_, sin_ = cosine[...], sine[...]
    sums = [jnp.zeros((1, head), f32), jnp.zeros((1, head), f32)]
    for index in range(q_heads + k_heads):
        which = 0 if index < q_heads else 1
        ref, result, spot = (
            (query_grad, query_out, index) if which == 0 else (key_grad, pair_out, index - q_heads)
        )
        turned = ref[:, spot * head : (spot + 1) * head]
        grad = turned * cos_ - half_turn(turned) * sin_
        rows = lin[:, index * head : (index + 1) * head].astype(f32)
        scale = inverse_root(rows)
        sums[which] = sums[which] + jnp.sum(grad * rows * scale, axis=0, keepdims=True)
        result[:, spot * head : (spot + 1) * head] = norm_back(
            grad * gains[which : which + 1, :], rows, scale
        ).astype(bf16)
    pair_out[:, k_heads * head :] = val_grad[...].astype(bf16)
    normed_grad = dot_nt(query_out[...], weight[:, : q_heads * head]) + dot_nt(
        pair_out[...], weight[:, q_heads * head :]
    )
    norm_grad[...] = normed_grad.astype(bf16)
    rows = held[...].astype(f32)
    gain_part = jnp.sum(normed_grad * rows * inverse_root(rows), axis=0, keepdims=True)

    @pl.when(pl.program_id(0) == 0)
    def _():
        gain_sum[...] = jnp.zeros_like(gain_sum)
        head_sum[...] = jnp.zeros_like(head_sum)

    gain_sum[...] += gain_part
    head_sum[...] += jnp.concatenate(sums, axis=0)


def unproject(query_grad, key_grad, val_grad, lin, cosine, sine, gains, weight, tok, q_heads, k_heads):
    count = len(tok)
    block, width = tok[0].shape
    total = block * count
    head = cosine.shape[1]
    q_width, kv_width = q_heads * head, 2 * k_heads * head
    return pl.pallas_call(
        functools.partial(unproject_kernel, q_heads, k_heads, count),
        grid=(count,),
        in_specs=[
            row_block(block, q_width),
            row_block(block, k_heads * head),
            row_block(block, k_heads * head),
            row_block(block, (q_heads + k_heads) * head),
            row_block(block, head),
            row_block(block, head),
            fixed_block(2, head),
            fixed_block(*weight.shape),
        ]
        + [fixed_block(block, width)] * count,
        out_specs=[
            row_block(block, q_width), row_block(block, kv_width), row_block(block, width),
            fixed_block(1, width), fixed_block(2, head),
        ],
        out_shape=[
            jax.ShapeDtypeStruct((total, q_width), bf16),
            jax.ShapeDtypeStruct((total, kv_width), bf16),
            jax.ShapeDtypeStruct((total, width), bf16),
            jax.ShapeDtypeStruct((1, width), f32),
            jax.ShapeDtypeStruct((2, head), f32),
        ],
        scratch_shapes=[pltpu.VMEM((block, width), bf16)],
        compiler_params=params(),
        cost_estimate=cost(2 * total * weight.size, 2 * weight.size + total * width * 16),
    )(query_grad, key_grad, val_grad, lin, cosine, sine, gains, weight, *tok)


def place_kernel(count, outs, moves, scalars, *refs):
    inputs, results = refs[:count], refs[count:]
    values = [scalars[i] for i in range(scalars.shape[0])]
    for source, index, rows, columns, target, spot in moves:
        piece = inputs[source][index + (slice(rows[0], rows[1]), slice(columns[0], columns[1]))]
        row, column = spot(*values)
        results[target][
            pl.ds(pl.multiple_of(row, 16), rows[1] - rows[0]),
            pl.ds(pl.multiple_of(column, 128), columns[1] - columns[0]),
        ] = piece.astype(results[target].dtype)


def place(scalars, inputs, out_shapes, moves):
    moved = sum(item.size * 2 for item in inputs) + sum(
        math.prod(shape) * (4 if kind == f32 else 2) for shape, kind in out_shapes
    )
    whole = pl.BlockSpec(memory_space=pltpu.VMEM)
    return pl.pallas_call(
        functools.partial(place_kernel, len(inputs), len(out_shapes), moves),
        in_specs=[pl.BlockSpec(memory_space=pltpu.SMEM)] + [whole] * len(inputs),
        out_specs=[whole] * len(out_shapes),
        out_shape=[jax.ShapeDtypeStruct(shape, kind) for shape, kind in out_shapes],
        compiler_params=params(),
        cost_estimate=cost(0, moved),
    )(scalars, *inputs)


def cut_kernel(sizes, which, scalars, *refs):
    inputs, (own, near, piece) = refs[: len(sizes)], refs[len(sizes) :]
    mine, part = scalars[0], scalars[which]
    half = piece.shape[1]
    begin = 0
    for ref, size in zip(inputs, sizes):
        lanes = lambda i: pl.ds(pl.multiple_of((mine ^ i) * size, 128), size)
        rows = pl.ds(pl.multiple_of(part * half, 16), half)
        own[:, begin : begin + size] = ref[:, lanes(0)]
        near[:, begin : begin + size] = ref[:, lanes(1)]
        piece[0, :, begin : begin + size] = ref[rows, lanes(2)]
        piece[1, :, begin : begin + size] = ref[rows, lanes(3)]
        begin += size


def cut(scalars, inputs, sizes, parts):
    rows = inputs[0].shape[0]
    wide = sum(sizes)
    whole = pl.BlockSpec(memory_space=pltpu.VMEM)
    shapes = [(rows, wide), (rows, wide), (2, rows // parts, wide)]
    return pl.pallas_call(
        functools.partial(cut_kernel, sizes, parts // 2 if parts == 2 else 3),
        in_specs=[pl.BlockSpec(memory_space=pltpu.SMEM)] + [whole] * len(inputs),
        out_specs=[whole] * 3,
        out_shape=[jax.ShapeDtypeStruct(shape, bf16) for shape in shapes],
        compiler_params=params(),
        cost_estimate=cost(0, 4 * sum(item.size for item in inputs)),
    )(scalars, *inputs)


def ring_kernel(layout, plan, count, sets, chunks, *refs):
    local = [refs[i * count : (i + 1) * count] for i in range(sets)]
    arrived = refs[sets * count : len(refs) - len(plan)]
    results = refs[len(refs) - len(plan) :]
    for result, (which, halves, adds) in zip(results, plan):
        for source, block, lane, size, to_block, to_lane in layout:
            for at, half in enumerate(halves):
                value = local[which][source][block, 0, half, :, lane : lane + size].astype(f32)
                for index, held in adds:
                    if half in held:
                        value = value + arrived[index][
                            to_block, held.index(half), :, to_lane : to_lane + size
                        ].astype(f32)
                result[to_block, at, :, to_lane : to_lane + size] = value.astype(bf16)


def ring_step(shares, layout, blocks, chunks, plan, arrived):
    lines, lanes = shares[0].shape[3], blocks[1]
    specs = []
    for which in range(len(chunks)):
        for share in shares:
            shape = (share.shape[0], 1) + share.shape[2:]
            specs.append(
                pl.BlockSpec(shape, lambda i, c, which=which: (0, c[which], 0, 0, 0))
            )
    whole = lambda shape: pl.BlockSpec(shape, lambda i, c: (0,) * len(shape))
    shapes = [(blocks[0], len(halves), lines, lanes) for _, halves, _ in plan]
    return pl.pallas_call(
        functools.partial(ring_kernel, layout, plan, len(shares), len(chunks)),
        grid_spec=pltpu.PrefetchScalarGridSpec(
            num_scalar_prefetch=1,
            grid=(1,),
            in_specs=specs + [whole(item.shape) for item in arrived],
            out_specs=[whole(shape) for shape in shapes],
        ),
        out_shape=[jax.ShapeDtypeStruct(shape, bf16) for shape in shapes],
        compiler_params=params(),
        cost_estimate=cost(0, 6 * sum(math.prod(shape) for shape in shapes)),
    )(jnp.stack(chunks).astype(jnp.int32), *shares * len(chunks), *arrived)


def split_kernel(pieces, scalars, chunk, own, near, far):
    mine = scalars[0]
    for i, (result, spot) in enumerate([(own, 0), (near, 0), (far, 0), (near, 1)]):
        begin = 0
        for block, lane, size in pieces(mine ^ i):
            result[spot, :, :, begin : begin + size] = chunk[
                block, :, :, pl.ds(pl.multiple_of(lane, 128), size)
            ]
            begin += size


def split(scalars, chunk, pieces, wide):
    whole = pl.BlockSpec(memory_space=pltpu.VMEM)
    lines = chunk.shape[1:3]
    shapes = [(1, *lines, wide), (2, *lines, wide), (1, *lines, wide)]
    return pl.pallas_call(
        functools.partial(split_kernel, pieces),
        in_specs=[pl.BlockSpec(memory_space=pltpu.SMEM), whole],
        out_specs=[whole] * 3,
        out_shape=[jax.ShapeDtypeStruct(shape, bf16) for shape in shapes],
        compiler_params=params(),
        cost_estimate=cost(0, 4 * chunk.size),
    )(scalars, chunk)


def pack_kernel(layout, *refs):
    inputs, result = refs[:-1], refs[-1]
    for source, block, lane, size, to_block, to_lane in layout:
        result[to_block, :, :, to_lane : to_lane + size] = inputs[source][
            block, :, :, lane : lane + size
        ]


def pack(inputs, layout, shape):
    whole = pl.BlockSpec(memory_space=pltpu.VMEM)
    return pl.pallas_call(
        functools.partial(pack_kernel, layout),
        in_specs=[whole] * len(inputs),
        out_specs=whole,
        out_shape=jax.ShapeDtypeStruct(shape, bf16),
        compiler_params=params(),
        cost_estimate=cost(0, 4 * math.prod(shape)),
    )(*inputs)


class Moves:
    def __init__(self):
        self.shards = lax.axis_size("shard")
        self.reps = lax.axis_size("rep")
        self.mine = lax.axis_index("shard")
        self.direct = self.shards == 4 and self.reps == 8
        self.flip = self.mine if self.direct else jnp.int32(0)
        rep = lax.axis_index("rep")
        self.bits = {1: rep % 2, 2: (rep // 2) % 2, 4: rep // 4}
        self.pos = jnp.where(rep % 2 == 0, rep // 2, 7 - rep // 2)
        self.ring = [0, 2, 4, 6, 7, 5, 3, 1]
        self.quarter = self.bits[1] * 2 + self.bits[2]
        self.scalars = jnp.stack([self.mine, self.bits[1], self.pos, self.quarter]).astype(jnp.int32)

    def up(self, item):
        ring = self.ring
        return lax.ppermute(item, "rep", [(ring[i], ring[(i + 1) % 8]) for i in range(8)])

    def down(self, item):
        ring = self.ring
        return lax.ppermute(item, "rep", [(ring[(i + 1) % 8], ring[i]) for i in range(8)])

    def swap(self, item, mask):
        return lax.ppermute(item, "shard", [(i, i ^ mask) for i in range(4)])

    def cross_rep(self, item, mask):
        return lax.ppermute(item, "rep", [(i, i ^ mask) for i in range(8)])

    def gather(self, item):
        if not self.direct:
            rows = item.shape[0]
            whole = lax.all_gather(item, "shard", axis=0, tiled=True)
            return [whole[i * rows : (i + 1) * rows] for i in range(self.shards)]
        far = self.swap(item, 2)
        near = self.swap(item, 1)
        cross = self.swap(far, 1)
        return [item, near, far, cross]

    def scatter(self, near_part, far_part):
        if not self.direct:
            item = jnp.concatenate([near_part, far_part], axis=0).astype(f32)
            return lax.psum_scatter(item, "shard", scatter_dimension=0, tiled=True)
        rows = near_part.shape[0] // 2
        far = self.swap(far_part[:rows] + self.swap(far_part[rows:], 1), 2)
        near = self.swap(near_part[rows:], 1)
        return near_part[:rows].astype(f32) + near.astype(f32) + far.astype(f32)

    def ring_scatter(self, shares, layout, blocks):
        return RingSum(self, shares, layout, blocks)

    def ring_gather(self, item, *before):
        u1, d1 = self.up(item), self.down(item)
        u2, d2 = self.up(u1), self.down(d1)
        u3, d3 = self.up(u2), self.down(d2)
        last = after(u3, *before) if before else u3
        u4, d4 = self.up(last[:, :1]), self.down(d3[:, 1:])
        return [
            (item, 0, None), (u1, -1, None), (d1, 1, None), (u2, -2, None), (d2, 2, None),
            (u3, -3, None), (d3, 3, None), (u4, 4, 0), (d4, 4, 1),
        ]

    def exchange(self, chunk, pieces, wide):
        own, near, far = split(self.scalars, chunk, pieces, wide)
        near = self.swap(near, 1)
        far = self.swap(jnp.concatenate([far, near[1:]], axis=0), 2)
        return own, near, far


class RingSum:
    def __init__(self, moves, shares, layout, blocks):
        self.moves = moves
        self.step = functools.partial(ring_step, shares, layout, blocks)
        self.send(*self.step([self.chunk(4)], [(0, (0,), []), (0, (1,), [])], []))
        self.at = 4

    def chunk(self, offset):
        return (self.moves.pos + offset) % 8

    def send(self, u, d):
        self.sent = u
        self.arrived = [self.moves.up(u), self.moves.down(d)]

    def advance(self, *before):
        self.at -= 1
        both = (0, 1)
        u, d = self.arrived
        u = after(u, *before) if before else u
        held = [(0,), (1,)] if self.at == 3 else [both, both]
        plan = [(0, both, [(0, held[0])]), (1, both, [(1, held[1])])]
        self.send(*self.step([self.chunk(self.at), self.chunk(8 - self.at)], plan, [u, d]))

    def finish(self, *before):
        both = (0, 1)
        u, d = self.arrived
        u = after(u, *before) if before else u
        return self.step([self.chunk(0)], [(0, both, [(0, both), (1, both)])], [u, d])[0]


class Fetch:
    def __init__(self, moves, own, near, piece, spot, shape):
        self.moves, self.own, self.near, self.piece = moves, own, near, piece
        self.spot, self.shape = spot, shape

    def start(self, *before):
        self.here = self.moves.swap(after(self.piece, *before), 2)
        self.there = self.moves.cross_rep(self.here, 1)

    def finish(self):
        moves, here, there, spot = self.moves, self.here, self.there, self.spot
        rows, width = self.own.shape
        half = rows // 2
        near = moves.swap(self.near, 1)
        inputs = [self.own, near, here, moves.swap(here[1], 1), there, moves.swap(there[1], 1)]
        todo = [
            (0, (), (0, rows), (0, width), 0, lambda shard, *_: spot(shard, 0)),
            (1, (), (0, rows), (0, width), 0, lambda shard, *_: spot(shard ^ 1, 0)),
            (2, (0,), (0, half), (0, width), 0, lambda shard, y, *_: spot(shard ^ 2, y * half)),
            (3, (), (0, half), (0, width), 0, lambda shard, y, *_: spot(shard ^ 3, y * half)),
            (4, (0,), (0, half), (0, width), 0, lambda shard, y, *_: spot(shard ^ 2, (1 - y) * half)),
            (5, (), (0, half), (0, width), 0, lambda shard, y, *_: spot(shard ^ 3, (1 - y) * half)),
        ]
        return place(moves.scalars, inputs, [(self.shape, bf16)], todo)[0]


class DeepFetch(Fetch):
    def start(self, *before):
        moves = self.moves
        self.here = moves.swap(after(self.piece, *before), 2)
        pair = jnp.concatenate([self.here, moves.cross_rep(self.here, 1)], axis=0)
        self.parts = [pair, moves.cross_rep(pair, 2)]

    def finish(self):
        moves, spot = self.moves, self.spot
        first, second = self.parts
        rows, width = self.own.shape
        size = rows // 4
        cross = moves.swap(jnp.stack([first[1], first[3], second[1], second[3]]), 1)
        inputs = [self.own, moves.swap(self.near, 1), first, second, cross]
        todo = [
            (0, (), (0, rows), (0, width), 0, lambda shard, *_: spot(shard, 0)),
            (1, (), (0, rows), (0, width), 0, lambda shard, *_: spot(shard ^ 1, 0)),
        ]
        for i, (source, index, mask) in enumerate([(2, 0, 0), (2, 2, 2), (3, 0, 1), (3, 2, 3)]):
            for which, where, at in ((2, source, index), (3, 4, i)):

                def to(shard, y, pos, quarter, which=which, mask=mask):
                    return spot(shard ^ which, (quarter ^ mask) * size)

                todo.append((where, (at,), (0, size), (0, width), 0, to))
        return place(moves.scalars, inputs, [(self.shape, bf16)], todo)[0]


def after(item, *others):
    return lax.optimization_barrier((item, *others))[0]


def per_device(
    tokens, segments, grad_out, attention_gain, query_weight, key_matrix, value_matrix, query_gain,
    key_gain, output_weight, mlp_gain, gate_weight, up_weight, down_weight,
):
    moves = Moves()
    shards, mine, direct = moves.shards, moves.mine, moves.direct
    rows, width = tokens.shape[1:]
    total = rows * shards
    slice_width = attention_gain.shape[0]
    head_slice = query_gain.shape[0]
    head = head_slice * shards
    k_heads = key_matrix.shape[1] // head // shards
    q_heads = query_weight.shape[1] // head // shards
    q_width, k_width = q_heads * head, k_heads * head
    units = down_weight.shape[0]
    own_tokens = tokens[0]
    cot = grad_out[0]

    if direct:
        by_rows = lambda source, line: (source * slice_width + line, 0)
        qkv = Fetch(
            moves,
            *cut(moves.scalars, [query_weight, key_matrix, value_matrix], [q_width, k_width, k_width], 2),
            by_rows,
            (width, q_width + 2 * k_width),
        )
        qkv.start()
        attention_gain = after(attention_gain, qkv.piece)
    small = jnp.concatenate(
        [attention_gain, mlp_gain, query_gain, key_gain, segments[0].astype(bf16)]
    )[None]
    small = jnp.concatenate(moves.gather(small), axis=0)
    if direct:
        whole = jnp.where(mine % 2 == 0, small, small[jnp.array([1, 0, 3, 2])])
        whole = jnp.where(mine // 2 == 0, whole, whole[jnp.array([2, 3, 0, 1])])
    else:
        whole = small
    cuts = [slice_width, 2 * slice_width, 2 * slice_width + head_slice, 2 * slice_width + 2 * head_slice]
    input_gain = whole[:, : cuts[0]].reshape(1, width).astype(f32)
    second_gain = whole[:, cuts[0] : cuts[1]].reshape(1, width).astype(f32)
    head_gains = jnp.stack(
        [whole[:, cuts[1] : cuts[2]].reshape(head), whole[:, cuts[2] : cuts[3]].reshape(head)]
    ).astype(f32)
    segs = small[:, cuts[3] :].reshape(total).astype(f32)
    index = jnp.arange(shards, dtype=jnp.int32) ^ moves.flip
    places = (index[:, None] * rows + jnp.arange(rows, dtype=jnp.int32)[None]).reshape(total)
    firsts = jnp.sum((segs < 0.5).astype(jnp.int32))
    seconds = jnp.sum((segs < 1.5).astype(jnp.int32))
    opening = jnp.where(segs < 0.5, 0, jnp.where(segs < 1.5, firsts, seconds))
    freqs = theta_base ** (-(jnp.arange(head // 2, dtype=f32) * 2.0) / head)
    angles = (places - opening).astype(f32)[:, None] * freqs
    cosine, sine = jnp.cos(angles), jnp.sin(angles)
    cosine = jnp.concatenate([cosine, cosine], axis=1)
    sine = jnp.concatenate([-sine, sine], axis=1)
    seg_col, seg_row = segs[:, None], segs[None, :]
    order = moves.flip.astype(jnp.int32)[None]

    all_tokens = all_cot = None
    if direct:
        outer = lambda i, begin, n: lax.dynamic_slice(
            output_weight, ((mine ^ i) * q_width + begin, 0), (n, slice_width)
        )
        half = q_width // 2
        output = Fetch(
            moves,
            outer(0, 0, q_width),
            outer(1, 0, q_width),
            jnp.stack([outer(2, moves.bits[1] * half, half), outer(3, moves.bits[1] * half, half)]),
            lambda source, line: (line, source * slice_width),
            (q_width, width),
        )
        both = DeepFetch(
            moves,
            *cut(moves.scalars, [gate_weight, up_weight], [units, units], 4),
            by_rows,
            (width, 2 * units),
        )
        all_tokens = moves.gather(after(own_tokens, qkv.here))
        output.start(all_tokens[2], qkv.there)
        qkv_weight = qkv.finish()
        both.start(output.here)
        out_weight = output.finish()
        all_cot = moves.gather(after(cot, both.here))
    else:
        spread = lambda item: lax.all_to_all(item, "shard", split_axis=1, concat_axis=0, tiled=True)
        qkv_weight = jnp.concatenate(
            [spread(query_weight), spread(key_matrix), spread(value_matrix)], axis=1
        )
        out_weight = lax.all_to_all(output_weight, "shard", split_axis=0, concat_axis=1, tiled=True)
        feed_weight = jnp.concatenate([spread(gate_weight), spread(up_weight)], axis=1)

    if not direct:
        all_tokens, all_cot = moves.gather(own_tokens), moves.gather(cot)
    normed_one, lin, rot, val = project(
        all_tokens, input_gain, qkv_weight, cosine, sine, head_gains, q_heads, k_heads
    )
    if direct:
        rot = after(rot, both.here)
    attended, attended_low, logs = attend(order, rot, val, seg_col, seg_row, q_heads, k_heads, head, shards)
    inputs = own_tokens.astype(f32)
    split = total // 2
    if direct:
        feed_weight = both.finish()
        attended_low = after(attended_low, all_cot[2])
    far_part = dot(attended_low[split:], out_weight).astype(bf16)
    near_part = dot(attended_low[:split], out_weight).astype(bf16)
    residual_one = inputs + moves.scatter(near_part, far_part)
    residual_scale = inverse_root(residual_one)
    normed_two = moves.gather((residual_one * residual_scale * second_gain).astype(bf16))

    hidden, gate_grad, up_grad, normed_two, all_cot, out_part, *norm_grad = feed(
        normed_two, all_cot, feed_weight, down_weight, 0, shards, []
    )
    if direct:
        crossed = norm_grad[2] + moves.swap(norm_grad[3], 1)
        hidden, gate_grad = after(hidden, crossed), after(gate_grad, crossed)
        up_grad = after(up_grad, crossed)
        near_grad = norm_grad[0].astype(f32) + moves.swap(norm_grad[1], 1).astype(f32)
        far_grad = moves.swap(crossed, 2)
    else:
        norm_grad = jnp.concatenate(norm_grad, axis=0)
        normed_grad_two = moves.scatter(norm_grad[:split], norm_grad[split:])
    share_down = dot_tn(hidden, all_cot).astype(bf16)
    share_gate = dot_tn(normed_two, gate_grad).astype(bf16)
    share_up = dot_tn(normed_two, up_grad).astype(bf16)
    if direct:
        lines = slice_width // 16
        rest = 2 * units - width
        as_chunks = lambda share: share.reshape(-1, 8, 2, lines, share.shape[1])
        spot_of = lambda values, offset: lax.rem(values[2] + (offset + 8), 8) * (2 * lines)

        downs = units // slice_width
        blocks = (6 + downs, width)
        layout = []
        for i in range(4):
            layout += [
                (0, i, 0, units, i, 0),
                (1, i, 0, width - units, i, units),
                (1, i, width - units, rest, 4 + i // 2, (i % 2) * rest),
            ]
        layout += [(2, b, 0, width, 6 + b, 0) for b in range(downs)]
        ring = moves.ring_scatter(
            [as_chunks(share_gate), as_chunks(share_up), as_chunks(share_down)], layout, blocks
        )
        normed_grad_two = near_grad + after(far_grad, ring.sent).astype(f32)
    mlp_gain_part = jnp.sum(normed_grad_two * residual_one * residual_scale, axis=0)
    residual_grad = cot.astype(f32) + norm_back(
        normed_grad_two * second_gain, residual_one, residual_scale
    )
    branch_low = residual_grad.astype(bf16)
    if direct:
        ring.advance(branch_low)
        far_branch = after(moves.swap(branch_low, 2), ring.sent)
        branch_grad = [
            branch_low, moves.swap(branch_low, 1), far_branch, moves.swap(far_branch, 1),
        ]
    else:
        branch_grad = moves.gather(branch_low)
    out_part = after(out_part, *branch_grad)
    layer_out = (residual_one + moves.scatter(out_part[:split], out_part[split:])).astype(bf16)

    out_grad, branch_grad = branch_back(branch_grad, out_weight)
    share_out = dot_tn(attended_low, branch_grad).astype(bf16)
    if direct:
        ring.advance(out_grad)
        out_grad = after(out_grad, ring.sent)
    query_grad, key_grad, val_grad = attend_back(
        order, rot, val, out_grad, attended, logs, seg_col, seg_row, q_heads, k_heads, head, shards
    )
    if direct:
        ring.advance(query_grad)
        query_grad = after(query_grad, ring.sent)
    query_lin_grad, pair_lin_grad, norm_one_part, gain_part, head_part = unproject(
        query_grad, key_grad, val_grad, lin, cosine, sine, head_gains, qkv_weight, all_tokens,
        q_heads, k_heads,
    )
    share_query = dot_tn(normed_one, query_lin_grad).astype(bf16)
    share_pair = dot_tn(normed_one, pair_lin_grad).astype(bf16)
    normed_grad_one = moves.scatter(norm_one_part[:split], norm_one_part[split:])
    grad_tokens = residual_grad + norm_back(normed_grad_one * input_gain, inputs, inverse_root(inputs))

    gains = jnp.concatenate([gain_part[0], mlp_gain_part, head_part.reshape(2 * head)])[None]
    if direct:
        gains = gains + moves.swap(gains, 1)
        gains = gains + moves.swap(gains, 2)
        for mask in (1, 2, 4):
            gains = gains + moves.cross_rep(gains, mask)
    else:
        gains = lax.psum(gains, ("shard", "rep"))
    gains = gains[0]

    def own_part(begin, size):
        return lax.dynamic_slice_in_dim(gains, begin + mine * size, size, 0)

    grad_attention_gain = own_part(0, slice_width)
    grad_mlp_gain = own_part(width, slice_width)
    grad_query_gain = own_part(2 * width, head_slice)
    grad_key_gain = own_part(2 * width + head, head_slice)

    if direct:
        chunk = ring.finish()
        own, near, far = moves.exchange(
            chunk, lambda at: [(at, 0, width), (4 + at // 2, (at % 2) * rest, rest)], 2 * units
        )
        layout = []
        for i, (source, index) in enumerate([(0, 0), (1, 0), (2, 0), (2, 1)]):
            layout += [
                (source, index, 0, width, i, 0),
                (source, index, width, rest, 4 + i // 2, (i % 2) * rest),
            ]
        layout += [(3, 6 + b, 0, width, 6 + b, 0) for b in range(downs)]
        parts = moves.ring_gather(
            pack([own, near, far, chunk], layout, (blocks[0], 2, lines, width))
        )
        todo = []
        for source, (part, offset, half) in enumerate(parts):
            for h in range(part.shape[1]):
                line = ((half or 0) + h) * lines
                for i in range(4):

                    def at(*values, i=i, line=line, offset=offset, begin=0):
                        return spot_of(values, offset) + line, (values[0] ^ i) * units + begin

                    first = width - units
                    todo += [
                        (source, (i, h), (0, lines), (0, units), 0, at),
                        (source, (i, h), (0, lines), (units, width), 1, at),
                        (
                            source, (4 + i // 2, h), (0, lines),
                            ((i % 2) * rest, (i % 2) * rest + rest), 1,
                            functools.partial(at, begin=first),
                        ),
                    ]
                for b in range(downs):

                    def at(*values, b=b, line=line, offset=offset):
                        return b * slice_width + spot_of(values, offset) + line, 0

                    todo.append((source, (6 + b, h), (0, lines), (0, width), 2, at))
        shapes = [((slice_width, units * 4), f32)] * 2 + [((units, width), f32)]
        grad_gate, grad_up, grad_down = place(
            moves.scalars, [part for part, _, _ in parts], shapes, todo
        )

        first_near, first_packed, first_last = near, parts[0][0], parts[-1][0]

        outs = q_width // slice_width
        pair = 2 * k_width
        wide = q_width + pair
        layout = []
        for i in range(4):
            layout += [(0, i, 0, q_width, i, 0), (1, i, 0, pair, i, q_width)]
        layout += [(2, b, 0, width, 4 + b, 0) for b in range(outs)]
        ring = moves.ring_scatter(
            [as_chunks(share_query), as_chunks(share_pair), as_chunks(share_out)],
            layout,
            (4 + outs, width),
        )
        ring.advance(first_near)
        ring.advance(first_packed)
        ring.advance()
        chunk = ring.finish()
        own, near, far = moves.exchange(
            chunk,
            lambda at: [(at, 0, wide)] + [(4 + b, at * slice_width, slice_width) for b in range(outs)],
            wide + outs * slice_width,
        )
        wide_all = wide + outs * slice_width
        layout = [
            (source, index, 0, wide_all, i, 0)
            for i, (source, index) in enumerate([(0, 0), (1, 0), (2, 0), (2, 1)])
        ]
        parts = moves.ring_gather(pack([own, near, far], layout, (4, 2, lines, wide_all)))
        todo = []
        for source, (part, offset, half) in enumerate(parts):
            for h in range(part.shape[1]):
                line = ((half or 0) + h) * lines
                for i in range(4):
                    begin = 0
                    for target, size in enumerate([q_width, k_width, k_width]):

                        def at(*values, i=i, line=line, offset=offset, size=size):
                            return spot_of(values, offset) + line, (values[0] ^ i) * size

                        todo.append((source, (i, h), (0, lines), (begin, begin + size), target, at))
                        begin += size
                    for b in range(outs):

                        def at(*values, i=i, b=b, line=line, offset=offset):
                            first = (values[0] ^ i) * q_width + b * slice_width
                            return first + spot_of(values, offset) + line, 0

                        todo.append(
                            (source, (i, h), (0, lines), (begin, begin + slice_width), 3, at)
                        )
                        begin += slice_width
        shapes = [((slice_width, size * 4), f32) for size in (q_width, k_width, k_width)]
        shapes.append(((q_width * 4, slice_width), f32))
        grad_query, grad_key, grad_value, grad_output = place(
            moves.scalars, [part for part, _, _ in parts], shapes, todo
        )
    else:

        def finish(share):
            part = lax.all_to_all(share, "shard", split_axis=0, concat_axis=1, tiled=True)
            return lax.psum(part, "rep").astype(f32)

        grad_down = lax.psum(share_down, "rep").astype(f32)
        grad_gate = finish(share_gate)
        grad_up = finish(share_up)
        grad_output = lax.psum(
            lax.all_to_all(share_out, "shard", split_axis=1, concat_axis=0, tiled=True), "rep"
        ).astype(f32)
        grad_query = finish(share_query)
        grad_key = finish(share_pair[:, :k_width])
        grad_value = finish(share_pair[:, k_width:])

    return (
        layer_out[None], grad_tokens[None], grad_attention_gain, grad_query, grad_key, grad_value,
        grad_query_gain, grad_key_gain, grad_output, grad_mlp_gain, grad_gate, grad_up, grad_down,
    )


def solution(mesh):
    rows_over = P("shard", None)
    return jax.shard_map(
        per_device,
        mesh=mesh,
        in_specs=(
            P("rep", "shard", None), P("rep", "shard"), P("rep", "shard", None), P("shard"), rows_over,
            rows_over, rows_over, P("shard"), P("shard"), P(None, "shard"), P("shard"), rows_over,
            rows_over, rows_over,
        ),
        out_specs=(
            P("rep", "shard", None), P("rep", "shard", None), P("shard"), rows_over, rows_over,
            rows_over, P("shard"), P("shard"), P(None, "shard"), P("shard"), rows_over, rows_over,
            rows_over,
        ),
        check_vma=False,
    )
```
